128 devices in a mesh: batch: 8 (over z, core), feat: 16 (over x, y).
Axes of the slice: x: 4, y: 4, z: 4, core: 2. Of those that a mesh axis runs over, the one named last changes fastest.
Arguments:
- view_one: float32 [4096, 8192], P('batch', 'feat'), may hold values from -400 to 400, as said below
- view_two: float32 [4096, 8192], P('batch', 'feat'), may hold values from -400 to 400, as said below
Outputs:
- grad_one: float32 [4096, 8192], P('batch', 'feat')
- grad_two: float32 [4096, 8192], P('batch', 'feat')
- loss_value: float32 [], replicated
The draws below stay inside these ranges and needn't reach their ends.
Inputs may be any that keep to these rules, and one draw needn't show every extreme that they name: `view_one`: finite values of order up to some tens. `view_two`: finite values of order up to some tens.
All inputs are finite; a program needn't handle non-finite values.
Results may differ from the reference program's by a relative error of at most 0.0003.
Values sent between devices are 32-bit elements; how exact they have to be, the bound alone decides.
No kernel may reach another device: no remote copies, remote signals or barrier semaphores. Data moves between devices by JAX's collectives and lax.ppermute only.
A program may use at most 128 MiB of HBM per device.

```python
import jax
import jax.numpy as jnp
from jax import lax

F = 8192
TOTAL_CLIPS = 4096


def shared_base(key):
    keys = jax.random.split(key, 6)
    normal_base = jax.random.normal(keys[0], (TOTAL_CLIPS, F), jnp.float32)
    base = normal_base
    linkage = jax.random.uniform(keys[4], (1, F), jnp.float32, 0.7, 0.95)
    noise = jax.random.normal(keys[5], (TOTAL_CLIPS, F), jnp.float32)
    second = linkage * base + jnp.sqrt(1.0 - linkage * linkage) * noise
    return (base, second)


def shape_view(key, values):
    keys = jax.random.split(key, 3)
    column_scale = jnp.exp(jax.random.uniform(keys[0], (1, F), jnp.float32, 0.0, 2.3025851))
    column_shift = 2.0 * jax.random.normal(keys[1], (1, F), jnp.float32)
    row_scale = jnp.exp(jax.random.uniform(keys[2], (TOTAL_CLIPS, 1), jnp.float32, -0.7, 0.7))
    return values * row_scale * column_scale + column_shift


def draw_view_one(key, part):
    base, second = shared_base(key)
    key = jax.random.fold_in(key, 11)
    return shape_view(key, base)


def draw_view_two(key, part):
    base, second = shared_base(key)
    key = jax.random.fold_in(key, 23)
    return shape_view(key, second)


def setup_inputs(seed: int = 0) -> dict:
    streams_of = jax.random.split(jax.random.key(seed), 3)
    view_one = draw_view_one(jax.random.fold_in(streams_of[2], 71), 0)
    view_two = draw_view_two(jax.random.fold_in(streams_of[2], 71), 0)
    return dict(view_one=view_one, view_two=view_two)


epsilon = 1e-05
off_weight = 0.005

def normalize(view):
    center = lax.optimization_barrier(jnp.mean(view, axis=0))
    deviate = view - center
    spread = lax.optimization_barrier(jnp.mean(deviate * deviate, axis=0))
    scale = 1.0 / jnp.sqrt(spread + epsilon)
    return (deviate * scale, scale)

def norm_back(gnorm, normed, scale):
    first_mean = lax.optimization_barrier(jnp.mean(gnorm, axis=0))
    second_mean = lax.optimization_barrier(jnp.mean(gnorm * normed, axis=0))
    return (gnorm - first_mean - normed * second_mean) * scale

def reference(view_one, view_two):
    clip_total = view_one.shape[0]
    normed_one, scale_one = normalize(view_one)
    normed_two, scale_two = normalize(view_two)
    corr = jnp.dot(normed_one.T, normed_two, precision=lax.Precision.HIGHEST) / clip_total
    diagonal = jnp.diagonal(corr)
    loss = jnp.sum((1.0 - diagonal) ** 2) + off_weight * (jnp.sum(corr * corr) - jnp.sum(diagonal * diagonal))
    dcorr = 2.0 * off_weight * corr + jnp.diag(-2.0 * (1.0 - diagonal) - 2.0 * off_weight * diagonal)
    gnorm_one = jnp.dot(normed_two, dcorr.T, precision=lax.Precision.HIGHEST) / clip_total
    gnorm_two = jnp.dot(normed_one, dcorr, precision=lax.Precision.HIGHEST) / clip_total
    grad_one = clip_total * norm_back(gnorm_one, normed_one, scale_one)
    grad_two = clip_total * norm_back(gnorm_two, normed_two, scale_two)
    return (grad_one, grad_two, loss / F)
```

```python
import jax
import jax.numpy as jnp
from jax import lax
from jax.experimental import pallas as pl
from jax.experimental.pallas import tpu as pltpu
from jax.sharding import PartitionSpec as P

epsilon = 1e-05
off_weight = 0.005
f32 = jnp.float32
bf16 = jnp.bfloat16

gray = (0, 1, 3, 2)
label_of = tuple(gray[i // 4] * 4 + gray[i % 4] for i in range(16))
feat_of = tuple(label_of.index(i) for i in range(16))
orders = ((3, 2, 1, 0), (2, 3, 0, 1), (1, 0, 3, 2), (0, 1, 2, 3))
masks = tuple(
    tuple(sum(((p >> (3 - j)) & 1) << order[j] for j in range(4)) for p in range(16))
    for order in orders
)

vmem = pl.BlockSpec(memory_space=pltpu.VMEM)
smem = pl.BlockSpec(memory_space=pltpu.SMEM)


def local_call(kernel, scalars, arrays, outs, scratch=(), flops=0):
    moved = sum(a.size * a.dtype.itemsize for a in (*arrays, *outs))
    call = pl.pallas_call(
        kernel,
        out_shape=list(outs),
        in_specs=[smem] * len(scalars) + [vmem] * len(arrays),
        out_specs=[vmem] * len(outs),
        scratch_shapes=list(scratch),
        compiler_params=pltpu.CompilerParams(vmem_limit_bytes=44 * 1024 * 1024),
        cost_estimate=pl.CostEstimate(flops=flops, bytes_accessed=moved, transcendentals=0),
    )
    return list(call(*scalars, *arrays))


def shape(rows, cols, dtype=f32):
    return jax.ShapeDtypeStruct((rows, cols), dtype)


def split(value):
    high = value.astype(bf16)
    return high, (value - high.astype(f32)).astype(bf16)


def dot3(left, right, left_dim, right_dim):
    def one(a, b):
        return lax.dot_general(
            a, b, (((left_dim,), (right_dim,)), ((), ())), preferred_element_type=f32
        )

    return one(left[0], right[0]) + (one(left[0], right[1]) + one(left[1], right[0]))


def normalize(first_ref, same, cross, center, scale, high, low):
    rows = same.shape[0]

    def put(source, at):
        high[at : at + rows, :], low[at : at + rows, :] = split(
            (source[...] - center[...]) * scale[...]
        )

    @pl.when(first_ref[0] == 1)
    def _():
        put(same, 0)
        put(cross, rows)

    @pl.when(first_ref[0] != 1)
    def _():
        put(cross, 0)
        put(same, rows)


def own_kernel(first, same, cross, center, scale, high, low, gram):
    normalize(first, same, cross, center, scale, high, low)
    quarter = gram.shape[1] // 4
    for q in range(4):
        part = slice(q * quarter, (q + 1) * quarter)
        gram[:, part] = dot3(
            (high[...], low[...]), (high[part, :], low[part, :]), 1, 1
        )


def cube_kernel(first, label, same, cross, center, scale, high_0, low_0, high, low, *rest):
    keeps, sends, whole = rest[:4], rest[4:8], rest[8]
    normalize(first, same, cross, center, scale, high, low)
    quarter = whole.shape[1]
    chunk = whole.shape[0] // 16
    for q in range(4):
        part = slice(q * quarter, (q + 1) * quarter)
        whole[...] = dot3((high_0[...], low_0[...]), (high[part, :], low[part, :]), 1, 1)
        for p in range(16):
            at = pl.multiple_of((label[0] ^ masks[q][p]) * chunk, chunk)
            target = keeps[q] if p < 8 else sends[q]
            target[p % 8 * chunk : (p % 8 + 1) * chunk, :] = whole[pl.ds(at, chunk), :]


def front_kernel(first, one, two, stats, same, cross):
    rows = one.shape[0]
    mean_one = jnp.sum(one[...], axis=0, keepdims=True) / rows
    mean_two = jnp.sum(two[...], axis=0, keepdims=True) / rows
    deviate_one = one[...] - mean_one
    deviate_two = two[...] - mean_two
    stats[...] = jnp.zeros(stats.shape, f32)
    stats[0:1, :] = mean_one
    stats[1:2, :] = mean_two
    stats[2:3, :] = jnp.sum(deviate_one * deviate_one, axis=0, keepdims=True)
    stats[3:4, :] = jnp.sum(deviate_two * deviate_two, axis=0, keepdims=True)
    stats[4:5, :] = jnp.sum(deviate_one * deviate_two, axis=0, keepdims=True)

    @pl.when(first[0] == 1)
    def _():
        same[...] = one[...]
        cross[...] = two[...]

    @pl.when(first[0] != 1)
    def _():
        same[...] = two[...]
        cross[...] = one[...]


def fold_kernel(*refs):
    half = refs[0].shape[0] // 2
    for q in range(4):
        keep, came, keep_out, send_out = refs[q::4]
        keep_out[...] = keep[:half, :] + came[:half, :]
        send_out[...] = keep[half:, :] + came[half:, :]


def last_fold_kernel(*refs):
    out = refs[8]
    cols = refs[0].shape[1]
    for q in range(4):
        out[:, q * cols : (q + 1) * cols] = refs[q][...] + refs[4 + q][...]


def match_kernel(mine, other, match, *parts):
    cols = parts[0].shape[1]
    for q in range(4):
        parts[q][...] = other[:, q * cols : (q + 1) * cols]
    match[...] = jnp.full(match.shape, jnp.sum(mine[...] * other[...]), f32)


def join_kernel(*refs):
    rows = refs[0].shape[0]
    for q in range(4):
        own, came, out = refs[q::4]
        out[:rows, :] = own[...]
        out[rows:, :] = came[...]


def gather_rows(label, q, own, came, high, low):
    half, cols = own.shape
    chunk = half // 8
    for p in range(16):
        source = own if p < 8 else came
        at = pl.multiple_of((label[0] ^ masks[q][p]) * chunk, chunk)
        high[pl.ds(at, chunk), :], low[pl.ds(at, chunk), :] = split(
            source[p % 8 * chunk : (p % 8 + 1) * chunk, :]
        )


def both_kernel(gathered, high_0, low_0, high_1, low_1, ahead, turned, high, low):
    quarter = gathered.shape[1] // 4
    chunk = gathered.shape[0] // 16
    for q in range(4):
        part = slice(q * quarter, (q + 1) * quarter)
        for i in range(16):
            at = slice(label_of[i] * chunk, (label_of[i] + 1) * chunk)
            high[at, :], low[at, :] = split(gathered[i * chunk : (i + 1) * chunk, part])
        gram = (high[...], low[...])
        term = dot3(gram, (high_1[part, :], low_1[part, :]), 1, 0)
        ahead[...] = term if q == 0 else ahead[...] + term
        turned[part, :] = dot3(gram, (high_0[...], low_0[...]), 0, 0)


def one_kernel(label, *refs):
    owns, cames = refs[:4], refs[4:8]
    high_2, low_2, ahead, high, low = refs[8:]
    quarter = owns[0].shape[1]
    for q in range(4):
        part = slice(q * quarter, (q + 1) * quarter)
        gather_rows(label, q, owns[q], cames[q], high, low)
        term = dot3((high[...], low[...]), (high_2[part, :], low_2[part, :]), 1, 0)
        ahead[...] = term if q == 0 else ahead[...] + term


def last_kernel(factor, core, gram, high_0, low_0, one, two, three, kept, sent, sums, total):
    rows = kept.shape[0]
    quarter = gram.shape[1] // 4
    total[...] = one[...] + two[...] + three[...]
    for q in range(4):
        part = slice(q * quarter, (q + 1) * quarter)
        total[...] += dot3(split(gram[:, part]), (high_0[part, :], low_0[part, :]), 1, 0)
    total[...] = total[...] * factor[0]
    normed = high_0[...].astype(f32) + low_0[...].astype(f32)
    sums[...] = jnp.zeros(sums.shape, f32)
    sums[0:1, :] = jnp.sum(total[...], axis=0, keepdims=True)
    sums[1:2, :] = jnp.sum(total[...] * normed, axis=0, keepdims=True)
    kept[...] = total[pl.ds(pl.multiple_of(core[0] * rows, rows), rows), :]
    sent[...] = total[pl.ds(pl.multiple_of((1 - core[0]) * rows, rows), rows), :]


def across(array, bit):
    return lax.ppermute(
        array, "feat", [(i, feat_of[label_of[i] ^ (1 << bit)]) for i in range(16)]
    )


def step_across(arrays, step):
    return [across(array, order[step]) for array, order in zip(arrays, orders)]


def fold(keeps, sends, step):
    cames = step_across(sends, step)
    rows, cols = keeps[0].shape
    if step == 3:
        return local_call(last_fold_kernel, (), (*keeps, *cames), [shape(rows, 4 * cols)])[0]
    outs = local_call(fold_kernel, (), (*keeps, *cames), [shape(rows // 2, cols)] * 8)
    return outs[:4], outs[4:]


def body(view_one, view_two):
    rows, cols = view_one.shape
    batch = lax.axis_size("batch")
    feats = lax.axis_size("feat")
    clip_total = rows * batch
    features = cols * feats
    core = lax.axis_index("batch") % 2
    on_first = core == 0
    first = (1 - core).astype(jnp.int32).reshape((1,))
    label = jnp.array(label_of, jnp.int32)[lax.axis_index("feat")].reshape((1,))
    swap = [(i, i ^ 1) for i in range(batch)]
    down = [(i, (i - 2) % batch) for i in range(batch)]
    up = [(i, (i + 2) % batch) for i in range(batch)]
    down_cross = [(i, (i ^ 1) - 2 if i > 1 else (i ^ 1) - 2 + batch) for i in range(batch)]
    up_cross = [(i, ((i ^ 1) + 2) % batch) for i in range(batch)]

    def pick(one, two):
        return jnp.where(on_first, one, two)

    mine, same_0, mine_cross = local_call(
        front_kernel,
        (first,),
        (view_one, view_two),
        [shape(8, cols), shape(rows, cols), shape(rows, cols)],
    )
    parts = lax.all_gather(mine, "batch", axis=0)
    cross_0 = lax.ppermute(mine_cross, "batch", swap)
    parts, far_same, far_cross = lax.optimization_barrier((parts, same_0, mine_cross))
    center_one = jnp.mean(parts[:, 0], axis=0)
    center_two = jnp.mean(parts[:, 1], axis=0)
    shift_one = parts[:, 0] - center_one
    shift_two = parts[:, 1] - center_two
    spread_one = jnp.sum(parts[:, 2] + rows * shift_one * shift_one, axis=0) / clip_total
    spread_two = jnp.sum(parts[:, 3] + rows * shift_two * shift_two, axis=0) / clip_total
    scale_one = 1.0 / jnp.sqrt(spread_one + epsilon)
    scale_two = 1.0 / jnp.sqrt(spread_two + epsilon)
    covary = jnp.sum(parts[:, 4] + rows * shift_one * shift_two, axis=0) / clip_total
    diagonal = covary * scale_one * scale_two
    center = pick(center_one, center_two).reshape((1, cols))
    scale = pick(scale_one, scale_two).reshape((1, cols))

    same_1 = lax.ppermute(far_same, "batch", down)
    cross_1 = lax.ppermute(far_cross, "batch", down_cross)
    cross_up = lax.ppermute(far_cross, "batch", up_cross)
    block = 2 * rows
    quarter = block // 4
    product = 3 * 2 * block * block * cols
    halves = [shape(block, cols, bf16)] * 2
    row_scratch = [pltpu.VMEM((block, quarter), bf16)] * 2

    high_0, low_0, gram = local_call(
        own_kernel,
        (first,),
        (same_0, cross_0, center, scale),
        halves + [shape(block, block)],
        flops=product,
    )
    piece_0 = lax.psum_scatter(gram, "feat", scatter_dimension=0, tiled=True)
    same_1, cross_1, high_0, low_0 = lax.optimization_barrier((same_1, cross_1, high_0, low_0))

    def cube_gram(same, cross):
        outs = local_call(
            cube_kernel,
            (first, label),
            (same, cross, center, scale, high_0, low_0),
            halves + [shape(block // 2, quarter)] * 8,
            scratch=[pltpu.VMEM((block, quarter), f32)],
            flops=product,
        )
        return outs[:2], outs[2:6], outs[6:]

    def other_core(piece):
        other = lax.ppermute(piece, "batch", swap)
        match, *owns = local_call(
            match_kernel, (), (piece, other), [shape(8, 128)] + [shape(block // 16, quarter)] * 4
        )
        return match[0, 0], other, owns

    halves_1, keeps_1, sends_1 = cube_gram(same_1, cross_1)
    keeps_1, sends_1 = fold(keeps_1, sends_1, 0)
    same_1, cross_up, keeps_1[0] = lax.optimization_barrier((same_1, cross_up, keeps_1[0]))
    same_2 = lax.ppermute(same_1, "batch", down)
    cross_2 = lax.ppermute(cross_up, "batch", up)
    for step in (1, 2):
        keeps_1, sends_1 = fold(keeps_1, sends_1, step)
    piece_1 = fold(keeps_1, sends_1, 3)

    same_2, cross_2, piece_1 = lax.optimization_barrier((same_2, cross_2, piece_1))
    match_1, other_1, _ = other_core(piece_1)
    gram_1 = lax.all_gather(other_1, "feat", axis=0, tiled=True)
    piece_0, other_1 = lax.optimization_barrier((piece_0, other_1))
    match_0, other_0, _ = other_core(piece_0)
    gram_0 = lax.all_gather(other_0, "feat", axis=0, tiled=True)

    halves_2, keeps_2, sends_2 = cube_gram(same_2, cross_2)
    for step in (0, 1, 2):
        keeps_2, sends_2 = fold(keeps_2, sends_2, step)
    piece_2 = fold(keeps_2, sends_2, 3)
    match_2, _, owns_2 = other_core(piece_2)
    gram_1, owns_2[0] = lax.optimization_barrier((gram_1, owns_2[0]))
    ahead_1, turned = local_call(
        both_kernel,
        (),
        (gram_1, high_0, low_0, *halves_1),
        [shape(block, cols)] * 2,
        scratch=row_scratch,
        flops=2 * product,
    )
    above = lax.ppermute(turned, "batch", up)
    for step in (3, 2, 1):
        cames = step_across(owns_2, step)
        owns_2 = local_call(
            join_kernel, (), (*owns_2, *cames), [shape(2 * owns_2[0].shape[0], quarter)] * 4
        )
    cames_2 = step_across(owns_2, 0)

    square = (match_0 + 2.0 * match_1 + match_2) * (0.5 / (float(clip_total) * float(clip_total)))
    local_loss = off_weight * square + (
        jnp.sum((1.0 - diagonal) ** 2) - off_weight * jnp.sum(diagonal * diagonal)
    ) / batch
    local_loss = jnp.broadcast_to(local_loss, (1, 128))
    for bit in range(4):
        local_loss = local_loss + across(local_loss, bit)
    cames_2[0], local_loss = lax.optimization_barrier((cames_2[0], local_loss))
    (ahead_2,) = local_call(
        one_kernel,
        (label,),
        (*owns_2, *cames_2, *halves_2),
        [shape(block, cols)],
        scratch=row_scratch,
        flops=product,
    )
    gram_0, ahead_2 = lax.optimization_barrier((gram_0, ahead_2))
    factor = 2.0 * off_weight / (float(clip_total) * float(clip_total))
    kept, sent, own_sums = local_call(
        last_kernel,
        (jnp.full((1,), factor, f32), core.astype(jnp.int32).reshape((1,))),
        (gram_0, high_0, low_0, ahead_1, ahead_2, above),
        [shape(rows, cols)] * 2 + [shape(8, cols)],
        scratch=[pltpu.VMEM((block, cols), f32)],
        flops=product,
    )

    came = lax.ppermute(sent, "batch", swap)
    normed_one = (view_one - center_one) * scale_one
    normed_two = (view_two - center_two) * scale_two
    weight = (-2.0 * (1.0 - diagonal) - 2.0 * off_weight * diagonal) / clip_total
    gnorm_one = pick(kept, came) + normed_two * weight
    gnorm_two = pick(came, kept) + normed_one * weight
    zero = jnp.zeros((cols,), f32)
    product_sum = jnp.sum(normed_one * normed_two, axis=0) * weight
    sums = jnp.stack(
        [
            pick(own_sums[0], zero) + jnp.sum(normed_two, axis=0) * weight,
            pick(own_sums[1], zero) + product_sum,
            pick(zero, own_sums[0]) + jnp.sum(normed_one, axis=0) * weight,
            pick(zero, own_sums[1]) + product_sum,
        ]
    )
    sums, loss_total = lax.psum((sums, local_loss), "batch")
    sums = sums / clip_total
    grad_one = clip_total * (gnorm_one - sums[0] - normed_one * sums[1]) * scale_one
    grad_two = clip_total * (gnorm_two - sums[2] - normed_two * sums[3]) * scale_two
    return (grad_one, grad_two, loss_total[0, 0] / features)


def solution(mesh):
    placed = (P("batch", "feat"), P("batch", "feat"))
    return jax.shard_map(
        body,
        mesh=mesh,
        in_specs=placed,
        out_specs=(P("batch", "feat"), P("batch", "feat"), P()),
        check_vma=False,
    )
```

```python
import jax
import jax.numpy as jnp
from jax import lax
from jax.experimental import pallas as pl
from jax.experimental.pallas import tpu as pltpu
from jax.sharding import PartitionSpec as P

epsilon = 1e-05
off_weight = 0.005
f32 = jnp.float32
bf16 = jnp.bfloat16

gray = (0, 1, 3, 2)
label_of = tuple(gray[i // 4] * 4 + gray[i % 4] for i in range(16))
feat_of = tuple(label_of.index(i) for i in range(16))
orders = ((3, 2, 1, 0), (2, 3, 0, 1), (1, 0, 3, 2), (0, 1, 2, 3))
masks = tuple(
    tuple(sum(((p >> (3 - j)) & 1) << order[j] for j in range(4)) for p in range(16))
    for order in orders
)

vmem = pl.BlockSpec(memory_space=pltpu.VMEM)
smem = pl.BlockSpec(memory_space=pltpu.SMEM)


def local_call(kernel, scalars, arrays, outs, scratch=(), flops=0):
    moved = sum(a.size * a.dtype.itemsize for a in (*arrays, *outs))
    call = pl.pallas_call(
        kernel,
        out_shape=list(outs),
        in_specs=[smem] * len(scalars) + [vmem] * len(arrays),
        out_specs=[vmem] * len(outs),
        scratch_shapes=list(scratch),
        compiler_params=pltpu.CompilerParams(vmem_limit_bytes=44 * 1024 * 1024),
        cost_estimate=pl.CostEstimate(flops=flops, bytes_accessed=moved, transcendentals=0),
    )
    return list(call(*scalars, *arrays))


def shape(rows, cols, dtype=f32):
    return jax.ShapeDtypeStruct((rows, cols), dtype)


def split(value):
    high = value.astype(bf16)
    return high, (value - high.astype(f32)).astype(bf16)


def dot3(left, right, left_dim, right_dim):
    def one(a, b):
        return lax.dot_general(
            a, b, (((left_dim,), (right_dim,)), ((), ())), preferred_element_type=f32
        )

    return one(left[0], right[0]) + (one(left[0], right[1]) + one(left[1], right[0]))


def normalize(first_ref, same, cross, center, scale, high, low):
    rows = same.shape[0]

    def put(source, at):
        high[at : at + rows, :], low[at : at + rows, :] = split(
            (source[...] - center[...]) * scale[...]
        )

    @pl.when(first_ref[0] == 1)
    def _():
        put(same, 0)
        put(cross, rows)

    @pl.when(first_ref[0] != 1)
    def _():
        put(cross, 0)
        put(same, rows)


def own_kernel(first, same, cross, center, scale, high, low, gram):
    normalize(first, same, cross, center, scale, high, low)
    quarter = gram.shape[1] // 4
    for q in range(4):
        part = slice(q * quarter, (q + 1) * quarter)
        gram[:, part] = dot3(
            (high[...], low[...]), (high[part, :], low[part, :]), 1, 1
        )


def far_kernel(first, same, cross, center, scale, high_0, low_0, high, low, gram):
    normalize(first, same, cross, center, scale, high, low)
    quarter = gram.shape[1] // 4
    for q in range(4):
        part = slice(q * quarter, (q + 1) * quarter)
        gram[:, part] = dot3((high_0[...], low_0[...]), (high[part, :], low[part, :]), 1, 1)


def cube_kernel(first, label, same, cross, center, scale, high_0, low_0, high, low, *rest):
    keeps, sends, whole = rest[:4], rest[4:8], rest[8]
    normalize(first, same, cross, center, scale, high, low)
    quarter = whole.shape[1]
    chunk = whole.shape[0] // 16
    for q in range(4):
        part = slice(q * quarter, (q + 1) * quarter)
        whole[...] = dot3((high_0[...], low_0[...]), (high[part, :], low[part, :]), 1, 1)
        for p in range(16):
            at = pl.multiple_of((label[0] ^ masks[q][p]) * chunk, chunk)
            target = keeps[q] if p < 8 else sends[q]
            target[p % 8 * chunk : (p % 8 + 1) * chunk, :] = whole[pl.ds(at, chunk), :]


def front_kernel(first, one, two, stats, same, cross):
    rows = one.shape[0]
    mean_one = jnp.sum(one[...], axis=0, keepdims=True) / rows
    mean_two = jnp.sum(two[...], axis=0, keepdims=True) / rows
    deviate_one = one[...] - mean_one
    deviate_two = two[...] - mean_two
    stats[...] = jnp.zeros(stats.shape, f32)
    stats[0:1, :] = mean_one
    stats[1:2, :] = mean_two
    stats[2:3, :] = jnp.sum(deviate_one * deviate_one, axis=0, keepdims=True)
    stats[3:4, :] = jnp.sum(deviate_two * deviate_two, axis=0, keepdims=True)
    stats[4:5, :] = jnp.sum(deviate_one * deviate_two, axis=0, keepdims=True)

    @pl.when(first[0] == 1)
    def _():
        same[...] = one[...]
        cross[...] = two[...]

    @pl.when(first[0] != 1)
    def _():
        same[...] = two[...]
        cross[...] = one[...]


def fold_kernel(*refs):
    half = refs[0].shape[0] // 2
    for q in range(4):
        keep, came, keep_out, send_out = refs[q::4]
        keep_out[...] = keep[:half, :] + came[:half, :]
        send_out[...] = keep[half:, :] + came[half:, :]


def last_fold_kernel(*refs):
    out = refs[8]
    cols = refs[0].shape[1]
    for q in range(4):
        out[:, q * cols : (q + 1) * cols] = refs[q][...] + refs[4 + q][...]


def match_kernel(mine, other, match, *parts):
    cols = parts[0].shape[1]
    for q in range(4):
        parts[q][...] = other[:, q * cols : (q + 1) * cols]
    match[...] = jnp.full(match.shape, jnp.sum(mine[...] * other[...]), f32)


def join_kernel(*refs):
    rows = refs[0].shape[0]
    for q in range(4):
        own, came, out = refs[q::4]
        out[:rows, :] = own[...]
        out[rows:, :] = came[...]


def gather_rows(label, q, own, came, high, low, by_feat):
    half, cols = own.shape
    chunk = half // 8
    for p in range(16):
        source = own if p < 8 else came
        owner = label[0] ^ masks[q][p]
        if by_feat:
            owner = owner ^ ((owner >> 1) & 5)
        at = pl.multiple_of(owner * chunk, chunk)
        high[pl.ds(at, chunk), :], low[pl.ds(at, chunk), :] = split(
            source[p % 8 * chunk : (p % 8 + 1) * chunk, :]
        )


def both_kernel(label, *refs):
    owns, cames = refs[:4], refs[4:8]
    high_0, low_0, high_1, low_1, ahead, turned, high, low = refs[8:]
    quarter = owns[0].shape[1]
    for q in range(4):
        part = slice(q * quarter, (q + 1) * quarter)
        gather_rows(label, q, owns[q], cames[q], high, low, False)
        gram = (high[...], low[...])
        term = dot3(gram, (high_1[part, :], low_1[part, :]), 1, 0)
        ahead[...] = term if q == 0 else ahead[...] + term
        turned[part, :] = dot3(gram, (high_0[...], low_0[...]), 0, 0)


def one_kernel(label, *refs):
    owns, cames = refs[:4], refs[4:8]
    high_2, low_2, one, two, ahead, high, low = refs[8:]
    quarter = owns[0].shape[1]
    ahead[...] = one[...] + two[...]
    for q in range(4):
        part = slice(q * quarter, (q + 1) * quarter)
        gather_rows(label, q, owns[q], cames[q], high, low, True)
        ahead[...] += dot3((high[...], low[...]), (high_2[part, :], low_2[part, :]), 1, 0)


def last_kernel(factor, core, gram, high_0, low_0, rest, kept, sent, sums, total, high, low):
    rows = kept.shape[0]
    quarter = gram.shape[1] // 4
    chunk = total.shape[0] // 16
    step = gram.shape[0] // 16
    total[...] = rest[...]
    for q in range(4):
        part = slice(q * quarter, (q + 1) * quarter)
        for i in range(16):
            at = slice(i * chunk, (i + 1) * chunk)
            high[at, :], low[at, :] = split(gram[i * step : i * step + chunk, part])
        total[...] += dot3((high[...], low[...]), (high_0[part, :], low_0[part, :]), 1, 0)
    total[...] = total[...] * factor[0]
    normed = high_0[...].astype(f32) + low_0[...].astype(f32)
    sums[...] = jnp.zeros(sums.shape, f32)
    sums[0:1, :] = jnp.sum(total[...], axis=0, keepdims=True)
    sums[1:2, :] = jnp.sum(total[...] * normed, axis=0, keepdims=True)
    for i in range(16):
        at = slice(i * step + chunk, i * step + chunk + 1)
        sums[2:3, :] = sums[2:3, :] + gram[at, : sums.shape[1]]
    kept[...] = total[pl.ds(pl.multiple_of(core[0] * rows, rows), rows), :]
    sent[...] = total[pl.ds(pl.multiple_of((1 - core[0]) * rows, rows), rows), :]


def across(array, bit):
    return lax.ppermute(
        array, "feat", [(i, feat_of[label_of[i] ^ (1 << bit)]) for i in range(16)]
    )


def step_across(arrays, step):
    return [across(array, order[step]) for array, order in zip(arrays, orders)]


def fold(keeps, sends, step):
    cames = step_across(sends, step)
    rows, cols = keeps[0].shape
    if step == 3:
        return local_call(last_fold_kernel, (), (*keeps, *cames), [shape(rows, 4 * cols)])[0]
    outs = local_call(fold_kernel, (), (*keeps, *cames), [shape(rows // 2, cols)] * 8)
    return outs[:4], outs[4:]


def body(view_one, view_two):
    rows, cols = view_one.shape
    batch = lax.axis_size("batch")
    feats = lax.axis_size("feat")
    clip_total = rows * batch
    features = cols * feats
    core = lax.axis_index("batch") % 2
    on_first = core == 0
    first = (1 - core).astype(jnp.int32).reshape((1,))
    label = jnp.array(label_of, jnp.int32)[lax.axis_index("feat")].reshape((1,))
    swap = [(i, i ^ 1) for i in range(batch)]
    down = [(i, (i - 2) % batch) for i in range(batch)]
    up = [(i, (i + 2) % batch) for i in range(batch)]
    down_cross = [(i, (i ^ 1) - 2 if i > 1 else (i ^ 1) - 2 + batch) for i in range(batch)]
    up_cross = [(i, ((i ^ 1) + 2) % batch) for i in range(batch)]

    def pick(one, two):
        return jnp.where(on_first, one, two)

    mine, same_0, mine_cross = local_call(
        front_kernel,
        (first,),
        (view_one, view_two),
        [shape(8, cols), shape(rows, cols), shape(rows, cols)],
    )
    parts = lax.all_gather(mine, "batch", axis=0)
    parts, far_same, far_cross = lax.optimization_barrier((parts, same_0, mine_cross))
    cross_0 = lax.ppermute(far_cross, "batch", swap)
    center_one = jnp.mean(parts[:, 0], axis=0)
    center_two = jnp.mean(parts[:, 1], axis=0)
    shift_one = parts[:, 0] - center_one
    shift_two = parts[:, 1] - center_two
    spread_one = jnp.sum(parts[:, 2] + rows * shift_one * shift_one, axis=0) / clip_total
    spread_two = jnp.sum(parts[:, 3] + rows * shift_two * shift_two, axis=0) / clip_total
    scale_one = 1.0 / jnp.sqrt(spread_one + epsilon)
    scale_two = 1.0 / jnp.sqrt(spread_two + epsilon)
    covary = jnp.sum(parts[:, 4] + rows * shift_one * shift_two, axis=0) / clip_total
    diagonal = covary * scale_one * scale_two
    center = pick(center_one, center_two).reshape((1, cols))
    scale = pick(scale_one, scale_two).reshape((1, cols))

    same_1 = lax.ppermute(far_same, "batch", down)
    cross_1 = lax.ppermute(far_cross, "batch", down_cross)
    cross_up = lax.ppermute(far_cross, "batch", up_cross)
    block = 2 * rows
    quarter = block // 4
    product = 3 * 2 * block * block * cols
    halves = [shape(block, cols, bf16)] * 2
    row_scratch = [pltpu.VMEM((block, quarter), bf16)] * 2

    high_0, low_0, gram = local_call(
        own_kernel,
        (first,),
        (same_0, cross_0, center, scale),
        halves + [shape(block, block)],
        flops=product,
    )
    piece_0 = lax.psum_scatter(gram, "feat", scatter_dimension=0, tiled=True)
    same_1, cross_1, high_0, low_0 = lax.optimization_barrier((same_1, cross_1, high_0, low_0))

    def cube_gram(same, cross):
        outs = local_call(
            cube_kernel,
            (first, label),
            (same, cross, center, scale, high_0, low_0),
            halves + [shape(block // 2, quarter)] * 8,
            scratch=[pltpu.VMEM((block, quarter), f32)],
            flops=product,
        )
        return outs[:2], outs[2:6], outs[6:]

    def other_core(piece):
        other = lax.ppermute(piece, "batch", swap)
        match, *owns = local_call(
            match_kernel, (), (piece, other), [shape(8, 128)] + [shape(block // 16, quarter)] * 4
        )
        return match[0, 0], other, owns

    def cube_gather(owns):
        for step in (3, 2, 1):
            cames = step_across(owns, step)
            owns = local_call(
                join_kernel, (), (*owns, *cames), [shape(2 * owns[0].shape[0], quarter)] * 4
            )
        return owns + step_across(owns, 0)

    halves_1, keeps_1, sends_1 = cube_gram(same_1, cross_1)
    same_2 = lax.ppermute(same_1, "batch", down)
    cross_2 = lax.ppermute(cross_up, "batch", up)
    for step in (0, 1):
        keeps_1, sends_1 = fold(keeps_1, sends_1, step)
    same_2, cross_2, keeps_1[0] = lax.optimization_barrier((same_2, cross_2, keeps_1[0]))
    high_2, low_2, gram = local_call(
        far_kernel,
        (first,),
        (same_2, cross_2, center, scale, high_0, low_0),
        halves + [shape(block, block)],
        flops=product,
    )
    sends_1[0], gram = lax.optimization_barrier((sends_1[0], gram))
    piece_2 = lax.psum_scatter(gram, "feat", scatter_dimension=0, tiled=True)
    keeps_1, sends_1 = fold(keeps_1, sends_1, 2)
    piece_1 = fold(keeps_1, sends_1, 3)
    match_1, _, owns_1 = other_core(piece_1)
    gathered_1 = cube_gather(owns_1)
    ahead_1, turned = local_call(
        both_kernel,
        (label,),
        (*gathered_1, high_0, low_0, *halves_1),
        [shape(block, cols)] * 2,
        scratch=row_scratch,
        flops=2 * product,
    )
    above = lax.ppermute(turned, "batch", up)

    piece_0, piece_2, ahead_1 = lax.optimization_barrier((piece_0, piece_2, ahead_1))
    match_0, other_0, _ = other_core(piece_0)
    match_2, _, owns_2 = other_core(piece_2)
    square = (match_0 + 2.0 * match_1 + match_2) * (0.5 / (float(clip_total) * float(clip_total)))
    local_loss = off_weight * square + (
        jnp.sum((1.0 - diagonal) ** 2) - off_weight * jnp.sum(diagonal * diagonal)
    ) / batch
    extended = jnp.concatenate([other_0, jnp.broadcast_to(local_loss, (8, block))], axis=0)
    gram_0 = lax.all_gather(extended, "feat", axis=0, tiled=True)
    gathered_2 = cube_gather(owns_2)
    (rest,) = local_call(
        one_kernel,
        (label,),
        (*gathered_2, high_2, low_2, ahead_1, above),
        [shape(block, cols)],
        scratch=row_scratch,
        flops=product,
    )
    gram_0, rest = lax.optimization_barrier((gram_0, rest))
    factor = 2.0 * off_weight / (float(clip_total) * float(clip_total))
    kept, sent, own_sums = local_call(
        last_kernel,
        (jnp.full((1,), factor, f32), core.astype(jnp.int32).reshape((1,))),
        (gram_0, high_0, low_0, rest),
        [shape(rows, cols)] * 2 + [shape(8, cols)],
        scratch=[pltpu.VMEM((block, cols), f32)] + row_scratch,
        flops=product,
    )

    came = lax.ppermute(sent, "batch", swap)
    normed_one = (view_one - center_one) * scale_one
    normed_two = (view_two - center_two) * scale_two
    weight = (-2.0 * (1.0 - diagonal) - 2.0 * off_weight * diagonal) / clip_total
    gnorm_one = pick(kept, came) + normed_two * weight
    gnorm_two = pick(came, kept) + normed_one * weight
    zero = jnp.zeros((cols,), f32)
    product_sum = jnp.sum(normed_one * normed_two, axis=0) * weight
    sums = jnp.stack(
        [
            pick(own_sums[0], zero) + jnp.sum(normed_two, axis=0) * weight,
            pick(own_sums[1], zero) + product_sum,
            pick(zero, own_sums[0]) + jnp.sum(normed_one, axis=0) * weight,
            pick(zero, own_sums[1]) + product_sum,
        ]
    )
    sums, loss_total = lax.psum((sums, own_sums[2, :128]), "batch")
    sums = sums / clip_total
    grad_one = clip_total * (gnorm_one - sums[0] - normed_one * sums[1]) * scale_one
    grad_two = clip_total * (gnorm_two - sums[2] - normed_two * sums[3]) * scale_two
    return (grad_one, grad_two, loss_total[0] / features)


def solution(mesh):
    placed = (P("batch", "feat"), P("batch", "feat"))
    return jax.shard_map(
        body,
        mesh=mesh,
        in_specs=placed,
        out_specs=(P("batch", "feat"), P("batch", "feat"), P()),
        check_vma=False,
    )
```

```python
import jax
import jax.numpy as jnp
from jax import lax
from jax.experimental import pallas as pl
from jax.experimental.pallas import tpu as pltpu
from jax.sharding import PartitionSpec as P

epsilon = 1e-05
off_weight = 0.005
f32 = jnp.float32
bf16 = jnp.bfloat16

gray = (0, 1, 3, 2)
label_of = tuple(gray[i // 4] * 4 + gray[i % 4] for i in range(16))
feat_of = tuple(label_of.index(i) for i in range(16))
orders = ((3, 2, 1, 0), (2, 3, 0, 1), (1, 0, 3, 2), (0, 1, 2, 3))
masks = tuple(
    tuple(sum(((p >> (3 - j)) & 1) << order[j] for j in range(4)) for p in range(16))
    for order in orders
)

vmem = pl.BlockSpec(memory_space=pltpu.VMEM)
smem = pl.BlockSpec(memory_space=pltpu.SMEM)


def local_call(kernel, scalars, arrays, outs, scratch=(), flops=0):
    moved = sum(a.size * a.dtype.itemsize for a in (*arrays, *outs))
    call = pl.pallas_call(
        kernel,
        out_shape=list(outs),
        in_specs=[smem] * len(scalars) + [vmem] * len(arrays),
        out_specs=[vmem] * len(outs),
        scratch_shapes=list(scratch),
        compiler_params=pltpu.CompilerParams(vmem_limit_bytes=44 * 1024 * 1024),
        cost_estimate=pl.CostEstimate(flops=flops, bytes_accessed=moved, transcendentals=0),
    )
    return list(call(*scalars, *arrays))


def shape(rows, cols, dtype=f32):
    return jax.ShapeDtypeStruct((rows, cols), dtype)


def split(value):
    high = value.astype(bf16)
    return high, (value - high.astype(f32)).astype(bf16)


def dot3(left, right, left_dim, right_dim):
    def one(a, b):
        return lax.dot_general(
            a, b, (((left_dim,), (right_dim,)), ((), ())), preferred_element_type=f32
        )

    return one(left[0], right[0]) + (one(left[0], right[1]) + one(left[1], right[0]))


def normalize(first_ref, same, cross, center, scale, high, low):
    rows = same.shape[0]

    def put(source, at):
        high[at : at + rows, :], low[at : at + rows, :] = split(
            (source[...] - center[...]) * scale[...]
        )

    @pl.when(first_ref[0] == 1)
    def _():
        put(same, 0)
        put(cross, rows)

    @pl.when(first_ref[0] != 1)
    def _():
        put(cross, 0)
        put(same, rows)


def own_kernel(first, same, cross, center, scale, high, low, gram):
    normalize(first, same, cross, center, scale, high, low)
    quarter = gram.shape[1] // 4
    for q in range(4):
        part = slice(q * quarter, (q + 1) * quarter)
        gram[:, part] = dot3(
            (high[...], low[...]), (high[part, :], low[part, :]), 1, 1
        )


def far_kernel(first, same, cross, center, scale, high_0, low_0, high, low, gram):
    normalize(first, same, cross, center, scale, high, low)
    quarter = gram.shape[1] // 4
    for q in range(4):
        part = slice(q * quarter, (q + 1) * quarter)
        gram[:, part] = dot3((high_0[...], low_0[...]), (high[part, :], low[part, :]), 1, 1)


def cube_kernel(first, label, same, cross, center, scale, high_0, low_0, high, low, *rest):
    keeps, sends, whole = rest[:4], rest[4:8], rest[8]
    normalize(first, same, cross, center, scale, high, low)
    quarter = whole.shape[1]
    chunk = whole.shape[0] // 16
    for q in range(4):
        part = slice(q * quarter, (q + 1) * quarter)
        whole[...] = dot3((high_0[...], low_0[...]), (high[part, :], low[part, :]), 1, 1)
        for p in range(16):
            at = pl.multiple_of((label[0] ^ masks[q][p]) * chunk, chunk)
            target = keeps[q] if p < 8 else sends[q]
            target[p % 8 * chunk : (p % 8 + 1) * chunk, :] = whole[pl.ds(at, chunk), :]


def front_kernel(first, one, two, stats, same, cross):
    rows = one.shape[0]
    mean_one = jnp.sum(one[...], axis=0, keepdims=True) / rows
    mean_two = jnp.sum(two[...], axis=0, keepdims=True) / rows
    deviate_one = one[...] - mean_one
    deviate_two = two[...] - mean_two
    stats[...] = jnp.zeros(stats.shape, f32)
    stats[0:1, :] = mean_one
    stats[1:2, :] = mean_two
    stats[2:3, :] = jnp.sum(deviate_one * deviate_one, axis=0, keepdims=True)
    stats[3:4, :] = jnp.sum(deviate_two * deviate_two, axis=0, keepdims=True)
    stats[4:5, :] = jnp.sum(deviate_one * deviate_two, axis=0, keepdims=True)

    @pl.when(first[0] == 1)
    def _():
        same[...] = one[...]
        cross[...] = two[...]

    @pl.when(first[0] != 1)
    def _():
        same[...] = two[...]
        cross[...] = one[...]


def fold_kernel(*refs):
    half = refs[0].shape[0] // 2
    for q in range(4):
        keep, came, keep_out, send_out = refs[q::4]
        keep_out[...] = keep[:half, :] + came[:half, :]
        send_out[...] = keep[half:, :] + came[half:, :]


def last_fold_kernel(*refs):
    out = refs[8]
    cols = refs[0].shape[1]
    for q in range(4):
        out[:, q * cols : (q + 1) * cols] = refs[q][...] + refs[4 + q][...]


def match_kernel(mine, other, match):
    match[...] = jnp.full(match.shape, jnp.sum(mine[...] * other[...]), f32)


def part_kernel(other, *parts):
    cols = parts[0].shape[1]
    for q in range(4):
        parts[q][...] = other[:, q * cols : (q + 1) * cols]


def part_loss_kernel(loss, mine, other, *parts):
    rows, cols = other.shape[0], parts[0].shape[1]
    share = loss[0] + loss[1] * jnp.sum(mine[...] * other[...])
    for q in range(4):
        parts[q][:rows, :] = other[:, q * cols : (q + 1) * cols]
        parts[q][rows:, :] = jnp.full((8, cols), share, f32)


def join_kernel(*refs):
    rows = refs[0].shape[0]
    for q in range(4):
        own, came, out = refs[q::4]
        out[:rows, :] = own[...]
        out[rows:, :] = came[...]


def gather_rows(label, q, own, came, high, low, by_feat):
    chunk = high.shape[0] // 16
    step = own.shape[0] // 8
    for p in range(16):
        source = own if p < 8 else came
        owner = label[0] ^ masks[q][p]
        if by_feat:
            owner = owner ^ ((owner >> 1) & 5)
        at = pl.multiple_of(owner * chunk, chunk)
        high[pl.ds(at, chunk), :], low[pl.ds(at, chunk), :] = split(
            source[p % 8 * step : p % 8 * step + chunk, :]
        )


def both_kernel(label, *refs):
    owns, cames = refs[:4], refs[4:8]
    high_0, low_0, high_1, low_1, ahead, turned, high, low = refs[8:]
    quarter = owns[0].shape[1]
    for q in range(4):
        part = slice(q * quarter, (q + 1) * quarter)
        gather_rows(label, q, owns[q], cames[q], high, low, False)
        gram = (high[...], low[...])
        term = dot3(gram, (high_1[part, :], low_1[part, :]), 1, 0)
        ahead[...] = term if q == 0 else ahead[...] + term
        turned[part, :] = dot3(gram, (high_0[...], low_0[...]), 0, 0)


def one_kernel(label, *refs):
    owns, cames = refs[:4], refs[4:8]
    high_2, low_2, one, two, ahead, loss, high, low = refs[8:]
    quarter = owns[0].shape[1]
    ahead[...] = one[...] + two[...]
    for q in range(4):
        part = slice(q * quarter, (q + 1) * quarter)
        gather_rows(label, q, owns[q], cames[q], high, low, True)
        ahead[...] += dot3((high[...], low[...]), (high_2[part, :], low_2[part, :]), 1, 0)
    chunk = high.shape[0] // 16
    step = owns[0].shape[0] // 8
    total = jnp.zeros((8, 128), f32)
    for p in range(8):
        at = slice(p * step + chunk, (p + 1) * step)
        total += owns[0][at, :128] + cames[0][at, :128]
    loss[...] = total


def last_kernel(factor, core, gram, high_0, low_0, rest, kept, sent, sums, total):
    rows = kept.shape[0]
    quarter = gram.shape[1]
    q = pl.program_id(0)

    @pl.when(q == 0)
    def _():
        total[...] = rest[...]

    part = pl.ds(pl.multiple_of(q * quarter, quarter), quarter)
    total[...] += dot3(split(gram[...]), (high_0[part, :], low_0[part, :]), 1, 0)

    @pl.when(q == 3)
    def _():
        scaled = total[...] * factor[0]
        total[...] = scaled
        normed = high_0[...].astype(f32) + low_0[...].astype(f32)
        sums[...] = jnp.zeros(sums.shape, f32)
        sums[0:1, :] = jnp.sum(scaled, axis=0, keepdims=True)
        sums[1:2, :] = jnp.sum(scaled * normed, axis=0, keepdims=True)
        kept[...] = total[pl.ds(pl.multiple_of(core[0] * rows, rows), rows), :]
        sent[...] = total[pl.ds(pl.multiple_of((1 - core[0]) * rows, rows), rows), :]


def across(array, bit):
    return lax.ppermute(
        array, "feat", [(i, feat_of[label_of[i] ^ (1 << bit)]) for i in range(16)]
    )


def step_across(arrays, step):
    return [across(array, order[step]) for array, order in zip(arrays, orders)]


def fold(keeps, sends, step):
    cames = step_across(sends, step)
    rows, cols = keeps[0].shape
    if step == 3:
        return local_call(last_fold_kernel, (), (*keeps, *cames), [shape(rows, 4 * cols)])[0]
    outs = local_call(fold_kernel, (), (*keeps, *cames), [shape(rows // 2, cols)] * 8)
    return outs[:4], outs[4:]


def body(view_one, view_two):
    rows, cols = view_one.shape
    batch = lax.axis_size("batch")
    feats = lax.axis_size("feat")
    clip_total = rows * batch
    features = cols * feats
    core = lax.axis_index("batch") % 2
    on_first = core == 0
    first = (1 - core).astype(jnp.int32).reshape((1,))
    label = jnp.array(label_of, jnp.int32)[lax.axis_index("feat")].reshape((1,))
    swap = [(i, i ^ 1) for i in range(batch)]
    down = [(i, (i - 2) % batch) for i in range(batch)]
    up = [(i, (i + 2) % batch) for i in range(batch)]
    down_cross = [(i, (i ^ 1) - 2 if i > 1 else (i ^ 1) - 2 + batch) for i in range(batch)]
    far_cross_pairs = [(i, ((i ^ 1) + 4) % batch) for i in range(batch)]

    def pick(one, two):
        return jnp.where(on_first, one, two)

    mine, same_0, mine_cross = local_call(
        front_kernel,
        (first,),
        (view_one, view_two),
        [shape(8, cols), shape(rows, cols), shape(rows, cols)],
    )
    parts = lax.all_gather(mine, "batch", axis=0)
    parts, far_same, far_cross = lax.optimization_barrier((parts, same_0, mine_cross))
    cross_0 = lax.ppermute(far_cross, "batch", swap)
    center_one = jnp.mean(parts[:, 0], axis=0)
    center_two = jnp.mean(parts[:, 1], axis=0)
    shift_one = parts[:, 0] - center_one
    shift_two = parts[:, 1] - center_two
    spread_one = jnp.sum(parts[:, 2] + rows * shift_one * shift_one, axis=0) / clip_total
    spread_two = jnp.sum(parts[:, 3] + rows * shift_two * shift_two, axis=0) / clip_total
    scale_one = 1.0 / jnp.sqrt(spread_one + epsilon)
    scale_two = 1.0 / jnp.sqrt(spread_two + epsilon)
    covary = jnp.sum(parts[:, 4] + rows * shift_one * shift_two, axis=0) / clip_total
    diagonal = covary * scale_one * scale_two
    center = pick(center_one, center_two).reshape((1, cols))
    scale = pick(scale_one, scale_two).reshape((1, cols))

    same_1 = lax.ppermute(far_same, "batch", down)
    cross_1 = lax.ppermute(far_cross, "batch", down_cross)
    cross_2 = lax.ppermute(far_cross, "batch", far_cross_pairs)
    block = 2 * rows
    quarter = block // 4
    product = 3 * 2 * block * block * cols
    halves = [shape(block, cols, bf16)] * 2
    row_scratch = [pltpu.VMEM((block, quarter), bf16)] * 2

    high_0, low_0, gram = local_call(
        own_kernel,
        (first,),
        (same_0, cross_0, center, scale),
        halves + [shape(block, block)],
        flops=product,
    )
    piece_0 = lax.psum_scatter(gram, "feat", scatter_dimension=0, tiled=True)
    same_1, cross_1, cross_2, high_0, low_0 = lax.optimization_barrier(
        (same_1, cross_1, cross_2, high_0, low_0)
    )

    def cube_gram(same, cross):
        outs = local_call(
            cube_kernel,
            (first, label),
            (same, cross, center, scale, high_0, low_0),
            halves + [shape(block // 2, quarter)] * 8,
            scratch=[pltpu.VMEM((block, quarter), f32)],
            flops=product,
        )
        return outs[:2], outs[2:6], outs[6:]

    def other_core(piece):
        return lax.ppermute(piece, "batch", swap)

    def match(piece, other):
        return local_call(match_kernel, (), (piece, other), [shape(8, 128)])[0][0, 0]

    def cube_gather(owns):
        for step in (3, 2, 1):
            cames = step_across(owns, step)
            owns = local_call(
                join_kernel, (), (*owns, *cames), [shape(2 * owns[0].shape[0], quarter)] * 4
            )
        return owns + step_across(owns, 0)

    halves_1, keeps_1, sends_1 = cube_gram(same_1, cross_1)
    same_2 = lax.ppermute(same_1, "batch", down)
    for step in (0, 1):
        keeps_1, sends_1 = fold(keeps_1, sends_1, step)
    same_2, cross_2, keeps_1[0] = lax.optimization_barrier((same_2, cross_2, keeps_1[0]))
    high_2, low_2, gram = local_call(
        far_kernel,
        (first,),
        (same_2, cross_2, center, scale, high_0, low_0),
        halves + [shape(block, block)],
        flops=product,
    )
    sends_1[0], gram = lax.optimization_barrier((sends_1[0], gram))
    piece_2 = lax.psum_scatter(gram, "feat", scatter_dimension=0, tiled=True)
    keeps_1, sends_1 = fold(keeps_1, sends_1, 2)
    piece_1 = fold(keeps_1, sends_1, 3)
    piece_0, piece_1 = lax.optimization_barrier((piece_0, piece_1))
    other_1 = other_core(piece_1)
    other_0 = other_core(piece_0)
    gram_0 = lax.all_gather(other_0, "feat", axis=0, tiled=True)
    owns_1 = local_call(
        part_kernel, (), (other_1,), [shape(block // 16, quarter)] * 4
    )
    gathered_1 = cube_gather(owns_1)
    square = match(piece_0, other_0) + 2.0 * match(piece_1, other_1)
    ahead_1, turned = local_call(
        both_kernel,
        (label,),
        (*gathered_1, high_0, low_0, *halves_1),
        [shape(block, cols)] * 2,
        scratch=row_scratch,
        flops=2 * product,
    )
    above = lax.ppermute(turned, "batch", up)

    square_weight = off_weight * 0.5 / (float(clip_total) * float(clip_total))
    share = square_weight * square + (
        jnp.sum((1.0 - diagonal) ** 2) - off_weight * jnp.sum(diagonal * diagonal)
    ) / batch
    share = jnp.stack([share, jnp.full((), square_weight, f32)])
    piece_2, ahead_1, share = lax.optimization_barrier((piece_2, ahead_1, share))
    other_2 = other_core(piece_2)
    owns_2 = local_call(
        part_loss_kernel,
        (share,),
        (piece_2, other_2),
        [shape(block // 16 + 8, quarter)] * 4,
    )
    gathered_2 = cube_gather(owns_2)
    rest, loss_sum = local_call(
        one_kernel,
        (label,),
        (*gathered_2, high_2, low_2, ahead_1, above),
        [shape(block, cols), shape(8, 128)],
        scratch=row_scratch,
        flops=product,
    )
    gram_0, rest = lax.optimization_barrier((gram_0, rest))
    factor = 2.0 * off_weight / (float(clip_total) * float(clip_total))

    def whole(rows, cols):
        return pl.BlockSpec((rows, cols), lambda q: (0, 0))

    kept, sent, own_sums = pl.pallas_call(
        last_kernel,
        out_shape=[shape(rows, cols), shape(rows, cols), shape(8, cols)],
        grid=(4,),
        in_specs=[
            smem,
            smem,
            pl.BlockSpec((block, quarter), lambda q: (0, q)),
            whole(block, cols),
            whole(block, cols),
            whole(block, cols),
        ],
        out_specs=[whole(rows, cols), whole(rows, cols), whole(8, cols)],
        scratch_shapes=[pltpu.VMEM((block, cols), f32)],
        compiler_params=pltpu.CompilerParams(vmem_limit_bytes=44 * 1024 * 1024),
        cost_estimate=pl.CostEstimate(
            flops=product, bytes_accessed=12 * 1024 * 1024, transcendentals=0
        ),
    )(
        jnp.full((1,), factor, f32),
        core.astype(jnp.int32).reshape((1,)),
        gram_0,
        high_0,
        low_0,
        rest,
    )

    came = lax.ppermute(sent, "batch", swap)
    normed_one = (view_one - center_one) * scale_one
    normed_two = (view_two - center_two) * scale_two
    weight = (-2.0 * (1.0 - diagonal) - 2.0 * off_weight * diagonal) / clip_total
    gnorm_one = pick(kept, came) + normed_two * weight
    gnorm_two = pick(came, kept) + normed_one * weight
    zero = jnp.zeros((cols,), f32)
    product_sum = jnp.sum(normed_one * normed_two, axis=0) * weight
    sums = jnp.stack(
        [
            pick(own_sums[0], zero) + jnp.sum(normed_two, axis=0) * weight,
            pick(own_sums[1], zero) + product_sum,
            pick(zero, own_sums[0]) + jnp.sum(normed_one, axis=0) * weight,
            pick(zero, own_sums[1]) + product_sum,
        ]
    )
    sums, loss_total = lax.psum((sums, loss_sum[0]), "batch")
    sums = sums / clip_total
    grad_one = clip_total * (gnorm_one - sums[0] - normed_one * sums[1]) * scale_one
    grad_two = clip_total * (gnorm_two - sums[2] - normed_two * sums[3]) * scale_two
    return (grad_one, grad_two, loss_total[0] / features)


def solution(mesh):
    placed = (P("batch", "feat"), P("batch", "feat"))
    return jax.shard_map(
        body,
        mesh=mesh,
        in_specs=placed,
        out_specs=(P("batch", "feat"), P("batch", "feat"), P()),
        check_vma=False,
    )
```

```python
import jax
import jax.numpy as jnp
from jax import lax
from jax.experimental import pallas as pl
from jax.experimental.pallas import tpu as pltpu
from jax.sharding import PartitionSpec as P

epsilon = 1e-05
off_weight = 0.005
f32 = jnp.float32
bf16 = jnp.bfloat16

gray = (0, 1, 3, 2)
label_of = tuple(gray[i // 4] * 4 + gray[i % 4] for i in range(16))
feat_of = tuple(label_of.index(i) for i in range(16))
orders = ((3, 2, 1, 0), (2, 3, 0, 1), (1, 0, 3, 2), (0, 1, 2, 3))
masks = tuple(
    tuple(sum(((p >> (3 - j)) & 1) << order[j] for j in range(4)) for p in range(16))
    for order in orders
)

vmem = pl.BlockSpec(memory_space=pltpu.VMEM)
smem = pl.BlockSpec(memory_space=pltpu.SMEM)


def local_call(kernel, scalars, arrays, outs, scratch=(), flops=0):
    moved = sum(a.size * a.dtype.itemsize for a in (*arrays, *outs))
    call = pl.pallas_call(
        kernel,
        out_shape=list(outs),
        in_specs=[smem] * len(scalars) + [vmem] * len(arrays),
        out_specs=[vmem] * len(outs),
        scratch_shapes=list(scratch),
        compiler_params=pltpu.CompilerParams(vmem_limit_bytes=44 * 1024 * 1024),
        cost_estimate=pl.CostEstimate(flops=flops, bytes_accessed=moved, transcendentals=0),
    )
    return list(call(*scalars, *arrays))


def shape(rows, cols, dtype=f32):
    return jax.ShapeDtypeStruct((rows, cols), dtype)


def split(value):
    high = value.astype(bf16)
    return high, (value - high.astype(f32)).astype(bf16)


def dot3(left, right, left_dim, right_dim):
    def one(a, b):
        return lax.dot_general(
            a, b, (((left_dim,), (right_dim,)), ((), ())), preferred_element_type=f32
        )

    return one(left[0], right[0]) + (one(left[0], right[1]) + one(left[1], right[0]))


def normalize(first_ref, same, cross, center, scale, high, low):
    rows = same.shape[0]

    def put(source, at):
        high[at : at + rows, :], low[at : at + rows, :] = split(
            (source[...] - center[...]) * scale[...]
        )

    @pl.when(first_ref[0] == 1)
    def _():
        put(same, 0)
        put(cross, rows)

    @pl.when(first_ref[0] != 1)
    def _():
        put(cross, 0)
        put(same, rows)


def own_kernel(first, same, cross, center, scale, high, low, gram):
    normalize(first, same, cross, center, scale, high, low)
    quarter = gram.shape[1] // 4
    for q in range(4):
        part = slice(q * quarter, (q + 1) * quarter)
        gram[:, part] = dot3(
            (high[...], low[...]), (high[part, :], low[part, :]), 1, 1
        )


def far_kernel(first, same, cross, center, scale, high_0, low_0, high, low, gram):
    normalize(first, same, cross, center, scale, high, low)
    quarter = gram.shape[1] // 4
    for q in range(4):
        part = slice(q * quarter, (q + 1) * quarter)
        gram[:, part] = dot3((high_0[...], low_0[...]), (high[part, :], low[part, :]), 1, 1)


def cube_kernel(first, label, same, cross, center, scale, high_0, low_0, high, low, *rest):
    keeps, sends, whole = rest[:4], rest[4:8], rest[8]
    normalize(first, same, cross, center, scale, high, low)
    quarter = whole.shape[1]
    chunk = whole.shape[0] // 16
    for q in range(4):
        part = slice(q * quarter, (q + 1) * quarter)
        whole[...] = dot3((high_0[...], low_0[...]), (high[part, :], low[part, :]), 1, 1)
        for p in range(16):
            at = pl.multiple_of((label[0] ^ masks[q][p]) * chunk, chunk)
            target = keeps[q] if p < 8 else sends[q]
            target[p % 8 * chunk : (p % 8 + 1) * chunk, :] = whole[pl.ds(at, chunk), :]


def front_kernel(first, one, two, stats, same, cross):
    rows = one.shape[0]
    mean_one = jnp.sum(one[...], axis=0, keepdims=True) / rows
    mean_two = jnp.sum(two[...], axis=0, keepdims=True) / rows
    deviate_one = one[...] - mean_one
    deviate_two = two[...] - mean_two
    stats[...] = jnp.zeros(stats.shape, f32)
    stats[0:1, :] = mean_one
    stats[1:2, :] = mean_two
    stats[2:3, :] = jnp.sum(deviate_one * deviate_one, axis=0, keepdims=True)
    stats[3:4, :] = jnp.sum(deviate_two * deviate_two, axis=0, keepdims=True)
    stats[4:5, :] = jnp.sum(deviate_one * deviate_two, axis=0, keepdims=True)

    @pl.when(first[0] == 1)
    def _():
        same[...] = one[...]
        cross[...] = two[...]

    @pl.when(first[0] != 1)
    def _():
        same[...] = two[...]
        cross[...] = one[...]


def fold_kernel(*refs):
    half = refs[0].shape[0] // 2
    for q in range(4):
        keep, came, keep_out, send_out = refs[q::4]
        keep_out[...] = keep[:half, :] + came[:half, :]
        send_out[...] = keep[half:, :] + came[half:, :]


def last_fold_kernel(*refs):
    out = refs[8]
    cols = refs[0].shape[1]
    for q in range(4):
        out[:, q * cols : (q + 1) * cols] = refs[q][...] + refs[4 + q][...]


def match_kernel(mine, other, match):
    match[...] = jnp.full(match.shape, jnp.sum(mine[...] * other[...]), f32)


def part_kernel(other, *parts):
    cols = parts[0].shape[1]
    for q in range(4):
        parts[q][...] = other[:, q * cols : (q + 1) * cols]


def part_loss_kernel(loss, mine, other, *parts):
    rows, cols = other.shape[0], parts[0].shape[1]
    share = loss[0] + loss[1] * jnp.sum(mine[...] * other[...])
    for q in range(4):
        parts[q][:rows, :] = other[:, q * cols : (q + 1) * cols]
        parts[q][rows:, :] = jnp.full((8, cols), share, f32)


def join_kernel(*refs):
    rows = refs[0].shape[0]
    for q in range(4):
        own, came, out = refs[q::4]
        out[:rows, :] = own[...]
        out[rows:, :] = came[...]


def gather_rows(label, q, own, came, high, low, by_feat):
    chunk = high.shape[0] // 16
    step = own.shape[0] // 8
    for p in range(16):
        source = own if p < 8 else came
        owner = label[0] ^ masks[q][p]
        if by_feat:
            owner = owner ^ ((owner >> 1) & 5)
        at = pl.multiple_of(owner * chunk, chunk)
        high[pl.ds(at, chunk), :], low[pl.ds(at, chunk), :] = split(
            source[p % 8 * step : p % 8 * step + chunk, :]
        )


def turned_kernel(label, *refs):
    owns, cames = refs[:4], refs[4:8]
    high_0, low_0, turned, high, low = refs[8:]
    quarter = owns[0].shape[1]
    for q in range(4):
        part = slice(q * quarter, (q + 1) * quarter)
        gather_rows(label, q, owns[q], cames[q], high, low, False)
        turned[part, :] = dot3((high[...], low[...]), (high_0[...], low_0[...]), 0, 0)


def ahead_kernel(label, *refs):
    owns, cames = refs[:4], refs[4:8]
    high_1, low_1, ahead, high, low = refs[8:]
    quarter = owns[0].shape[1]
    for q in range(4):
        part = slice(q * quarter, (q + 1) * quarter)
        gather_rows(label, q, owns[q], cames[q], high, low, False)
        term = dot3((high[...], low[...]), (high_1[part, :], low_1[part, :]), 1, 0)
        ahead[...] = term if q == 0 else ahead[...] + term


def own_times_kernel(gram, high_0, low_0, one, ahead):
    quarter = gram.shape[1] // 4
    ahead[...] = one[...]
    for q in range(4):
        part = slice(q * quarter, (q + 1) * quarter)
        ahead[...] += dot3(split(gram[:, part]), (high_0[part, :], low_0[part, :]), 1, 0)


def last_kernel(factor, core, label, *refs):
    owns, cames = refs[:4], refs[4:8]
    high_2, low_2, high_0, low_0, one, two, kept, sent, sums, total, high, low = refs[8:]
    rows = kept.shape[0]
    quarter = owns[0].shape[1]
    total[...] = one[...] + two[...]
    for q in range(4):
        part = slice(q * quarter, (q + 1) * quarter)
        gather_rows(label, q, owns[q], cames[q], high, low, True)
        total[...] += dot3((high[...], low[...]), (high_2[part, :], low_2[part, :]), 1, 0)
    scaled = total[...] * factor[0]
    total[...] = scaled
    normed = high_0[...].astype(f32) + low_0[...].astype(f32)
    sums[...] = jnp.zeros(sums.shape, f32)
    sums[0:1, :] = jnp.sum(scaled, axis=0, keepdims=True)
    sums[1:2, :] = jnp.sum(scaled * normed, axis=0, keepdims=True)
    chunk = high.shape[0] // 16
    step = owns[0].shape[0] // 8
    loss = jnp.zeros((8, quarter), f32)
    for p in range(8):
        at = slice(p * step + chunk, (p + 1) * step)
        loss += owns[0][at, :] + cames[0][at, :]
    sums[2:3, :quarter] = loss[0:1, :]
    kept[...] = total[pl.ds(pl.multiple_of(core[0] * rows, rows), rows), :]
    sent[...] = total[pl.ds(pl.multiple_of((1 - core[0]) * rows, rows), rows), :]


def across(array, bit):
    return lax.ppermute(
        array, "feat", [(i, feat_of[label_of[i] ^ (1 << bit)]) for i in range(16)]
    )


def step_across(arrays, step):
    return [across(array, order[step]) for array, order in zip(arrays, orders)]


def fold(keeps, sends, step):
    cames = step_across(sends, step)
    rows, cols = keeps[0].shape
    if step == 3:
        return local_call(last_fold_kernel, (), (*keeps, *cames), [shape(rows, 4 * cols)])[0]
    outs = local_call(fold_kernel, (), (*keeps, *cames), [shape(rows // 2, cols)] * 8)
    return outs[:4], outs[4:]


def body(view_one, view_two):
    rows, cols = view_one.shape
    batch = lax.axis_size("batch")
    feats = lax.axis_size("feat")
    clip_total = rows * batch
    features = cols * feats
    core = lax.axis_index("batch") % 2
    on_first = core == 0
    first = (1 - core).astype(jnp.int32).reshape((1,))
    label = jnp.array(label_of, jnp.int32)[lax.axis_index("feat")].reshape((1,))
    swap = [(i, i ^ 1) for i in range(batch)]
    down = [(i, (i - 2) % batch) for i in range(batch)]
    up = [(i, (i + 2) % batch) for i in range(batch)]
    down_cross = [(i, (i ^ 1) - 2 if i > 1 else (i ^ 1) - 2 + batch) for i in range(batch)]
    up_cross = [(i, ((i ^ 1) + 2) % batch) for i in range(batch)]

    def pick(one, two):
        return jnp.where(on_first, one, two)

    mine, same_0, mine_cross = local_call(
        front_kernel,
        (first,),
        (view_one, view_two),
        [shape(8, cols), shape(rows, cols), shape(rows, cols)],
    )
    parts = lax.all_gather(mine, "batch", axis=0)
    parts, far_same, far_cross = lax.optimization_barrier((parts, same_0, mine_cross))
    cross_0 = lax.ppermute(far_cross, "batch", swap)
    center_one = jnp.mean(parts[:, 0], axis=0)
    center_two = jnp.mean(parts[:, 1], axis=0)
    shift_one = parts[:, 0] - center_one
    shift_two = parts[:, 1] - center_two
    spread_one = jnp.sum(parts[:, 2] + rows * shift_one * shift_one, axis=0) / clip_total
    spread_two = jnp.sum(parts[:, 3] + rows * shift_two * shift_two, axis=0) / clip_total
    scale_one = 1.0 / jnp.sqrt(spread_one + epsilon)
    scale_two = 1.0 / jnp.sqrt(spread_two + epsilon)
    covary = jnp.sum(parts[:, 4] + rows * shift_one * shift_two, axis=0) / clip_total
    diagonal = covary * scale_one * scale_two
    center = pick(center_one, center_two).reshape((1, cols))
    scale = pick(scale_one, scale_two).reshape((1, cols))

    same_1 = lax.ppermute(far_same, "batch", down)
    cross_1 = lax.ppermute(far_cross, "batch", down_cross)
    cross_up = lax.ppermute(far_cross, "batch", up_cross)
    block = 2 * rows
    quarter = block // 4
    product = 3 * 2 * block * block * cols
    halves = [shape(block, cols, bf16)] * 2
    row_scratch = [pltpu.VMEM((block, quarter), bf16)] * 2

    high_0, low_0, gram = local_call(
        own_kernel,
        (first,),
        (same_0, cross_0, center, scale),
        halves + [shape(block, block)],
        flops=product,
    )
    piece_0 = lax.psum_scatter(gram, "feat", scatter_dimension=0, tiled=True)
    same_1, cross_1, cross_up, high_0, low_0 = lax.optimization_barrier(
        (same_1, cross_1, cross_up, high_0, low_0)
    )

    def cube_gram(same, cross):
        outs = local_call(
            cube_kernel,
            (first, label),
            (same, cross, center, scale, high_0, low_0),
            halves + [shape(block // 2, quarter)] * 8,
            scratch=[pltpu.VMEM((block, quarter), f32)],
            flops=product,
        )
        return outs[:2], outs[2:6], outs[6:]

    def other_core(piece):
        return lax.ppermute(piece, "batch", swap)

    def match(piece, other):
        return local_call(match_kernel, (), (piece, other), [shape(8, 128)])[0][0, 0]

    def cube_gather(owns, also=None):
        for step in (3, 2, 1):
            cames = step_across(owns, step)
            owns = local_call(
                join_kernel, (), (*owns, *cames), [shape(2 * owns[0].shape[0], quarter)] * 4
            )
        if also is not None:
            owns[0], also = lax.optimization_barrier((owns[0], also))
        return owns + step_across(owns, 0), also

    halves_1, keeps_1, sends_1 = cube_gram(same_1, cross_1)
    same_2 = lax.ppermute(same_1, "batch", down)
    cross_2 = lax.ppermute(cross_up, "batch", up)
    keeps_1, sends_1 = fold(keeps_1, sends_1, 0)
    same_2, cross_2, keeps_1[0] = lax.optimization_barrier((same_2, cross_2, keeps_1[0]))
    high_2, low_2, gram = local_call(
        far_kernel,
        (first,),
        (same_2, cross_2, center, scale, high_0, low_0),
        halves + [shape(block, block)],
        flops=product,
    )
    keeps_1, sends_1 = fold(keeps_1, sends_1, 1)
    sends_1[0], gram = lax.optimization_barrier((sends_1[0], gram))
    piece_2 = lax.psum_scatter(gram, "feat", scatter_dimension=0, tiled=True)
    keeps_1, sends_1 = fold(keeps_1, sends_1, 2)
    piece_1 = fold(keeps_1, sends_1, 3)
    other_1 = other_core(piece_1)
    piece_0, other_1 = lax.optimization_barrier((piece_0, other_1))
    other_0 = other_core(piece_0)
    gram_0 = lax.all_gather(other_0, "feat", axis=0, tiled=True)
    owns_1 = local_call(
        part_kernel, (), (other_1,), [shape(block // 16, quarter)] * 4
    )
    gathered_1, _ = cube_gather(owns_1)
    square = match(piece_0, other_0) + 2.0 * match(piece_1, other_1)
    (turned,) = local_call(
        turned_kernel,
        (label,),
        (*gathered_1, high_0, low_0),
        [shape(block, cols)],
        scratch=row_scratch,
        flops=product,
    )
    above = lax.ppermute(turned, "batch", up)
    (ahead_1,) = local_call(
        ahead_kernel,
        (label,),
        (*gathered_1, *halves_1),
        [shape(block, cols)],
        scratch=row_scratch,
        flops=product,
    )

    square_weight = off_weight * 0.5 / (float(clip_total) * float(clip_total))
    share = square_weight * square + (
        jnp.sum((1.0 - diagonal) ** 2) - off_weight * jnp.sum(diagonal * diagonal)
    ) / batch
    share = jnp.stack([share, jnp.full((), square_weight, f32)])
    piece_2, turned, share = lax.optimization_barrier((piece_2, turned, share))
    other_2 = other_core(piece_2)
    owns_2 = local_call(
        part_loss_kernel,
        (share,),
        (piece_2, other_2),
        [shape(block // 16 + 8, quarter)] * 4,
    )
    gathered_2, gram_0 = cube_gather(owns_2, gram_0)
    (rest,) = local_call(
        own_times_kernel,
        (),
        (gram_0, high_0, low_0, ahead_1),
        [shape(block, cols)],
        flops=product,
    )
    factor = 2.0 * off_weight / (float(clip_total) * float(clip_total))
    kept, sent, own_sums = local_call(
        last_kernel,
        (jnp.full((1,), factor, f32), core.astype(jnp.int32).reshape((1,)), label),
        (*gathered_2, high_2, low_2, high_0, low_0, rest, above),
        [shape(rows, cols)] * 2 + [shape(8, cols)],
        scratch=[pltpu.VMEM((block, cols), f32)] + row_scratch,
        flops=product,
    )

    came = lax.ppermute(sent, "batch", swap)
    normed_one = (view_one - center_one) * scale_one
    normed_two = (view_two - center_two) * scale_two
    weight = (-2.0 * (1.0 - diagonal) - 2.0 * off_weight * diagonal) / clip_total
    gnorm_one = pick(kept, came) + normed_two * weight
    gnorm_two = pick(came, kept) + normed_one * weight
    zero = jnp.zeros((cols,), f32)
    product_sum = jnp.sum(normed_one * normed_two, axis=0) * weight
    sums = jnp.stack(
        [
            pick(own_sums[0], zero) + jnp.sum(normed_two, axis=0) * weight,
            pick(own_sums[1], zero) + product_sum,
            pick(zero, own_sums[0]) + jnp.sum(normed_one, axis=0) * weight,
            pick(zero, own_sums[1]) + product_sum,
        ]
    )
    sums, loss_total = lax.psum((sums, own_sums[2, :128]), "batch")
    sums = sums / clip_total
    grad_one = clip_total * (gnorm_one - sums[0] - normed_one * sums[1]) * scale_one
    grad_two = clip_total * (gnorm_two - sums[2] - normed_two * sums[3]) * scale_two
    return (grad_one, grad_two, loss_total[0] / features)


def solution(mesh):
    placed = (P("batch", "feat"), P("batch", "feat"))
    return jax.shard_map(
        body,
        mesh=mesh,
        in_specs=placed,
        out_specs=(P("batch", "feat"), P("batch", "feat"), P()),
        check_vma=False,
    )
```

```python
import jax
import jax.numpy as jnp
from jax import lax
from jax.experimental import pallas as pl
from jax.experimental.pallas import tpu as pltpu
from jax.sharding import PartitionSpec as P

epsilon = 1e-05
off_weight = 0.005
f32 = jnp.float32
bf16 = jnp.bfloat16

gray = (0, 1, 3, 2)
label_of = tuple(gray[i // 4] * 4 + gray[i % 4] for i in range(16))
feat_of = tuple(label_of.index(i) for i in range(16))
orders = ((3, 2, 1, 0), (2, 3, 0, 1), (1, 0, 3, 2), (0, 1, 2, 3))
masks = tuple(
    tuple(sum(((p >> (3 - j)) & 1) << order[j] for j in range(4)) for p in range(16))
    for order in orders
)

vmem = pl.BlockSpec(memory_space=pltpu.VMEM)
smem = pl.BlockSpec(memory_space=pltpu.SMEM)


def local_call(kernel, scalars, arrays, outs, scratch=(), flops=0):
    moved = sum(a.size * a.dtype.itemsize for a in (*arrays, *outs))
    call = pl.pallas_call(
        kernel,
        out_shape=list(outs),
        in_specs=[smem] * len(scalars) + [vmem] * len(arrays),
        out_specs=[vmem] * len(outs),
        scratch_shapes=list(scratch),
        compiler_params=pltpu.CompilerParams(vmem_limit_bytes=44 * 1024 * 1024),
        cost_estimate=pl.CostEstimate(flops=flops, bytes_accessed=moved, transcendentals=0),
    )
    return list(call(*scalars, *arrays))


def shape(rows, cols, dtype=f32):
    return jax.ShapeDtypeStruct((rows, cols), dtype)


def split(value):
    high = value.astype(bf16)
    return high, (value - high.astype(f32)).astype(bf16)


def dot3(left, right, left_dim, right_dim):
    def one(a, b):
        return lax.dot_general(
            a, b, (((left_dim,), (right_dim,)), ((), ())), preferred_element_type=f32
        )

    return one(left[0], right[0]) + (one(left[0], right[1]) + one(left[1], right[0]))


def normalize(first_ref, same, cross, center, scale, high, low):
    rows = same.shape[0]

    def put(source, at):
        high[at : at + rows, :], low[at : at + rows, :] = split(
            (source[...] - center[...]) * scale[...]
        )

    @pl.when(first_ref[0] == 1)
    def _():
        put(same, 0)
        put(cross, rows)

    @pl.when(first_ref[0] != 1)
    def _():
        put(cross, 0)
        put(same, rows)


def own_kernel(first, same, cross, center, scale, high, low, gram):
    normalize(first, same, cross, center, scale, high, low)
    quarter = gram.shape[1] // 4
    for q in range(4):
        part = slice(q * quarter, (q + 1) * quarter)
        gram[:, part] = dot3(
            (high[...], low[...]), (high[part, :], low[part, :]), 1, 1
        )


def far_kernel(first, same, cross, center, scale, high_0, low_0, high, low, gram):
    normalize(first, same, cross, center, scale, high, low)
    quarter = gram.shape[1] // 4
    for q in range(4):
        part = slice(q * quarter, (q + 1) * quarter)
        gram[:, part] = dot3((high_0[...], low_0[...]), (high[part, :], low[part, :]), 1, 1)


def cube_kernel(first, label, same, cross, center, scale, high_0, low_0, high, low, *rest):
    keeps, sends, whole = rest[:4], rest[4:8], rest[8]
    normalize(first, same, cross, center, scale, high, low)
    quarter = whole.shape[1]
    chunk = whole.shape[0] // 16
    for q in range(4):
        part = slice(q * quarter, (q + 1) * quarter)
        whole[...] = dot3((high_0[...], low_0[...]), (high[part, :], low[part, :]), 1, 1)
        for p in range(16):
            at = pl.multiple_of((label[0] ^ masks[q][p]) * chunk, chunk)
            target = keeps[q] if p < 8 else sends[q]
            target[p % 8 * chunk : (p % 8 + 1) * chunk, :] = whole[pl.ds(at, chunk), :]


def front_kernel(first, one, two, stats, same, cross):
    rows = one.shape[0]
    mean_one = jnp.sum(one[...], axis=0, keepdims=True) / rows
    mean_two = jnp.sum(two[...], axis=0, keepdims=True) / rows
    deviate_one = one[...] - mean_one
    deviate_two = two[...] - mean_two
    stats[...] = jnp.zeros(stats.shape, f32)
    stats[0:1, :] = mean_one
    stats[1:2, :] = mean_two
    stats[2:3, :] = jnp.sum(deviate_one * deviate_one, axis=0, keepdims=True)
    stats[3:4, :] = jnp.sum(deviate_two * deviate_two, axis=0, keepdims=True)
    stats[4:5, :] = jnp.sum(deviate_one * deviate_two, axis=0, keepdims=True)

    @pl.when(first[0] == 1)
    def _():
        same[...] = one[...]
        cross[...] = two[...]

    @pl.when(first[0] != 1)
    def _():
        same[...] = two[...]
        cross[...] = one[...]


def fold_kernel(*refs):
    half = refs[0].shape[0] // 2
    for q in range(4):
        keep, came, keep_out, send_out = refs[q::4]
        keep_out[...] = keep[:half, :] + came[:half, :]
        send_out[...] = keep[half:, :] + came[half:, :]


def last_fold_kernel(*refs):
    out = refs[8]
    cols = refs[0].shape[1]
    for q in range(4):
        out[:, q * cols : (q + 1) * cols] = refs[q][...] + refs[4 + q][...]


def match_kernel(mine, other, match):
    match[...] = jnp.full(match.shape, jnp.sum(mine[...] * other[...]), f32)


def part_kernel(other, *parts):
    cols = parts[0].shape[1]
    for q in range(4):
        parts[q][...] = other[:, q * cols : (q + 1) * cols]


def part_loss_kernel(loss, mine, other, *parts):
    rows, cols = other.shape[0], parts[0].shape[1]
    share = loss[0] + loss[1] * jnp.sum(mine[...] * other[...])
    for q in range(4):
        parts[q][:rows, :] = other[:, q * cols : (q + 1) * cols]
        parts[q][rows:, :] = jnp.full((8, cols), share, f32)


def join_kernel(*refs):
    rows = refs[0].shape[0]
    for q in range(4):
        own, came, out = refs[q::4]
        out[:rows, :] = own[...]
        out[rows:, :] = came[...]


def gather_rows(label, q, own, came, high, low, by_feat):
    chunk = high.shape[0] // 16
    step = own.shape[0] // 8
    for p in range(16):
        source = own if p < 8 else came
        owner = label[0] ^ masks[q][p]
        if by_feat:
            owner = owner ^ ((owner >> 1) & 5)
        at = pl.multiple_of(owner * chunk, chunk)
        high[pl.ds(at, chunk), :], low[pl.ds(at, chunk), :] = split(
            source[p % 8 * step : p % 8 * step + chunk, :]
        )


def turned_kernel(label, *refs):
    owns, cames = refs[:4], refs[4:8]
    high_0, low_0, turned, high, low = refs[8:]
    quarter = owns[0].shape[1]
    for q in range(4):
        part = slice(q * quarter, (q + 1) * quarter)
        gather_rows(label, q, owns[q], cames[q], high, low, False)
        turned[part, :] = dot3((high[...], low[...]), (high_0[...], low_0[...]), 0, 0)


def ahead_kernel(label, *refs):
    owns, cames = refs[:4], refs[4:8]
    high_1, low_1, ahead, high, low = refs[8:]
    quarter = owns[0].shape[1]
    for q in range(4):
        part = slice(q * quarter, (q + 1) * quarter)
        gather_rows(label, q, owns[q], cames[q], high, low, False)
        term = dot3((high[...], low[...]), (high_1[part, :], low_1[part, :]), 1, 0)
        ahead[...] = term if q == 0 else ahead[...] + term


def one_kernel(label, *refs):
    owns, cames = refs[:4], refs[4:8]
    high_2, low_2, one, two, ahead, loss, high, low = refs[8:]
    quarter = owns[0].shape[1]
    ahead[...] = one[...] + two[...]
    for q in range(4):
        part = slice(q * quarter, (q + 1) * quarter)
        gather_rows(label, q, owns[q], cames[q], high, low, True)
        ahead[...] += dot3((high[...], low[...]), (high_2[part, :], low_2[part, :]), 1, 0)
    chunk = high.shape[0] // 16
    step = owns[0].shape[0] // 8
    total = jnp.zeros((8, 128), f32)
    for p in range(8):
        at = slice(p * step + chunk, (p + 1) * step)
        total += owns[0][at, :128] + cames[0][at, :128]
    loss[...] = total


def last_kernel(factor, core, gram, high_0, low_0, rest, kept, sent, sums, total):
    rows = kept.shape[0]
    quarter = gram.shape[1]
    q = pl.program_id(0)

    @pl.when(q == 0)
    def _():
        total[...] = rest[...]

    part = pl.ds(pl.multiple_of(q * quarter, quarter), quarter)
    total[...] += dot3(split(gram[...]), (high_0[part, :], low_0[part, :]), 1, 0)

    @pl.when(q == 3)
    def _():
        scaled = total[...] * factor[0]
        total[...] = scaled
        normed = high_0[...].astype(f32) + low_0[...].astype(f32)
        sums[...] = jnp.zeros(sums.shape, f32)
        sums[0:1, :] = jnp.sum(scaled, axis=0, keepdims=True)
        sums[1:2, :] = jnp.sum(scaled * normed, axis=0, keepdims=True)
        kept[...] = total[pl.ds(pl.multiple_of(core[0] * rows, rows), rows), :]
        sent[...] = total[pl.ds(pl.multiple_of((1 - core[0]) * rows, rows), rows), :]


def across(array, bit):
    return lax.ppermute(
        array, "feat", [(i, feat_of[label_of[i] ^ (1 << bit)]) for i in range(16)]
    )


def step_across(arrays, step):
    return [across(array, order[step]) for array, order in zip(arrays, orders)]


def fold(keeps, sends, step):
    cames = step_across(sends, step)
    rows, cols = keeps[0].shape
    if step == 3:
        return local_call(last_fold_kernel, (), (*keeps, *cames), [shape(rows, 4 * cols)])[0]
    outs = local_call(fold_kernel, (), (*keeps, *cames), [shape(rows // 2, cols)] * 8)
    return outs[:4], outs[4:]


def body(view_one, view_two):
    rows, cols = view_one.shape
    batch = lax.axis_size("batch")
    feats = lax.axis_size("feat")
    clip_total = rows * batch
    features = cols * feats
    core = lax.axis_index("batch") % 2
    on_first = core == 0
    first = (1 - core).astype(jnp.int32).reshape((1,))
    label = jnp.array(label_of, jnp.int32)[lax.axis_index("feat")].reshape((1,))
    swap = [(i, i ^ 1) for i in range(batch)]
    down = [(i, (i - 2) % batch) for i in range(batch)]
    up = [(i, (i + 2) % batch) for i in range(batch)]
    down_cross = [(i, (i ^ 1) - 2 if i > 1 else (i ^ 1) - 2 + batch) for i in range(batch)]
    up_cross = [(i, ((i ^ 1) + 2) % batch) for i in range(batch)]

    def pick(one, two):
        return jnp.where(on_first, one, two)

    mine, same_0, mine_cross = local_call(
        front_kernel,
        (first,),
        (view_one, view_two),
        [shape(8, cols), shape(rows, cols), shape(rows, cols)],
    )
    same_1 = lax.ppermute(same_0, "batch", down)
    cross_1 = lax.ppermute(mine_cross, "batch", down_cross)
    mate = lax.ppermute(mine, "batch", swap)
    pairs = [jnp.stack([pick(mine, mate), pick(mate, mine)])]
    for _ in range(batch // 2 - 1):
        pairs.append(lax.ppermute(pairs[-1], "batch", up))
    parts = jnp.concatenate(pairs, axis=0)
    parts, far_cross = lax.optimization_barrier((parts, mine_cross))
    cross_0 = lax.ppermute(mine_cross, "batch", swap)
    cross_0, same_1 = lax.optimization_barrier((cross_0, same_1))
    center_one = jnp.mean(parts[:, 0], axis=0)
    center_two = jnp.mean(parts[:, 1], axis=0)
    shift_one = parts[:, 0] - center_one
    shift_two = parts[:, 1] - center_two
    spread_one = jnp.sum(parts[:, 2] + rows * shift_one * shift_one, axis=0) / clip_total
    spread_two = jnp.sum(parts[:, 3] + rows * shift_two * shift_two, axis=0) / clip_total
    scale_one = 1.0 / jnp.sqrt(spread_one + epsilon)
    scale_two = 1.0 / jnp.sqrt(spread_two + epsilon)
    covary = jnp.sum(parts[:, 4] + rows * shift_one * shift_two, axis=0) / clip_total
    diagonal = covary * scale_one * scale_two
    center = pick(center_one, center_two).reshape((1, cols))
    scale = pick(scale_one, scale_two).reshape((1, cols))

    cross_up = lax.ppermute(far_cross, "batch", up_cross)
    block = 2 * rows
    quarter = block // 4
    product = 3 * 2 * block * block * cols
    halves = [shape(block, cols, bf16)] * 2
    row_scratch = [pltpu.VMEM((block, quarter), bf16)] * 2

    high_0, low_0, gram = local_call(
        own_kernel,
        (first,),
        (same_0, cross_0, center, scale),
        halves + [shape(block, block)],
        flops=product,
    )
    piece_0 = lax.psum_scatter(gram, "feat", scatter_dimension=0, tiled=True)
    same_1, cross_1, cross_up, high_0, low_0 = lax.optimization_barrier(
        (same_1, cross_1, cross_up, high_0, low_0)
    )

    def cube_gram(same, cross):
        outs = local_call(
            cube_kernel,
            (first, label),
            (same, cross, center, scale, high_0, low_0),
            halves + [shape(block // 2, quarter)] * 8,
            scratch=[pltpu.VMEM((block, quarter), f32)],
            flops=product,
        )
        return outs[:2], outs[2:6], outs[6:]

    def other_core(piece):
        return lax.ppermute(piece, "batch", swap)

    def match(piece, other):
        return local_call(match_kernel, (), (piece, other), [shape(8, 128)])[0][0, 0]

    def cube_gather(owns):
        for step in (3, 2, 1):
            cames = step_across(owns, step)
            owns = local_call(
                join_kernel, (), (*owns, *cames), [shape(2 * owns[0].shape[0], quarter)] * 4
            )
        return owns + step_across(owns, 0)

    halves_1, keeps_1, sends_1 = cube_gram(same_1, cross_1)
    same_2 = lax.ppermute(same_1, "batch", down)
    cross_2 = lax.ppermute(cross_up, "batch", up)
    keeps_1, sends_1 = fold(keeps_1, sends_1, 0)
    same_2, cross_2, keeps_1[0] = lax.optimization_barrier((same_2, cross_2, keeps_1[0]))
    high_2, low_2, gram = local_call(
        far_kernel,
        (first,),
        (same_2, cross_2, center, scale, high_0, low_0),
        halves + [shape(block, block)],
        flops=product,
    )
    *sends_1, gram = lax.optimization_barrier((*sends_1, gram))
    keeps_1, sends_1 = fold(keeps_1, sends_1, 1)
    piece_2 = lax.psum_scatter(gram, "feat", scatter_dimension=0, tiled=True)
    keeps_1, sends_1 = fold(keeps_1, sends_1, 2)
    piece_1 = fold(keeps_1, sends_1, 3)
    other_1 = other_core(piece_1)
    piece_0, other_1 = lax.optimization_barrier((piece_0, other_1))
    other_0 = other_core(piece_0)
    gram_0 = lax.all_gather(other_0, "feat", axis=0, tiled=True)
    owns_1 = local_call(
        part_kernel, (), (other_1,), [shape(block // 16, quarter)] * 4
    )
    gathered_1 = cube_gather(owns_1)
    square = match(piece_0, other_0) + 2.0 * match(piece_1, other_1)
    (turned,) = local_call(
        turned_kernel,
        (label,),
        (*gathered_1, high_0, low_0),
        [shape(block, cols)],
        scratch=row_scratch,
        flops=product,
    )
    above = lax.ppermute(turned, "batch", up)
    (ahead_1,) = local_call(
        ahead_kernel,
        (label,),
        (*gathered_1, *halves_1),
        [shape(block, cols)],
        scratch=row_scratch,
        flops=product,
    )

    square_weight = off_weight * 0.5 / (float(clip_total) * float(clip_total))
    share = square_weight * square + (
        jnp.sum((1.0 - diagonal) ** 2) - off_weight * jnp.sum(diagonal * diagonal)
    ) / batch
    share = jnp.stack([share, jnp.full((), square_weight, f32)])
    piece_2, turned, share = lax.optimization_barrier((piece_2, turned, share))
    other_2 = other_core(piece_2)
    owns_2 = local_call(
        part_loss_kernel,
        (share,),
        (piece_2, other_2),
        [shape(block // 16 + 8, quarter)] * 4,
    )
    gathered_2 = cube_gather(owns_2)
    rest, loss_sum = local_call(
        one_kernel,
        (label,),
        (*gathered_2, high_2, low_2, ahead_1, above),
        [shape(block, cols), shape(8, 128)],
        scratch=row_scratch,
        flops=product,
    )
    gram_0, rest = lax.optimization_barrier((gram_0, rest))
    factor = 2.0 * off_weight / (float(clip_total) * float(clip_total))

    def whole(rows, cols):
        return pl.BlockSpec((rows, cols), lambda q: (0, 0))

    kept, sent, own_sums = pl.pallas_call(
        last_kernel,
        out_shape=[shape(rows, cols), shape(rows, cols), shape(8, cols)],
        grid=(4,),
        in_specs=[
            smem,
            smem,
            pl.BlockSpec((block, quarter), lambda q: (0, q)),
            whole(block, cols),
            whole(block, cols),
            whole(block, cols),
        ],
        out_specs=[whole(rows, cols), whole(rows, cols), whole(8, cols)],
        scratch_shapes=[pltpu.VMEM((block, cols), f32)],
        compiler_params=pltpu.CompilerParams(vmem_limit_bytes=44 * 1024 * 1024),
        cost_estimate=pl.CostEstimate(
            flops=product, bytes_accessed=12 * 1024 * 1024, transcendentals=0
        ),
    )(
        jnp.full((1,), factor, f32),
        core.astype(jnp.int32).reshape((1,)),
        gram_0,
        high_0,
        low_0,
        rest,
    )

    came = lax.ppermute(sent, "batch", swap)
    normed_one = (view_one - center_one) * scale_one
    normed_two = (view_two - center_two) * scale_two
    weight = (-2.0 * (1.0 - diagonal) - 2.0 * off_weight * diagonal) / clip_total
    gnorm_one = pick(kept, came) + normed_two * weight
    gnorm_two = pick(came, kept) + normed_one * weight
    zero = jnp.zeros((cols,), f32)
    product_sum = jnp.sum(normed_one * normed_two, axis=0) * weight
    sums = jnp.stack(
        [
            pick(own_sums[0], zero) + jnp.sum(normed_two, axis=0) * weight,
            pick(own_sums[1], zero) + product_sum,
            pick(zero, own_sums[0]) + jnp.sum(normed_one, axis=0) * weight,
            pick(zero, own_sums[1]) + product_sum,
        ]
    )
    sums, loss_total = lax.psum((sums, loss_sum[0]), "batch")
    sums = sums / clip_total
    grad_one = clip_total * (gnorm_one - sums[0] - normed_one * sums[1]) * scale_one
    grad_two = clip_total * (gnorm_two - sums[2] - normed_two * sums[3]) * scale_two
    return (grad_one, grad_two, loss_total[0] / features)


def solution(mesh):
    placed = (P("batch", "feat"), P("batch", "feat"))
    return jax.shard_map(
        body,
        mesh=mesh,
        in_specs=placed,
        out_specs=(P("batch", "feat"), P("batch", "feat"), P()),
        check_vma=False,
    )
```

```python
import jax
import jax.numpy as jnp
from jax import lax
from jax.experimental import pallas as pl
from jax.experimental.pallas import tpu as pltpu
from jax.sharding import PartitionSpec as P

epsilon = 1e-05
off_weight = 0.005
f32 = jnp.float32
bf16 = jnp.bfloat16

gray = (0, 1, 3, 2)
label_of = tuple(gray[i // 4] * 4 + gray[i % 4] for i in range(16))
feat_of = tuple(label_of.index(i) for i in range(16))
orders = ((3, 2, 1, 0), (2, 3, 0, 1), (1, 0, 3, 2), (0, 1, 2, 3))
masks = tuple(
    tuple(sum(((p >> (3 - j)) & 1) << order[j] for j in range(4)) for p in range(16))
    for order in orders
)

vmem = pl.BlockSpec(memory_space=pltpu.VMEM)
smem = pl.BlockSpec(memory_space=pltpu.SMEM)


def local_call(kernel, scalars, arrays, outs, scratch=(), flops=0):
    moved = sum(a.size * a.dtype.itemsize for a in (*arrays, *outs))
    call = pl.pallas_call(
        kernel,
        out_shape=list(outs),
        in_specs=[smem] * len(scalars) + [vmem] * len(arrays),
        out_specs=[vmem] * len(outs),
        scratch_shapes=list(scratch),
        compiler_params=pltpu.CompilerParams(vmem_limit_bytes=28 * 1024 * 1024),
        cost_estimate=pl.CostEstimate(flops=flops, bytes_accessed=moved, transcendentals=0),
    )
    return list(call(*scalars, *arrays))


def shape(rows, cols, dtype=f32):
    return jax.ShapeDtypeStruct((rows, cols), dtype)


def split(value):
    high = value.astype(bf16)
    return high, (value - high.astype(f32)).astype(bf16)


def dot3(left, right, left_dim, right_dim):
    def one(a, b):
        return lax.dot_general(
            a, b, (((left_dim,), (right_dim,)), ((), ())), preferred_element_type=f32
        )

    return one(left[0], right[0]) + (one(left[0], right[1]) + one(left[1], right[0]))


def normalize(first_ref, same, cross, center, scale, high, low):
    rows = cross[0].shape[0]

    def put(pieces, at):
        for source in pieces:
            part = slice(at, at + source.shape[0])
            high[part, :], low[part, :] = split((source[...] - center[...]) * scale[...])
            at += source.shape[0]

    @pl.when(first_ref[0] == 1)
    def _():
        put(same, 0)
        put(cross, rows)

    @pl.when(first_ref[0] != 1)
    def _():
        put(cross, 0)
        put(same, rows)


def own_kernel(first, same_a, same_b, cross, center, scale, high, low, gram):
    normalize(first, (same_a, same_b), (cross,), center, scale, high, low)
    quarter = gram.shape[1] // 4
    for q in range(4):
        part = slice(q * quarter, (q + 1) * quarter)
        gram[:, part] = dot3(
            (high[...], low[...]), (high[part, :], low[part, :]), 1, 1
        )


def far_kernel(first, same, cross, center, scale, high_0, low_0, high, low, gram):
    normalize(first, (same,), (cross,), center, scale, high, low)
    quarter = gram.shape[1] // 4
    for q in range(4):
        part = slice(q * quarter, (q + 1) * quarter)
        gram[:, part] = dot3((high_0[...], low_0[...]), (high[part, :], low[part, :]), 1, 1)


def cube_kernel(first, label, same_a, same_b, cross, center, scale, high_0, low_0, *rest):
    high, low, forward = rest[:3]
    keeps, sends, whole = rest[3:7], rest[7:11], rest[11]
    half = same_a.shape[0]
    forward[:half, :] = same_a[...]
    forward[half:, :] = same_b[...]
    normalize(first, (same_a, same_b), (cross,), center, scale, high, low)
    quarter = whole.shape[1]
    chunk = whole.shape[0] // 16
    for q in range(4):
        part = slice(q * quarter, (q + 1) * quarter)
        whole[...] = dot3((high_0[...], low_0[...]), (high[part, :], low[part, :]), 1, 1)
        for p in range(16):
            at = pl.multiple_of((label[0] ^ masks[q][p]) * chunk, chunk)
            target = keeps[q] if p < 8 else sends[q]
            target[p % 8 * chunk : (p % 8 + 1) * chunk, :] = whole[pl.ds(at, chunk), :]


def front_kernel(first, one, two, stats, same_a, same_b, cross):
    rows = one.shape[0]
    half = rows // 2
    mean_one = jnp.sum(one[...], axis=0, keepdims=True) / rows
    mean_two = jnp.sum(two[...], axis=0, keepdims=True) / rows
    deviate_one = one[...] - mean_one
    deviate_two = two[...] - mean_two
    stats[...] = jnp.zeros(stats.shape, f32)
    stats[0:1, :] = mean_one
    stats[1:2, :] = mean_two
    stats[2:3, :] = jnp.sum(deviate_one * deviate_one, axis=0, keepdims=True)
    stats[3:4, :] = jnp.sum(deviate_two * deviate_two, axis=0, keepdims=True)
    stats[4:5, :] = jnp.sum(deviate_one * deviate_two, axis=0, keepdims=True)

    @pl.when(first[0] == 1)
    def _():
        same_a[...] = one[:half, :]
        same_b[...] = one[half:, :]
        cross[...] = two[...]

    @pl.when(first[0] != 1)
    def _():
        same_a[...] = two[:half, :]
        same_b[...] = two[half:, :]
        cross[...] = one[...]


def fold_kernel(*refs):
    half = refs[0].shape[0] // 2
    for q in range(4):
        keep, came, keep_out, send_out = refs[q::4]
        keep_out[...] = keep[:half, :] + came[:half, :]
        send_out[...] = keep[half:, :] + came[half:, :]


def last_fold_kernel(*refs):
    out = refs[8]
    cols = refs[0].shape[1]
    for q in range(4):
        out[:, q * cols : (q + 1) * cols] = refs[q][...] + refs[4 + q][...]


def part_kernel(mine, other, match, *parts):
    cols = parts[0].shape[1]
    for q in range(4):
        parts[q][...] = other[:, q * cols : (q + 1) * cols]
    match[...] = jnp.full(match.shape, jnp.sum(mine[...] * other[...]), f32)


def extend_kernel(share, match_1, match_0, mine, other, token, out):
    del token
    rows = other.shape[0]
    square = (
        2.0 * match_1[0:1, 0:1]
        + match_0[0:1, 0:1]
        + jnp.sum(mine[...] * other[...], keepdims=True)
    )
    out[:rows, :] = other[...]
    out[rows:, :] = jnp.broadcast_to(share[0] + share[1] * square, (8, out.shape[1]))


def join_kernel(*refs):
    rows = refs[0].shape[0]
    for q in range(4):
        own, came, out = refs[q::4]
        out[:rows, :] = own[...]
        out[rows:, :] = came[...]


def gather_rows(label, q, own, came, high, low, by_feat):
    chunk = high.shape[0] // 16
    for p in range(16):
        source = own if p < 8 else came
        owner = label[0] ^ masks[q][p]
        if by_feat:
            owner = owner ^ ((owner >> 1) & 5)
        at = pl.multiple_of(owner * chunk, chunk)
        high[pl.ds(at, chunk), :], low[pl.ds(at, chunk), :] = split(
            source[p % 8 * chunk : (p % 8 + 1) * chunk, :]
        )


def turned_kernel(label, *refs):
    owns, cames = refs[:4], refs[4:8]
    high_0, low_0, turned, high, low = refs[8:]
    quarter = high.shape[1]
    for q in range(4):
        part = slice(q * quarter, (q + 1) * quarter)
        gather_rows(label, q, owns[q], cames[q], high, low, False)
        turned[part, :] = dot3((high[...], low[...]), (high_0[...], low_0[...]), 0, 0)


def ahead_kernel(label, *refs):
    owns, cames = refs[:4], refs[4:8]
    high_1, low_1, ahead, high, low = refs[8:]
    quarter = high.shape[1]
    for q in range(4):
        part = slice(q * quarter, (q + 1) * quarter)
        gather_rows(label, q, owns[q], cames[q], high, low, False)
        term = dot3((high[...], low[...]), (high_1[part, :], low_1[part, :]), 1, 0)
        ahead[...] = term if q == 0 else ahead[...] + term


def own_times_kernel(label, *refs):
    owns, cames = refs[:4], refs[4:8]
    high_0, low_0, one, ahead, high, low = refs[8:]
    quarter = high.shape[1]
    ahead[...] = one[...]
    for q in range(4):
        part = slice(q * quarter, (q + 1) * quarter)
        gather_rows(label, q, owns[q], cames[q], high, low, True)
        ahead[...] += dot3((high[...], low[...]), (high_0[part, :], low_0[part, :]), 1, 0)


def last_kernel(
    factor, core, gram, high_2, low_2, high_0, low_0, one, two, kept, sent, sums, total, high, low
):
    rows = kept.shape[0]
    quarter = gram.shape[1]
    chunk = high.shape[0] // 16
    step = gram.shape[0] // 16
    q = pl.program_id(0)

    @pl.when(q == 0)
    def _():
        total[...] = one[...] + two[...]
        sums[...] = jnp.zeros(sums.shape, f32)

    loss = jnp.zeros((1, quarter), f32)
    for i in range(16):
        at = i * step
        high[i * chunk : (i + 1) * chunk, :], low[i * chunk : (i + 1) * chunk, :] = split(
            gram[at : at + chunk, :]
        )
        loss += gram[at + chunk : at + chunk + 1, :]
    part = pl.ds(pl.multiple_of(q * quarter, quarter), quarter)
    total[...] += dot3((high[...], low[...]), (high_2[part, :], low_2[part, :]), 1, 0)

    @pl.when(q == 3)
    def _():
        scaled = total[...] * factor[0]
        total[...] = scaled
        normed = high_0[...].astype(f32) + low_0[...].astype(f32)
        sums[0:1, :] = jnp.sum(scaled, axis=0, keepdims=True)
        sums[1:2, :] = jnp.sum(scaled * normed, axis=0, keepdims=True)
        sums[2:3, :quarter] = loss
        kept[...] = total[pl.ds(pl.multiple_of(core[0] * rows, rows), rows), :]
        sent[...] = total[pl.ds(pl.multiple_of((1 - core[0]) * rows, rows), rows), :]


def across(array, bit):
    return lax.ppermute(
        array, "feat", [(i, feat_of[label_of[i] ^ (1 << bit)]) for i in range(16)]
    )


def step_across(arrays, step):
    return [across(array, order[step]) for array, order in zip(arrays, orders)]


def fold(keeps, sends, step):
    cames = step_across(sends, step)
    rows, cols = keeps[0].shape
    if step == 3:
        return local_call(last_fold_kernel, (), (*keeps, *cames), [shape(rows, 4 * cols)])[0]
    outs = local_call(fold_kernel, (), (*keeps, *cames), [shape(rows // 2, cols)] * 8)
    return outs[:4], outs[4:]


def body(view_one, view_two):
    rows, cols = view_one.shape
    batch = lax.axis_size("batch")
    feats = lax.axis_size("feat")
    clip_total = rows * batch
    features = cols * feats
    core = lax.axis_index("batch") % 2
    on_first = core == 0
    first = (1 - core).astype(jnp.int32).reshape((1,))
    label = jnp.array(label_of, jnp.int32)[lax.axis_index("feat")].reshape((1,))
    swap = [(i, i ^ 1) for i in range(batch)]
    down = [(i, (i - 2) % batch) for i in range(batch)]
    up = [(i, (i + 2) % batch) for i in range(batch)]
    down_cross = [(i, (i ^ 1) - 2 if i > 1 else (i ^ 1) - 2 + batch) for i in range(batch)]
    up_cross = [(i, ((i ^ 1) + 2) % batch) for i in range(batch)]

    def pick(one, two):
        return jnp.where(on_first, one, two)

    mine, same_a0, same_b0, mine_cross = local_call(
        front_kernel,
        (first,),
        (view_one, view_two),
        [shape(8, cols), shape(rows // 2, cols), shape(rows // 2, cols), shape(rows, cols)],
    )
    same_a1 = lax.ppermute(same_a0, "batch", down)
    same_b1 = lax.ppermute(same_b0, "batch", down)
    cross_1 = lax.ppermute(mine_cross, "batch", down_cross)
    mate = lax.ppermute(mine, "batch", swap)
    pairs = [jnp.stack([pick(mine, mate), pick(mate, mine)])]
    for _ in range(batch // 2 - 1):
        pairs.append(lax.ppermute(pairs[-1], "batch", up))
    parts = jnp.concatenate(pairs, axis=0)
    parts, far_cross = lax.optimization_barrier((parts, mine_cross))
    cross_0 = lax.ppermute(mine_cross, "batch", swap)
    cross_0, same_a1 = lax.optimization_barrier((cross_0, same_a1))
    center_one = jnp.mean(parts[:, 0], axis=0)
    center_two = jnp.mean(parts[:, 1], axis=0)
    shift_one = parts[:, 0] - center_one
    shift_two = parts[:, 1] - center_two
    spread_one = jnp.sum(parts[:, 2] + rows * shift_one * shift_one, axis=0) / clip_total
    spread_two = jnp.sum(parts[:, 3] + rows * shift_two * shift_two, axis=0) / clip_total
    scale_one = 1.0 / jnp.sqrt(spread_one + epsilon)
    scale_two = 1.0 / jnp.sqrt(spread_two + epsilon)
    covary = jnp.sum(parts[:, 4] + rows * shift_one * shift_two, axis=0) / clip_total
    diagonal = covary * scale_one * scale_two
    center = pick(center_one, center_two).reshape((1, cols))
    scale = pick(scale_one, scale_two).reshape((1, cols))

    cross_up = lax.ppermute(far_cross, "batch", up_cross)
    block = 2 * rows
    quarter = block // 4
    product = 3 * 2 * block * block * cols
    halves = [shape(block, cols, bf16)] * 2
    row_scratch = [pltpu.VMEM((block, quarter), bf16)] * 2

    high_0, low_0, gram = local_call(
        own_kernel,
        (first,),
        (same_a0, same_b0, cross_0, center, scale),
        halves + [shape(block, block)],
        flops=product,
    )
    piece_0 = lax.psum_scatter(gram, "feat", scatter_dimension=0, tiled=True)
    same_a1, same_b1, cross_1, cross_up, high_0, low_0 = lax.optimization_barrier(
        (same_a1, same_b1, cross_1, cross_up, high_0, low_0)
    )

    high_1, low_1, forward, *outs = local_call(
        cube_kernel,
        (first, label),
        (same_a1, same_b1, cross_1, center, scale, high_0, low_0),
        halves + [shape(rows, cols)] + [shape(block // 2, quarter)] * 8,
        scratch=[pltpu.VMEM((block, quarter), f32)],
        flops=product,
    )
    keeps, sends = outs[:4], outs[4:]
    same_2 = lax.ppermute(forward, "batch", down)
    cross_2 = lax.ppermute(cross_up, "batch", up)
    keeps, sends = fold(keeps, sends, 0)

    same_2, cross_2, keeps[0] = lax.optimization_barrier((same_2, cross_2, keeps[0]))
    high_2, low_2, gram = local_call(
        far_kernel,
        (first,),
        (same_2, cross_2, center, scale, high_0, low_0),
        halves + [shape(block, block)],
        flops=product,
    )
    piece_2 = lax.psum_scatter(gram, "feat", scatter_dimension=0, tiled=True)
    *sends, gram = lax.optimization_barrier((*sends, gram))
    for step in (1, 2):
        keeps, sends = fold(keeps, sends, step)
    piece_1 = fold(keeps, sends, 3)

    def parts_of(piece, other):
        match, *owns = local_call(
            part_kernel,
            (),
            (piece, other),
            [shape(8, 128)] + [shape(block // 16, quarter)] * 4,
        )
        return match, owns

    def cube_gather(owns):
        for step in (3, 2, 1):
            cames = step_across(owns, step)
            owns = local_call(
                join_kernel, (), (*owns, *cames), [shape(2 * owns[0].shape[0], quarter)] * 4
            )
        return owns + step_across(owns, 0)

    other_1 = lax.ppermute(piece_1, "batch", swap)
    match_1, owns_1 = parts_of(piece_1, other_1)
    gathered_1 = cube_gather(owns_1)
    (turned,) = local_call(
        turned_kernel,
        (label,),
        (*gathered_1, high_0, low_0),
        [shape(block, cols)],
        scratch=row_scratch,
        flops=product,
    )
    above = lax.ppermute(turned, "batch", up)
    piece_0, piece_2, turned = lax.optimization_barrier((piece_0, piece_2, turned))
    other_2 = lax.ppermute(piece_2, "batch", swap)
    other_0 = lax.ppermute(piece_0, "batch", swap)
    match_0, owns_0 = parts_of(piece_0, other_0)
    square_weight = off_weight * 0.5 / (float(clip_total) * float(clip_total))
    share = (
        jnp.sum((1.0 - diagonal) ** 2) - off_weight * jnp.sum(diagonal * diagonal)
    ) / batch
    share = jnp.stack([share, jnp.full((), square_weight, f32)])
    (extended,) = local_call(
        extend_kernel,
        (share,),
        (match_1, match_0, piece_2, other_2, turned[:8, :128]),
        [shape(block // 16 + 8, block)],
    )
    owns_0[0], extended = lax.optimization_barrier((owns_0[0], extended))
    gram_2 = lax.all_gather(extended, "feat", axis=0, tiled=True)
    gathered_0 = cube_gather(owns_0)
    (ahead,) = local_call(
        ahead_kernel,
        (label,),
        (*gathered_1, high_1, low_1),
        [shape(block, cols)],
        scratch=row_scratch,
        flops=product,
    )
    (rest,) = local_call(
        own_times_kernel,
        (label,),
        (*gathered_0, high_0, low_0, ahead),
        [shape(block, cols)],
        scratch=row_scratch,
        flops=product,
    )
    gram_2, rest = lax.optimization_barrier((gram_2, rest))
    factor = 2.0 * off_weight / (float(clip_total) * float(clip_total))

    def whole(rows, cols):
        return pl.BlockSpec((rows, cols), lambda q: (0, 0))

    kept, sent, own_sums = pl.pallas_call(
        last_kernel,
        out_shape=[shape(rows, cols), shape(rows, cols), shape(8, cols)],
        grid=(4,),
        in_specs=[smem, smem, pl.BlockSpec((block + 128, quarter), lambda q: (0, q))]
        + [whole(block, cols)] * 6,
        out_specs=[whole(rows, cols), whole(rows, cols), whole(8, cols)],
        scratch_shapes=[pltpu.VMEM((block, cols), f32)] + row_scratch,
        compiler_params=pltpu.CompilerParams(vmem_limit_bytes=28 * 1024 * 1024),
        cost_estimate=pl.CostEstimate(
            flops=product, bytes_accessed=14 * 1024 * 1024, transcendentals=0
        ),
    )(
        jnp.full((1,), factor, f32),
        core.astype(jnp.int32).reshape((1,)),
        gram_2,
        high_2,
        low_2,
        high_0,
        low_0,
        rest,
        above,
    )

    came = lax.ppermute(sent, "batch", swap)
    normed_one = (view_one - center_one) * scale_one
    normed_two = (view_two - center_two) * scale_two
    weight = (-2.0 * (1.0 - diagonal) - 2.0 * off_weight * diagonal) / clip_total
    gnorm_one = pick(kept, came) + normed_two * weight
    gnorm_two = pick(came, kept) + normed_one * weight
    zero = jnp.zeros((cols,), f32)
    product_sum = jnp.sum(normed_one * normed_two, axis=0) * weight
    sums = jnp.stack(
        [
            pick(own_sums[0], zero) + jnp.sum(normed_two, axis=0) * weight,
            pick(own_sums[1], zero) + product_sum,
            pick(zero, own_sums[0]) + jnp.sum(normed_one, axis=0) * weight,
            pick(zero, own_sums[1]) + product_sum,
        ]
    )
    sums, loss_total = lax.psum((sums, own_sums[2, :128]), "batch")
    sums = sums / clip_total
    grad_one = clip_total * (gnorm_one - sums[0] - normed_one * sums[1]) * scale_one
    grad_two = clip_total * (gnorm_two - sums[2] - normed_two * sums[3]) * scale_two
    return (grad_one, grad_two, loss_total[0] / features)


def solution(mesh):
    placed = (P("batch", "feat"), P("batch", "feat"))
    return jax.shard_map(
        body,
        mesh=mesh,
        in_specs=placed,
        out_specs=(P("batch", "feat"), P("batch", "feat"), P()),
        check_vma=False,
    )
```

```python
import jax
import jax.numpy as jnp
from jax import lax
from jax.experimental import pallas as pl
from jax.experimental.pallas import tpu as pltpu
from jax.sharding import PartitionSpec as P

epsilon = 1e-05
off_weight = 0.005
f32 = jnp.float32
bf16 = jnp.bfloat16

gray = (0, 1, 3, 2)
label_of = tuple(gray[i // 4] * 4 + gray[i % 4] for i in range(16))
feat_of = tuple(label_of.index(i) for i in range(16))
orders = ((3, 2, 1, 0), (2, 3, 0, 1), (1, 0, 3, 2), (0, 1, 2, 3))
masks = tuple(
    tuple(sum(((p >> (3 - j)) & 1) << order[j] for j in range(4)) for p in range(16))
    for order in orders
)

vmem = pl.BlockSpec(memory_space=pltpu.VMEM)
smem = pl.BlockSpec(memory_space=pltpu.SMEM)


def local_call(kernel, scalars, arrays, outs, scratch=(), flops=0):
    moved = sum(a.size * a.dtype.itemsize for a in (*arrays, *outs))
    call = pl.pallas_call(
        kernel,
        out_shape=list(outs),
        in_specs=[smem] * len(scalars) + [vmem] * len(arrays),
        out_specs=[vmem] * len(outs),
        scratch_shapes=list(scratch),
        compiler_params=pltpu.CompilerParams(vmem_limit_bytes=28 * 1024 * 1024),
        cost_estimate=pl.CostEstimate(flops=flops, bytes_accessed=moved, transcendentals=0),
    )
    return list(call(*scalars, *arrays))


def shape(rows, cols, dtype=f32):
    return jax.ShapeDtypeStruct((rows, cols), dtype)


def split(value):
    high = value.astype(bf16)
    return high, (value - high.astype(f32)).astype(bf16)


def dot3(left, right, left_dim, right_dim):
    def one(a, b):
        return lax.dot_general(
            a, b, (((left_dim,), (right_dim,)), ((), ())), preferred_element_type=f32
        )

    return one(left[0], right[0]) + (one(left[0], right[1]) + one(left[1], right[0]))


def normalize(first_ref, same, cross, center, scale, high, low):
    rows = cross[0].shape[0]

    def put(pieces, at):
        for source in pieces:
            part = slice(at, at + source.shape[0])
            high[part, :], low[part, :] = split((source[...] - center[...]) * scale[...])
            at += source.shape[0]

    @pl.when(first_ref[0] == 1)
    def _():
        put(same, 0)
        put(cross, rows)

    @pl.when(first_ref[0] != 1)
    def _():
        put(cross, 0)
        put(same, rows)


def own_kernel(first, same_a, same_b, cross, center, scale, high, low, gram):
    normalize(first, (same_a, same_b), (cross,), center, scale, high, low)
    quarter = gram.shape[1] // 4
    for q in range(4):
        part = slice(q * quarter, (q + 1) * quarter)
        gram[:, part] = dot3(
            (high[...], low[...]), (high[part, :], low[part, :]), 1, 1
        )


def far_kernel(first, same, cross, center, scale, high_0, low_0, high, low, gram):
    normalize(first, (same,), (cross,), center, scale, high, low)
    quarter = gram.shape[1] // 4
    for q in range(4):
        part = slice(q * quarter, (q + 1) * quarter)
        gram[:, part] = dot3((high_0[...], low_0[...]), (high[part, :], low[part, :]), 1, 1)


def cube_kernel(first, label, same_a, same_b, cross, center, scale, high_0, low_0, *rest):
    high, low, forward = rest[:3]
    keeps, sends, whole = rest[3:7], rest[7:11], rest[11]
    half = same_a.shape[0]
    forward[:half, :] = same_a[...]
    forward[half:, :] = same_b[...]
    normalize(first, (same_a, same_b), (cross,), center, scale, high, low)
    quarter = whole.shape[1]
    chunk = whole.shape[0] // 16
    for q in range(4):
        part = slice(q * quarter, (q + 1) * quarter)
        whole[...] = dot3((high_0[...], low_0[...]), (high[part, :], low[part, :]), 1, 1)
        for p in range(16):
            at = pl.multiple_of((label[0] ^ masks[q][p]) * chunk, chunk)
            target = keeps[q] if p < 8 else sends[q]
            target[p % 8 * chunk : (p % 8 + 1) * chunk, :] = whole[pl.ds(at, chunk), :]


def front_kernel(first, one, two, stats, same_a, same_b, cross):
    rows = one.shape[0]
    half = rows // 2
    mean_one = jnp.sum(one[...], axis=0, keepdims=True) / rows
    mean_two = jnp.sum(two[...], axis=0, keepdims=True) / rows
    deviate_one = one[...] - mean_one
    deviate_two = two[...] - mean_two
    stats[...] = jnp.zeros(stats.shape, f32)
    stats[0:1, :] = mean_one
    stats[1:2, :] = mean_two
    stats[2:3, :] = jnp.sum(deviate_one * deviate_one, axis=0, keepdims=True)
    stats[3:4, :] = jnp.sum(deviate_two * deviate_two, axis=0, keepdims=True)
    stats[4:5, :] = jnp.sum(deviate_one * deviate_two, axis=0, keepdims=True)

    @pl.when(first[0] == 1)
    def _():
        same_a[...] = one[:half, :]
        same_b[...] = one[half:, :]
        cross[...] = two[...]

    @pl.when(first[0] != 1)
    def _():
        same_a[...] = two[:half, :]
        same_b[...] = two[half:, :]
        cross[...] = one[...]


def fold_kernel(*refs):
    half = refs[0].shape[0] // 2
    for q in range(4):
        keep, came, keep_out, send_out = refs[q::4]
        keep_out[...] = keep[:half, :] + came[:half, :]
        send_out[...] = keep[half:, :] + came[half:, :]


def last_fold_kernel(*refs):
    out = refs[8]
    cols = refs[0].shape[1]
    for q in range(4):
        out[:, q * cols : (q + 1) * cols] = refs[q][...] + refs[4 + q][...]


def part_kernel(mine, other, match, *parts):
    cols = parts[0].shape[1]
    for q in range(4):
        parts[q][...] = other[:, q * cols : (q + 1) * cols]
    match[...] = jnp.full(match.shape, jnp.sum(mine[...] * other[...]), f32)


def extend_kernel(share, match_1, match_0, mine, other, out):
    rows = other.shape[0]
    square = (
        2.0 * match_1[0:1, 0:1]
        + match_0[0:1, 0:1]
        + jnp.sum(mine[...] * other[...], keepdims=True)
    )
    out[:rows, :] = other[...]
    out[rows:, :] = jnp.broadcast_to(share[0] + share[1] * square, (8, out.shape[1]))


def join_kernel(*refs):
    rows = refs[0].shape[0]
    for q in range(4):
        own, came, out = refs[q::4]
        out[:rows, :] = own[...]
        out[rows:, :] = came[...]


def gather_rows(label, q, own, came, high, low, by_feat):
    chunk = high.shape[0] // 16
    for p in range(16):
        source = own if p < 8 else came
        owner = label[0] ^ masks[q][p]
        if by_feat:
            owner = owner ^ ((owner >> 1) & 5)
        at = pl.multiple_of(owner * chunk, chunk)
        high[pl.ds(at, chunk), :], low[pl.ds(at, chunk), :] = split(
            source[p % 8 * chunk : (p % 8 + 1) * chunk, :]
        )


def turned_kernel(label, *refs):
    owns, cames = refs[:4], refs[4:8]
    high_0, low_0, turned, high, low = refs[8:]
    quarter = high.shape[1]
    for q in range(4):
        part = slice(q * quarter, (q + 1) * quarter)
        gather_rows(label, q, owns[q], cames[q], high, low, False)
        turned[part, :] = dot3((high[...], low[...]), (high_0[...], low_0[...]), 0, 0)


def ahead_kernel(label, *refs):
    owns, cames = refs[:4], refs[4:8]
    high_1, low_1, ahead, high, low = refs[8:]
    quarter = high.shape[1]
    for q in range(4):
        part = slice(q * quarter, (q + 1) * quarter)
        gather_rows(label, q, owns[q], cames[q], high, low, False)
        term = dot3((high[...], low[...]), (high_1[part, :], low_1[part, :]), 1, 0)
        ahead[...] = term if q == 0 else ahead[...] + term


def own_times_kernel(label, *refs):
    owns, cames = refs[:4], refs[4:8]
    high_0, low_0, one, ahead, high, low = refs[8:]
    quarter = high.shape[1]
    ahead[...] = one[...]
    for q in range(4):
        part = slice(q * quarter, (q + 1) * quarter)
        gather_rows(label, q, owns[q], cames[q], high, low, True)
        ahead[...] += dot3((high[...], low[...]), (high_0[part, :], low_0[part, :]), 1, 0)


def last_kernel(
    factor, core, gram, high_2, low_2, high_0, low_0, one, two, kept, sent, sums, total, high, low
):
    rows = kept.shape[0]
    quarter = gram.shape[1]
    chunk = high.shape[0] // 16
    step = gram.shape[0] // 16
    q = pl.program_id(0)

    @pl.when(q == 0)
    def _():
        total[...] = one[...] + two[...]
        sums[...] = jnp.zeros(sums.shape, f32)

    loss = jnp.zeros((1, quarter), f32)
    for i in range(16):
        at = i * step
        high[i * chunk : (i + 1) * chunk, :], low[i * chunk : (i + 1) * chunk, :] = split(
            gram[at : at + chunk, :]
        )
        loss += gram[at + chunk : at + chunk + 1, :]
    part = pl.ds(pl.multiple_of(q * quarter, quarter), quarter)
    total[...] += dot3((high[...], low[...]), (high_2[part, :], low_2[part, :]), 1, 0)

    @pl.when(q == 3)
    def _():
        scaled = total[...] * factor[0]
        total[...] = scaled
        normed = high_0[...].astype(f32) + low_0[...].astype(f32)
        sums[0:1, :] = jnp.sum(scaled, axis=0, keepdims=True)
        sums[1:2, :] = jnp.sum(scaled * normed, axis=0, keepdims=True)
        sums[2:3, :quarter] = loss
        kept[...] = total[pl.ds(pl.multiple_of(core[0] * rows, rows), rows), :]
        sent[...] = total[pl.ds(pl.multiple_of((1 - core[0]) * rows, rows), rows), :]


def across(array, bit):
    return lax.ppermute(
        array, "feat", [(i, feat_of[label_of[i] ^ (1 << bit)]) for i in range(16)]
    )


def step_across(arrays, step):
    return [across(array, order[step]) for array, order in zip(arrays, orders)]


def fold(keeps, sends, step):
    cames = step_across(sends, step)
    rows, cols = keeps[0].shape
    if step == 3:
        return local_call(last_fold_kernel, (), (*keeps, *cames), [shape(rows, 4 * cols)])[0]
    outs = local_call(fold_kernel, (), (*keeps, *cames), [shape(rows // 2, cols)] * 8)
    return outs[:4], outs[4:]


def body(view_one, view_two):
    rows, cols = view_one.shape
    batch = lax.axis_size("batch")
    feats = lax.axis_size("feat")
    clip_total = rows * batch
    features = cols * feats
    core = lax.axis_index("batch") % 2
    on_first = core == 0
    first = (1 - core).astype(jnp.int32).reshape((1,))
    label = jnp.array(label_of, jnp.int32)[lax.axis_index("feat")].reshape((1,))
    swap = [(i, i ^ 1) for i in range(batch)]
    down = [(i, (i - 2) % batch) for i in range(batch)]
    up = [(i, (i + 2) % batch) for i in range(batch)]
    down_cross = [(i, (i ^ 1) - 2 if i > 1 else (i ^ 1) - 2 + batch) for i in range(batch)]
    up_cross = [(i, ((i ^ 1) + 2) % batch) for i in range(batch)]

    def pick(one, two):
        return jnp.where(on_first, one, two)

    mine, same_a0, same_b0, mine_cross = local_call(
        front_kernel,
        (first,),
        (view_one, view_two),
        [shape(8, cols), shape(rows // 2, cols), shape(rows // 2, cols), shape(rows, cols)],
    )
    same_a1 = lax.ppermute(same_a0, "batch", down)
    same_b1 = lax.ppermute(same_b0, "batch", down)
    cross_1 = lax.ppermute(mine_cross, "batch", down_cross)
    mate = lax.ppermute(mine, "batch", swap)
    pairs = [jnp.stack([pick(mine, mate), pick(mate, mine)])]
    for _ in range(batch // 2 - 1):
        pairs.append(lax.ppermute(pairs[-1], "batch", up))
    parts = jnp.concatenate(pairs, axis=0)
    parts, far_cross = lax.optimization_barrier((parts, mine_cross))
    cross_0 = lax.ppermute(mine_cross, "batch", swap)
    cross_0, same_a1 = lax.optimization_barrier((cross_0, same_a1))
    center_one = jnp.mean(parts[:, 0], axis=0)
    center_two = jnp.mean(parts[:, 1], axis=0)
    shift_one = parts[:, 0] - center_one
    shift_two = parts[:, 1] - center_two
    spread_one = jnp.sum(parts[:, 2] + rows * shift_one * shift_one, axis=0) / clip_total
    spread_two = jnp.sum(parts[:, 3] + rows * shift_two * shift_two, axis=0) / clip_total
    scale_one = 1.0 / jnp.sqrt(spread_one + epsilon)
    scale_two = 1.0 / jnp.sqrt(spread_two + epsilon)
    covary = jnp.sum(parts[:, 4] + rows * shift_one * shift_two, axis=0) / clip_total
    diagonal = covary * scale_one * scale_two
    center = pick(center_one, center_two).reshape((1, cols))
    scale = pick(scale_one, scale_two).reshape((1, cols))

    cross_up = lax.ppermute(far_cross, "batch", up_cross)
    block = 2 * rows
    quarter = block // 4
    product = 3 * 2 * block * block * cols
    halves = [shape(block, cols, bf16)] * 2
    row_scratch = [pltpu.VMEM((block, quarter), bf16)] * 2

    high_0, low_0, gram = local_call(
        own_kernel,
        (first,),
        (same_a0, same_b0, cross_0, center, scale),
        halves + [shape(block, block)],
        flops=product,
    )
    piece_0 = lax.psum_scatter(gram, "feat", scatter_dimension=0, tiled=True)
    same_a1, same_b1, cross_1, cross_up, high_0, low_0 = lax.optimization_barrier(
        (same_a1, same_b1, cross_1, cross_up, high_0, low_0)
    )

    high_1, low_1, forward, *outs = local_call(
        cube_kernel,
        (first, label),
        (same_a1, same_b1, cross_1, center, scale, high_0, low_0),
        halves + [shape(rows, cols)] + [shape(block // 2, quarter)] * 8,
        scratch=[pltpu.VMEM((block, quarter), f32)],
        flops=product,
    )
    keeps, sends = outs[:4], outs[4:]
    same_2 = lax.ppermute(forward, "batch", down)
    cross_2 = lax.ppermute(cross_up, "batch", up)
    keeps, sends = fold(keeps, sends, 0)

    same_2, cross_2, keeps[0] = lax.optimization_barrier((same_2, cross_2, keeps[0]))
    high_2, low_2, gram = local_call(
        far_kernel,
        (first,),
        (same_2, cross_2, center, scale, high_0, low_0),
        halves + [shape(block, block)],
        flops=product,
    )
    piece_2 = lax.psum_scatter(gram, "feat", scatter_dimension=0, tiled=True)
    *sends, gram = lax.optimization_barrier((*sends, gram))
    for step in (1, 2):
        keeps, sends = fold(keeps, sends, step)
    piece_1 = fold(keeps, sends, 3)

    def parts_of(piece, other):
        match, *owns = local_call(
            part_kernel,
            (),
            (piece, other),
            [shape(8, 128)] + [shape(block // 16, quarter)] * 4,
        )
        return match, owns

    def cube_gather(owns):
        for step in (3, 2, 1):
            cames = step_across(owns, step)
            owns = local_call(
                join_kernel, (), (*owns, *cames), [shape(2 * owns[0].shape[0], quarter)] * 4
            )
        return owns + step_across(owns, 0)

    square_weight = off_weight * 0.5 / (float(clip_total) * float(clip_total))
    share = (
        jnp.sum((1.0 - diagonal) ** 2) - off_weight * jnp.sum(diagonal * diagonal)
    ) / batch
    share = jnp.stack([share, jnp.full((), square_weight, f32)])
    piece_1, share = lax.optimization_barrier((piece_1, share))
    other_1 = lax.ppermute(piece_1, "batch", swap)
    match_1, owns_1 = parts_of(piece_1, other_1)
    gathered_1 = cube_gather(owns_1)
    (turned,) = local_call(
        turned_kernel,
        (label,),
        (*gathered_1, high_0, low_0),
        [shape(block, cols)],
        scratch=row_scratch,
        flops=product,
    )
    above = lax.ppermute(turned, "batch", up)
    (ahead,) = local_call(
        ahead_kernel,
        (label,),
        (*gathered_1, high_1, low_1),
        [shape(block, cols)],
        scratch=row_scratch,
        flops=product,
    )
    piece_0, piece_2, ahead = lax.optimization_barrier((piece_0, piece_2, ahead))
    other_2 = lax.ppermute(piece_2, "batch", swap)
    other_0 = lax.ppermute(piece_0, "batch", swap)
    match_0, owns_0 = parts_of(piece_0, other_0)
    (extended,) = local_call(
        extend_kernel,
        (share,),
        (match_1, match_0, piece_2, other_2),
        [shape(block // 16 + 8, block)],
    )
    owns_0[0], extended = lax.optimization_barrier((owns_0[0], extended))
    gram_2 = lax.all_gather(extended, "feat", axis=0, tiled=True)
    gathered_0 = cube_gather(owns_0)
    (rest,) = local_call(
        own_times_kernel,
        (label,),
        (*gathered_0, high_0, low_0, ahead),
        [shape(block, cols)],
        scratch=row_scratch,
        flops=product,
    )
    gram_2, rest = lax.optimization_barrier((gram_2, rest))
    factor = 2.0 * off_weight / (float(clip_total) * float(clip_total))

    def whole(rows, cols):
        return pl.BlockSpec((rows, cols), lambda q: (0, 0))

    kept, sent, own_sums = pl.pallas_call(
        last_kernel,
        out_shape=[shape(rows, cols), shape(rows, cols), shape(8, cols)],
        grid=(4,),
        in_specs=[smem, smem, pl.BlockSpec((block + 128, quarter), lambda q: (0, q))]
        + [whole(block, cols)] * 6,
        out_specs=[whole(rows, cols), whole(rows, cols), whole(8, cols)],
        scratch_shapes=[pltpu.VMEM((block, cols), f32)] + row_scratch,
        compiler_params=pltpu.CompilerParams(vmem_limit_bytes=60 * 1024 * 1024),
        cost_estimate=pl.CostEstimate(
            flops=product, bytes_accessed=14 * 1024 * 1024, transcendentals=0
        ),
    )(
        jnp.full((1,), factor, f32),
        core.astype(jnp.int32).reshape((1,)),
        gram_2,
        high_2,
        low_2,
        high_0,
        low_0,
        rest,
        above,
    )

    came = lax.ppermute(sent, "batch", swap)
    normed_one = (view_one - center_one) * scale_one
    normed_two = (view_two - center_two) * scale_two
    weight = (-2.0 * (1.0 - diagonal) - 2.0 * off_weight * diagonal) / clip_total
    gnorm_one = pick(kept, came) + normed_two * weight
    gnorm_two = pick(came, kept) + normed_one * weight
    zero = jnp.zeros((cols,), f32)
    product_sum = jnp.sum(normed_one * normed_two, axis=0) * weight
    sums = jnp.stack(
        [
            pick(own_sums[0], zero) + jnp.sum(normed_two, axis=0) * weight,
            pick(own_sums[1], zero) + product_sum,
            pick(zero, own_sums[0]) + jnp.sum(normed_one, axis=0) * weight,
            pick(zero, own_sums[1]) + product_sum,
        ]
    )
    sums, loss_total = lax.psum((sums, own_sums[2, :128]), "batch")
    sums = sums / clip_total
    grad_one = clip_total * (gnorm_one - sums[0] - normed_one * sums[1]) * scale_one
    grad_two = clip_total * (gnorm_two - sums[2] - normed_two * sums[3]) * scale_two
    return (grad_one, grad_two, loss_total[0] / features)


def solution(mesh):
    placed = (P("batch", "feat"), P("batch", "feat"))
    return jax.shard_map(
        body,
        mesh=mesh,
        in_specs=placed,
        out_specs=(P("batch", "feat"), P("batch", "feat"), P()),
        check_vma=False,
    )
```

```python
import jax
import jax.numpy as jnp
from jax import lax
from jax.experimental import pallas as pl
from jax.experimental.pallas import tpu as pltpu
from jax.sharding import PartitionSpec as P

epsilon = 1e-05
off_weight = 0.005
f32 = jnp.float32
bf16 = jnp.bfloat16

gray = (0, 1, 3, 2)
label_of = tuple(gray[i // 4] * 4 + gray[i % 4] for i in range(16))
feat_of = tuple(label_of.index(i) for i in range(16))
orders = ((3, 2, 1, 0), (2, 3, 0, 1), (1, 0, 3, 2), (0, 1, 2, 3))
masks = tuple(
    tuple(sum(((p >> (3 - j)) & 1) << order[j] for j in range(4)) for p in range(16))
    for order in orders
)

vmem = pl.BlockSpec(memory_space=pltpu.VMEM)
smem = pl.BlockSpec(memory_space=pltpu.SMEM)


def local_call(kernel, scalars, arrays, outs, scratch=(), flops=0):
    moved = sum(a.size * a.dtype.itemsize for a in (*arrays, *outs))
    call = pl.pallas_call(
        kernel,
        out_shape=list(outs),
        in_specs=[smem] * len(scalars) + [vmem] * len(arrays),
        out_specs=[vmem] * len(outs),
        scratch_shapes=list(scratch),
        compiler_params=pltpu.CompilerParams(vmem_limit_bytes=40 * 1024 * 1024),
        cost_estimate=pl.CostEstimate(flops=flops, bytes_accessed=moved, transcendentals=0),
    )
    return list(call(*scalars, *arrays))


def shape(rows, cols, dtype=f32):
    return jax.ShapeDtypeStruct((rows, cols), dtype)


def split(value):
    high = value.astype(bf16)
    return high, (value - high.astype(f32)).astype(bf16)


def dot3(left, right, left_dim, right_dim):
    def one(a, b):
        return lax.dot_general(
            a, b, (((left_dim,), (right_dim,)), ((), ())), preferred_element_type=f32
        )

    return one(left[0], right[0]) + (one(left[0], right[1]) + one(left[1], right[0]))


def normalize(first_ref, same, cross, center, scale, high, low):
    rows = cross[0].shape[0]

    def put(pieces, at):
        for source in pieces:
            part = slice(at, at + source.shape[0])
            high[part, :], low[part, :] = split((source[...] - center[...]) * scale[...])
            at += source.shape[0]

    @pl.when(first_ref[0] == 1)
    def _():
        put(same, 0)
        put(cross, rows)

    @pl.when(first_ref[0] != 1)
    def _():
        put(cross, 0)
        put(same, rows)


def near_kernel(
    first, same_0, cross_0, same_1, cross_1, center, scale, high_0, low_0, high_1, low_1, gram
):
    normalize(first, (same_0,), (cross_0,), center, scale, high_0, low_0)
    normalize(first, (same_1,), (cross_1,), center, scale, high_1, low_1)
    quarter = gram.shape[1] // 4
    for q in range(4):
        part = slice(q * quarter, (q + 1) * quarter)
        gram[:, part] = dot3((high_0[...], low_0[...]), (high_1[part, :], low_1[part, :]), 1, 1)


def cube_kernel(first, label, same, cross, center, scale, high_0, low_0, high, low, *rest):
    keeps, sends, whole = rest[:4], rest[4:8], rest[8]
    normalize(first, (same,), (cross,), center, scale, high, low)
    quarter = whole.shape[1]
    chunk = whole.shape[0] // 16
    for q in range(4):
        part = slice(q * quarter, (q + 1) * quarter)
        for right, at_col in (((high_0, low_0), 0), ((high, low), quarter)):
            whole[...] = dot3(
                (high_0[...], low_0[...]), (right[0][part, :], right[1][part, :]), 1, 1
            )
            for p in range(16):
                at = pl.multiple_of((label[0] ^ masks[q][p]) * chunk, chunk)
                target = keeps[q] if p < 8 else sends[q]
                target[p % 8 * chunk : (p % 8 + 1) * chunk, at_col : at_col + quarter] = whole[
                    pl.ds(at, chunk), :
                ]


def front_kernel(first, one, two, stats, same, cross):
    rows = one.shape[0]
    mean_one = jnp.sum(one[...], axis=0, keepdims=True) / rows
    mean_two = jnp.sum(two[...], axis=0, keepdims=True) / rows
    deviate_one = one[...] - mean_one
    deviate_two = two[...] - mean_two
    stats[...] = jnp.zeros(stats.shape, f32)
    stats[0:1, :] = mean_one
    stats[1:2, :] = mean_two
    stats[2:3, :] = jnp.sum(deviate_one * deviate_one, axis=0, keepdims=True)
    stats[3:4, :] = jnp.sum(deviate_two * deviate_two, axis=0, keepdims=True)
    stats[4:5, :] = jnp.sum(deviate_one * deviate_two, axis=0, keepdims=True)

    @pl.when(first[0] == 1)
    def _():
        same[...] = one[...]
        cross[...] = two[...]

    @pl.when(first[0] != 1)
    def _():
        same[...] = two[...]
        cross[...] = one[...]


def fold_kernel(*refs):
    half = refs[0].shape[0] // 2
    for q in range(4):
        keep, came, keep_out, send_out = refs[q::4]
        keep_out[...] = keep[:half, :] + came[:half, :]
        send_out[...] = keep[half:, :] + came[half:, :]


def last_fold_kernel(*refs):
    out = refs[8]
    cols = refs[0].shape[1]
    for q in range(4):
        out[:, q * cols : (q + 1) * cols] = refs[q][...] + refs[4 + q][...]


def match_kernel(mine, other, match):
    match[...] = jnp.full(match.shape, jnp.sum(mine[...] * other[...]), f32)


def part_kernel(share, match, mine, other, *parts):
    rows, cols = other.shape[0], parts[0].shape[1]
    square = 2.0 * match[0:1, 0:1] + jnp.sum(mine[...] * other[...], keepdims=True)
    for q in range(4):
        parts[q][:rows, :] = other[:, q * cols : (q + 1) * cols]
        parts[q][rows:, :] = jnp.broadcast_to(share[0] + share[1] * square, (8, cols))


def join_kernel(*refs):
    rows = refs[0].shape[0]
    for q in range(4):
        own, came, out = refs[q::4]
        out[:rows, :] = own[...]
        out[rows:, :] = came[...]


def gather_rows(label, q, own, came, high, low, second):
    chunk, cols = high.shape[0] // 16, high.shape[1]
    step = own.shape[0] // 8
    part = slice(cols, 2 * cols) if second else slice(0, cols)
    for p in range(16):
        source = own if p < 8 else came
        at = pl.multiple_of((label[0] ^ masks[q][p]) * chunk, chunk)
        high[pl.ds(at, chunk), :], low[pl.ds(at, chunk), :] = split(
            source[p % 8 * step : p % 8 * step + chunk, part]
        )


def turned_kernel(gram, high_0, low_0, token, turned):
    del token
    quarter = gram.shape[1] // 4
    for q in range(4):
        part = slice(q * quarter, (q + 1) * quarter)
        turned[part, :] = dot3(split(gram[:, part]), (high_0[...], low_0[...]), 0, 0)


def ahead_kernel(gram, high_1, low_1, ahead):
    quarter = gram.shape[1] // 4
    for q in range(4):
        part = slice(q * quarter, (q + 1) * quarter)
        term = dot3(split(gram[:, part]), (high_1[part, :], low_1[part, :]), 1, 0)
        ahead[...] = term if q == 0 else ahead[...] + term


def apply_kernel(label, *refs):
    owns, cames = refs[:4], refs[4:8]
    high_0, low_0, high_2, low_2, one, rest, loss, high, low = refs[8:]
    quarter = high.shape[1]
    rest[...] = one[...]
    for q in range(4):
        part = slice(q * quarter, (q + 1) * quarter)
        gather_rows(label, q, owns[q], cames[q], high, low, False)
        rest[...] += dot3((high[...], low[...]), (high_0[part, :], low_0[part, :]), 1, 0)
        gather_rows(label, q, owns[q], cames[q], high, low, True)
        rest[...] += dot3((high[...], low[...]), (high_2[part, :], low_2[part, :]), 1, 0)
    chunk = high.shape[0] // 16
    step = owns[0].shape[0] // 8
    total = jnp.zeros((8, 128), f32)
    for p in range(8):
        at = slice(p * step + chunk, (p + 1) * step)
        total += owns[0][at, :128] + cames[0][at, :128]
    loss[...] = total


def last_kernel(factor, core, rest, above, high_0, low_0, kept, sent, sums, total):
    rows = kept.shape[0]
    scaled = (rest[...] + above[...]) * factor[0]
    total[...] = scaled
    normed = high_0[...].astype(f32) + low_0[...].astype(f32)
    sums[...] = jnp.zeros(sums.shape, f32)
    sums[0:1, :] = jnp.sum(scaled, axis=0, keepdims=True)
    sums[1:2, :] = jnp.sum(scaled * normed, axis=0, keepdims=True)
    kept[...] = total[pl.ds(pl.multiple_of(core[0] * rows, rows), rows), :]
    sent[...] = total[pl.ds(pl.multiple_of((1 - core[0]) * rows, rows), rows), :]


def across(array, bit):
    return lax.ppermute(
        array, "feat", [(i, feat_of[label_of[i] ^ (1 << bit)]) for i in range(16)]
    )


def step_across(arrays, step):
    return [across(array, order[step]) for array, order in zip(arrays, orders)]


def fold(keeps, sends, step):
    cames = step_across(sends, step)
    rows, cols = keeps[0].shape
    if step == 3:
        return local_call(last_fold_kernel, (), (*keeps, *cames), [shape(rows, 4 * cols)])[0]
    outs = local_call(fold_kernel, (), (*keeps, *cames), [shape(rows // 2, cols)] * 8)
    return outs[:4], outs[4:]


def body(view_one, view_two):
    rows, cols = view_one.shape
    batch = lax.axis_size("batch")
    feats = lax.axis_size("feat")
    clip_total = rows * batch
    features = cols * feats
    core = lax.axis_index("batch") % 2
    on_first = core == 0
    first = (1 - core).astype(jnp.int32).reshape((1,))
    label = jnp.array(label_of, jnp.int32)[lax.axis_index("feat")].reshape((1,))
    swap = [(i, i ^ 1) for i in range(batch)]
    down = [(i, (i - 2) % batch) for i in range(batch)]
    up = [(i, (i + 2) % batch) for i in range(batch)]
    down_cross = [(i, (i ^ 1) - 2 if i > 1 else (i ^ 1) - 2 + batch) for i in range(batch)]
    up_cross = [(i, ((i ^ 1) + 2) % batch) for i in range(batch)]

    def pick(one, two):
        return jnp.where(on_first, one, two)

    mine, same_0, mine_cross = local_call(
        front_kernel,
        (first,),
        (view_one, view_two),
        [shape(8, cols), shape(rows, cols), shape(rows, cols)],
    )
    same_1 = lax.ppermute(same_0, "batch", down)
    cross_1 = lax.ppermute(mine_cross, "batch", down_cross)
    cross_up = lax.ppermute(mine_cross, "batch", up_cross)
    mate = lax.ppermute(mine, "batch", swap)
    pairs = [jnp.stack([pick(mine, mate), pick(mate, mine)])]
    for _ in range(batch // 2 - 1):
        pairs.append(lax.ppermute(pairs[-1], "batch", up))
    parts = jnp.concatenate(pairs, axis=0)
    cross_0 = lax.ppermute(mine_cross, "batch", swap)
    center_one = jnp.mean(parts[:, 0], axis=0)
    center_two = jnp.mean(parts[:, 1], axis=0)
    shift_one = parts[:, 0] - center_one
    shift_two = parts[:, 1] - center_two
    spread_one = jnp.sum(parts[:, 2] + rows * shift_one * shift_one, axis=0) / clip_total
    spread_two = jnp.sum(parts[:, 3] + rows * shift_two * shift_two, axis=0) / clip_total
    scale_one = 1.0 / jnp.sqrt(spread_one + epsilon)
    scale_two = 1.0 / jnp.sqrt(spread_two + epsilon)
    covary = jnp.sum(parts[:, 4] + rows * shift_one * shift_two, axis=0) / clip_total
    diagonal = covary * scale_one * scale_two
    center = pick(center_one, center_two).reshape((1, cols))
    scale = pick(scale_one, scale_two).reshape((1, cols))

    block = 2 * rows
    quarter = block // 4
    product = 3 * 2 * block * block * cols
    halves = [shape(block, cols, bf16)] * 2
    row_scratch = [pltpu.VMEM((block, quarter), bf16)] * 2

    high_0, low_0, high_1, low_1, gram = local_call(
        near_kernel,
        (first,),
        (same_0, cross_0, same_1, cross_1, center, scale),
        halves * 2 + [shape(block, block)],
        flops=product,
    )
    piece_1 = lax.psum_scatter(gram, "feat", scatter_dimension=0, tiled=True)

    same_1, cross_up, high_0 = lax.optimization_barrier((same_1, cross_up, high_0))
    same_2 = lax.ppermute(same_1, "batch", down)
    cross_2 = lax.ppermute(cross_up, "batch", up)

    high_2, low_2, *outs = local_call(
        cube_kernel,
        (first, label),
        (same_2, cross_2, center, scale, high_0, low_0),
        halves + [shape(block // 2, 2 * quarter)] * 8,
        scratch=[pltpu.VMEM((block, quarter), f32)],
        flops=2 * product,
    )
    keeps, sends = outs[:4], outs[4:]
    for step in (0, 1):
        keeps, sends = fold(keeps, sends, step)
    piece_1, keeps[0] = lax.optimization_barrier((piece_1, keeps[0]))
    other_1 = lax.ppermute(piece_1, "batch", swap)
    gram_1 = lax.all_gather(other_1, "feat", axis=0, tiled=True)
    (match_1,) = local_call(match_kernel, (), (piece_1, other_1), [shape(8, 128)])
    keeps, sends = fold(keeps, sends, 2)
    piece = fold(keeps, sends, 3)

    square_weight = off_weight * 0.5 / (float(clip_total) * float(clip_total))
    share = (
        jnp.sum((1.0 - diagonal) ** 2) - off_weight * jnp.sum(diagonal * diagonal)
    ) / batch
    share = jnp.stack([share, jnp.full((), square_weight, f32)])
    piece, share, match_1 = lax.optimization_barrier((piece, share, match_1))
    other = lax.ppermute(piece, "batch", swap)
    owns = local_call(
        part_kernel,
        (share,),
        (match_1, piece, other),
        [shape(block // 16 + 8, 2 * quarter)] * 4,
    )
    for step in (3, 2, 1):
        cames = step_across(owns, step)
        owns = local_call(
            join_kernel, (), (*owns, *cames), [shape(2 * owns[0].shape[0], 2 * quarter)] * 4
        )
        if step == 2:
            token = owns[0][:8, :128]
    gathered = owns + step_across(owns, 0)

    (turned,) = local_call(
        turned_kernel,
        (),
        (gram_1, high_0, low_0, token),
        [shape(block, cols)],
        flops=product,
    )
    above = lax.ppermute(turned, "batch", up)
    (ahead,) = local_call(
        ahead_kernel, (), (gram_1, high_1, low_1), [shape(block, cols)], flops=product
    )
    rest, loss_sum = local_call(
        apply_kernel,
        (label,),
        (*gathered, high_0, low_0, high_2, low_2, ahead),
        [shape(block, cols), shape(8, 128)],
        scratch=row_scratch,
        flops=2 * product,
    )
    factor = 2.0 * off_weight / (float(clip_total) * float(clip_total))
    kept, sent, own_sums = local_call(
        last_kernel,
        (jnp.full((1,), factor, f32), core.astype(jnp.int32).reshape((1,))),
        (rest, above, high_0, low_0),
        [shape(rows, cols)] * 2 + [shape(8, cols)],
        scratch=[pltpu.VMEM((block, cols), f32)],
    )

    came = lax.ppermute(sent, "batch", swap)
    normed_one = (view_one - center_one) * scale_one
    normed_two = (view_two - center_two) * scale_two
    weight = (-2.0 * (1.0 - diagonal) - 2.0 * off_weight * diagonal) / clip_total
    gnorm_one = pick(kept, came) + normed_two * weight
    gnorm_two = pick(came, kept) + normed_one * weight
    zero = jnp.zeros((cols,), f32)
    product_sum = jnp.sum(normed_one * normed_two, axis=0) * weight
    sums = jnp.stack(
        [
            pick(own_sums[0], zero) + jnp.sum(normed_two, axis=0) * weight,
            pick(own_sums[1], zero) + product_sum,
            pick(zero, own_sums[0]) + jnp.sum(normed_one, axis=0) * weight,
            pick(zero, own_sums[1]) + product_sum,
        ]
    )
    sums, loss_total = lax.psum((sums, loss_sum[0]), "batch")
    sums = sums / clip_total
    grad_one = clip_total * (gnorm_one - sums[0] - normed_one * sums[1]) * scale_one
    grad_two = clip_total * (gnorm_two - sums[2] - normed_two * sums[3]) * scale_two
    return (grad_one, grad_two, loss_total[0] / features)


def solution(mesh):
    placed = (P("batch", "feat"), P("batch", "feat"))
    return jax.shard_map(
        body,
        mesh=mesh,
        in_specs=placed,
        out_specs=(P("batch", "feat"), P("batch", "feat"), P()),
        check_vma=False,
    )
```

```python
import jax
import jax.numpy as jnp
from jax import lax
from jax.experimental import pallas as pl
from jax.experimental.pallas import tpu as pltpu
from jax.sharding import PartitionSpec as P

epsilon = 1e-05
off_weight = 0.005
f32 = jnp.float32
bf16 = jnp.bfloat16

gray = (0, 1, 3, 2)
label_of = tuple(gray[i // 4] * 4 + gray[i % 4] for i in range(16))
feat_of = tuple(label_of.index(i) for i in range(16))
orders = ((3, 2, 1, 0), (2, 3, 0, 1), (1, 0, 3, 2), (0, 1, 2, 3))
masks = tuple(
    tuple(sum(((p >> (3 - j)) & 1) << order[j] for j in range(4)) for p in range(16))
    for order in orders
)

vmem = pl.BlockSpec(memory_space=pltpu.VMEM)
smem = pl.BlockSpec(memory_space=pltpu.SMEM)


def local_call(kernel, scalars, arrays, outs, scratch=(), flops=0, mib=40):
    moved = sum(a.size * a.dtype.itemsize for a in (*arrays, *outs))
    call = pl.pallas_call(
        kernel,
        out_shape=list(outs),
        in_specs=[smem] * len(scalars) + [vmem] * len(arrays),
        out_specs=[vmem] * len(outs),
        scratch_shapes=list(scratch),
        compiler_params=pltpu.CompilerParams(vmem_limit_bytes=mib * 1024 * 1024),
        cost_estimate=pl.CostEstimate(flops=flops, bytes_accessed=moved, transcendentals=0),
    )
    return list(call(*scalars, *arrays))


def shape(rows, cols, dtype=f32):
    return jax.ShapeDtypeStruct((rows, cols), dtype)


def split(value):
    high = value.astype(bf16)
    return high, (value - high.astype(f32)).astype(bf16)


def dot3(left, right, left_dim, right_dim):
    def one(a, b):
        return lax.dot_general(
            a, b, (((left_dim,), (right_dim,)), ((), ())), preferred_element_type=f32
        )

    return one(left[0], right[0]) + (one(left[0], right[1]) + one(left[1], right[0]))


def normalize(first_ref, same, cross, center, scale, high, low):
    rows = cross[0].shape[0]

    def put(pieces, at):
        for source in pieces:
            part = slice(at, at + source.shape[0])
            high[part, :], low[part, :] = split((source[...] - center[...]) * scale[...])
            at += source.shape[0]

    @pl.when(first_ref[0] == 1)
    def _():
        put(same, 0)
        put(cross, rows)

    @pl.when(first_ref[0] != 1)
    def _():
        put(cross, 0)
        put(same, rows)


def near_kernel(
    first, same_0, cross_0, same_1, cross_1, center, scale, high_0, low_0, high_1, low_1, gram
):
    normalize(first, (same_0,), (cross_0,), center, scale, high_0, low_0)
    normalize(first, (same_1,), (cross_1,), center, scale, high_1, low_1)
    quarter = gram.shape[1] // 4
    for q in range(4):
        part = slice(q * quarter, (q + 1) * quarter)
        gram[:, part] = dot3((high_0[...], low_0[...]), (high_1[part, :], low_1[part, :]), 1, 1)


def cube_kernel(first, label, same, cross, center, scale, high_0, low_0, high, low, *rest):
    keeps, sends, whole = rest[:4], rest[4:8], rest[8]
    normalize(first, (same,), (cross,), center, scale, high, low)
    quarter = whole.shape[1]
    chunk = whole.shape[0] // 16
    for q in range(4):
        part = slice(q * quarter, (q + 1) * quarter)
        for right, at_col in (((high_0, low_0), 0), ((high, low), quarter)):
            whole[...] = dot3(
                (high_0[...], low_0[...]), (right[0][part, :], right[1][part, :]), 1, 1
            )
            for p in range(16):
                at = pl.multiple_of((label[0] ^ masks[q][p]) * chunk, chunk)
                target = keeps[q] if p < 8 else sends[q]
                target[p % 8 * chunk : (p % 8 + 1) * chunk, at_col : at_col + quarter] = whole[
                    pl.ds(at, chunk), :
                ]


def front_kernel(first, one, two, stats, same, cross):
    rows = one.shape[0]
    mean_one = jnp.sum(one[...], axis=0, keepdims=True) / rows
    mean_two = jnp.sum(two[...], axis=0, keepdims=True) / rows
    deviate_one = one[...] - mean_one
    deviate_two = two[...] - mean_two
    stats[...] = jnp.zeros(stats.shape, f32)
    stats[0:1, :] = mean_one
    stats[1:2, :] = mean_two
    stats[2:3, :] = jnp.sum(deviate_one * deviate_one, axis=0, keepdims=True)
    stats[3:4, :] = jnp.sum(deviate_two * deviate_two, axis=0, keepdims=True)
    stats[4:5, :] = jnp.sum(deviate_one * deviate_two, axis=0, keepdims=True)

    @pl.when(first[0] == 1)
    def _():
        same[...] = one[...]
        cross[...] = two[...]

    @pl.when(first[0] != 1)
    def _():
        same[...] = two[...]
        cross[...] = one[...]


def fold_kernel(*refs):
    half = refs[0].shape[0] // 2
    for q in range(4):
        keep, came, keep_out, send_out = refs[q::4]
        keep_out[...] = keep[:half, :] + came[:half, :]
        send_out[...] = keep[half:, :] + came[half:, :]


def last_fold_kernel(*refs):
    out = refs[8]
    cols = refs[0].shape[1]
    for q in range(4):
        out[:, q * cols : (q + 1) * cols] = refs[q][...] + refs[4 + q][...]


def match_kernel(mine, other, match):
    match[...] = jnp.full(match.shape, jnp.sum(mine[...] * other[...]), f32)


def part_kernel(share, match, mine, other, *parts):
    rows, cols = other.shape[0], parts[0].shape[1]
    square = 2.0 * match[0:1, 0:1] + jnp.sum(mine[...] * other[...], keepdims=True)
    for q in range(4):
        parts[q][:rows, :] = other[:, q * cols : (q + 1) * cols]
        parts[q][rows:, :] = jnp.broadcast_to(share[0] + share[1] * square, (8, cols))


def join_kernel(*refs):
    rows = refs[0].shape[0]
    for q in range(4):
        own, came, out = refs[q::4]
        out[:rows, :] = own[...]
        out[rows:, :] = came[...]


def gather_rows(label, q, own, came, high, low, second):
    chunk, cols = high.shape[0] // 16, high.shape[1]
    step = own.shape[0] // 8
    part = slice(cols, 2 * cols) if second else slice(0, cols)
    for p in range(16):
        source = own if p < 8 else came
        at = pl.multiple_of((label[0] ^ masks[q][p]) * chunk, chunk)
        high[pl.ds(at, chunk), :], low[pl.ds(at, chunk), :] = split(
            source[p % 8 * step : p % 8 * step + chunk, part]
        )


def turned_kernel(gram, high_0, low_0, token, turned):
    del token
    quarter = gram.shape[1] // 4
    for q in range(4):
        part = slice(q * quarter, (q + 1) * quarter)
        turned[part, :] = dot3(split(gram[:, part]), (high_0[...], low_0[...]), 0, 0)


def ahead_kernel(gram, high_1, low_1, ahead):
    quarter = gram.shape[1] // 4
    for q in range(4):
        part = slice(q * quarter, (q + 1) * quarter)
        term = dot3(split(gram[:, part]), (high_1[part, :], low_1[part, :]), 1, 0)
        ahead[...] = term if q == 0 else ahead[...] + term


def apply_kernel(label, *refs):
    owns, cames = refs[:4], refs[4:8]
    high_0, low_0, high_2, low_2, one, rest, loss, high, low = refs[8:]
    quarter = high.shape[1]
    rest[...] = one[...]
    for q in range(4):
        part = slice(q * quarter, (q + 1) * quarter)
        gather_rows(label, q, owns[q], cames[q], high, low, False)
        rest[...] += dot3((high[...], low[...]), (high_0[part, :], low_0[part, :]), 1, 0)
        gather_rows(label, q, owns[q], cames[q], high, low, True)
        rest[...] += dot3((high[...], low[...]), (high_2[part, :], low_2[part, :]), 1, 0)
    chunk = high.shape[0] // 16
    step = owns[0].shape[0] // 8
    total = jnp.zeros((8, 128), f32)
    for p in range(8):
        at = slice(p * step + chunk, (p + 1) * step)
        total += owns[0][at, :128] + cames[0][at, :128]
    loss[...] = total


def last_kernel(factor, core, rest, above, high_0, low_0, kept, sent, sums, total):
    rows = kept.shape[0]
    scaled = (rest[...] + above[...]) * factor[0]
    total[...] = scaled
    normed = high_0[...].astype(f32) + low_0[...].astype(f32)
    sums[...] = jnp.zeros(sums.shape, f32)
    sums[0:1, :] = jnp.sum(scaled, axis=0, keepdims=True)
    sums[1:2, :] = jnp.sum(scaled * normed, axis=0, keepdims=True)
    kept[...] = total[pl.ds(pl.multiple_of(core[0] * rows, rows), rows), :]
    sent[...] = total[pl.ds(pl.multiple_of((1 - core[0]) * rows, rows), rows), :]


def across(array, bit):
    return lax.ppermute(
        array, "feat", [(i, feat_of[label_of[i] ^ (1 << bit)]) for i in range(16)]
    )


def step_across(arrays, step):
    return [across(array, order[step]) for array, order in zip(arrays, orders)]


def fold(keeps, sends, step):
    cames = step_across(sends, step)
    rows, cols = keeps[0].shape
    if step == 3:
        return local_call(last_fold_kernel, (), (*keeps, *cames), [shape(rows, 4 * cols)])[0]
    outs = local_call(fold_kernel, (), (*keeps, *cames), [shape(rows // 2, cols)] * 8)
    return outs[:4], outs[4:]


def body(view_one, view_two):
    rows, cols = view_one.shape
    batch = lax.axis_size("batch")
    feats = lax.axis_size("feat")
    clip_total = rows * batch
    features = cols * feats
    core = lax.axis_index("batch") % 2
    on_first = core == 0
    first = (1 - core).astype(jnp.int32).reshape((1,))
    label = jnp.array(label_of, jnp.int32)[lax.axis_index("feat")].reshape((1,))
    swap = [(i, i ^ 1) for i in range(batch)]
    down = [(i, (i - 2) % batch) for i in range(batch)]
    up = [(i, (i + 2) % batch) for i in range(batch)]
    down_cross = [(i, (i ^ 1) - 2 if i > 1 else (i ^ 1) - 2 + batch) for i in range(batch)]
    up_cross = [(i, ((i ^ 1) + 2) % batch) for i in range(batch)]

    def pick(one, two):
        return jnp.where(on_first, one, two)

    mine, same_0, mine_cross = local_call(
        front_kernel,
        (first,),
        (view_one, view_two),
        [shape(8, cols), shape(rows, cols), shape(rows, cols)],
        mib=60,
    )
    same_1 = lax.ppermute(same_0, "batch", down)
    cross_1 = lax.ppermute(mine_cross, "batch", down_cross)
    cross_up = lax.ppermute(mine_cross, "batch", up_cross)
    mate = lax.ppermute(mine, "batch", swap)
    pairs = [jnp.stack([pick(mine, mate), pick(mate, mine)])]
    for _ in range(batch // 2 - 1):
        pairs.append(lax.ppermute(pairs[-1], "batch", up))
    parts = jnp.concatenate(pairs, axis=0)
    cross_0 = lax.ppermute(mine_cross, "batch", swap)
    cross_0, cross_up = lax.optimization_barrier((cross_0, cross_up))
    center_one = jnp.mean(parts[:, 0], axis=0)
    center_two = jnp.mean(parts[:, 1], axis=0)
    shift_one = parts[:, 0] - center_one
    shift_two = parts[:, 1] - center_two
    spread_one = jnp.sum(parts[:, 2] + rows * shift_one * shift_one, axis=0) / clip_total
    spread_two = jnp.sum(parts[:, 3] + rows * shift_two * shift_two, axis=0) / clip_total
    scale_one = 1.0 / jnp.sqrt(spread_one + epsilon)
    scale_two = 1.0 / jnp.sqrt(spread_two + epsilon)
    covary = jnp.sum(parts[:, 4] + rows * shift_one * shift_two, axis=0) / clip_total
    diagonal = covary * scale_one * scale_two
    center = pick(center_one, center_two).reshape((1, cols))
    scale = pick(scale_one, scale_two).reshape((1, cols))

    block = 2 * rows
    quarter = block // 4
    product = 3 * 2 * block * block * cols
    halves = [shape(block, cols, bf16)] * 2
    row_scratch = [pltpu.VMEM((block, quarter), bf16)] * 2

    high_0, low_0, high_1, low_1, gram = local_call(
        near_kernel,
        (first,),
        (same_0, cross_0, same_1, cross_1, center, scale),
        halves * 2 + [shape(block, block)],
        flops=product,
    )
    piece_1 = lax.psum_scatter(gram, "feat", scatter_dimension=0, tiled=True)

    same_1, cross_up, high_0 = lax.optimization_barrier((same_1, cross_up, high_0))
    same_2 = lax.ppermute(same_1, "batch", down)
    cross_2 = lax.ppermute(cross_up, "batch", up)

    high_2, low_2, *outs = local_call(
        cube_kernel,
        (first, label),
        (same_2, cross_2, center, scale, high_0, low_0),
        halves + [shape(block // 2, 2 * quarter)] * 8,
        scratch=[pltpu.VMEM((block, quarter), f32)],
        flops=2 * product,
    )
    keeps, sends = outs[:4], outs[4:]
    for step in (0, 1):
        keeps, sends = fold(keeps, sends, step)
    piece_1, keeps[0] = lax.optimization_barrier((piece_1, keeps[0]))
    other_1 = lax.ppermute(piece_1, "batch", swap)
    gram_1 = lax.all_gather(other_1, "feat", axis=0, tiled=True)
    (match_1,) = local_call(match_kernel, (), (piece_1, other_1), [shape(8, 128)])
    keeps, sends = fold(keeps, sends, 2)
    piece = fold(keeps, sends, 3)

    square_weight = off_weight * 0.5 / (float(clip_total) * float(clip_total))
    share = (
        jnp.sum((1.0 - diagonal) ** 2) - off_weight * jnp.sum(diagonal * diagonal)
    ) / batch
    share = jnp.stack([share, jnp.full((), square_weight, f32)])
    piece, share, match_1 = lax.optimization_barrier((piece, share, match_1))
    other = lax.ppermute(piece, "batch", swap)
    owns = local_call(
        part_kernel,
        (share,),
        (match_1, piece, other),
        [shape(block // 16 + 8, 2 * quarter)] * 4,
    )
    for step in (3, 2, 1):
        cames = step_across(owns, step)
        owns = local_call(
            join_kernel, (), (*owns, *cames), [shape(2 * owns[0].shape[0], 2 * quarter)] * 4
        )
        if step == 2:
            token = owns[0][:8, :128]
    gathered = owns + step_across(owns, 0)

    (turned,) = local_call(
        turned_kernel,
        (),
        (gram_1, high_0, low_0, token),
        [shape(block, cols)],
        flops=product,
    )
    above = lax.ppermute(turned, "batch", up)
    (ahead,) = local_call(
        ahead_kernel, (), (gram_1, high_1, low_1), [shape(block, cols)], flops=product
    )
    rest, loss_sum = local_call(
        apply_kernel,
        (label,),
        (*gathered, high_0, low_0, high_2, low_2, ahead),
        [shape(block, cols), shape(8, 128)],
        scratch=row_scratch,
        flops=2 * product,
    )
    factor = 2.0 * off_weight / (float(clip_total) * float(clip_total))
    kept, sent, own_sums = local_call(
        last_kernel,
        (jnp.full((1,), factor, f32), core.astype(jnp.int32).reshape((1,))),
        (rest, above, high_0, low_0),
        [shape(rows, cols)] * 2 + [shape(8, cols)],
        scratch=[pltpu.VMEM((block, cols), f32)],
    )

    came = lax.ppermute(sent, "batch", swap)
    normed_one = (view_one - center_one) * scale_one
    normed_two = (view_two - center_two) * scale_two
    weight = (-2.0 * (1.0 - diagonal) - 2.0 * off_weight * diagonal) / clip_total
    gnorm_one = pick(kept, came) + normed_two * weight
    gnorm_two = pick(came, kept) + normed_one * weight
    zero = jnp.zeros((cols,), f32)
    product_sum = jnp.sum(normed_one * normed_two, axis=0) * weight
    sums = jnp.stack(
        [
            pick(own_sums[0], zero) + jnp.sum(normed_two, axis=0) * weight,
            pick(own_sums[1], zero) + product_sum,
            pick(zero, own_sums[0]) + jnp.sum(normed_one, axis=0) * weight,
            pick(zero, own_sums[1]) + product_sum,
        ]
    )
    sums, loss_total = lax.psum((sums, loss_sum[0]), "batch")
    sums = sums / clip_total
    grad_one = clip_total * (gnorm_one - sums[0] - normed_one * sums[1]) * scale_one
    grad_two = clip_total * (gnorm_two - sums[2] - normed_two * sums[3]) * scale_two
    return (grad_one, grad_two, loss_total[0] / features)


def solution(mesh):
    placed = (P("batch", "feat"), P("batch", "feat"))
    return jax.shard_map(
        body,
        mesh=mesh,
        in_specs=placed,
        out_specs=(P("batch", "feat"), P("batch", "feat"), P()),
        check_vma=False,
    )
```

```python
import jax
import jax.numpy as jnp
from jax import lax
from jax.experimental import pallas as pl
from jax.experimental.pallas import tpu as pltpu
from jax.sharding import PartitionSpec as P

epsilon = 1e-05
off_weight = 0.005
f32 = jnp.float32
bf16 = jnp.bfloat16

gray = (0, 1, 3, 2)
label_of = tuple(gray[i // 4] * 4 + gray[i % 4] for i in range(16))
feat_of = tuple(label_of.index(i) for i in range(16))
orders = ((3, 2, 1, 0), (2, 3, 0, 1), (1, 0, 3, 2), (0, 1, 2, 3))
masks = tuple(
    tuple(sum(((p >> (3 - j)) & 1) << order[j] for j in range(4)) for p in range(16))
    for order in orders
)

vmem = pl.BlockSpec(memory_space=pltpu.VMEM)
smem = pl.BlockSpec(memory_space=pltpu.SMEM)


def local_call(kernel, scalars, arrays, outs, scratch=(), flops=0, mib=40):
    moved = sum(a.size * a.dtype.itemsize for a in (*arrays, *outs))
    call = pl.pallas_call(
        kernel,
        out_shape=list(outs),
        in_specs=[smem] * len(scalars) + [vmem] * len(arrays),
        out_specs=[vmem] * len(outs),
        scratch_shapes=list(scratch),
        compiler_params=pltpu.CompilerParams(vmem_limit_bytes=mib * 1024 * 1024),
        cost_estimate=pl.CostEstimate(flops=flops, bytes_accessed=moved, transcendentals=0),
    )
    return list(call(*scalars, *arrays))


def shape(rows, cols, dtype=f32):
    return jax.ShapeDtypeStruct((rows, cols), dtype)


def split(value):
    high = value.astype(bf16)
    return high, (value - high.astype(f32)).astype(bf16)


def dot3(left, right, left_dim, right_dim):
    def one(a, b):
        return lax.dot_general(
            a, b, (((left_dim,), (right_dim,)), ((), ())), preferred_element_type=f32
        )

    return one(left[0], right[0]) + (one(left[0], right[1]) + one(left[1], right[0]))


def normalize(first_ref, same, cross, center, scale, high, low):
    rows = cross[0].shape[0]

    def put(pieces, at):
        for source in pieces:
            part = slice(at, at + source.shape[0])
            high[part, :], low[part, :] = split((source[...] - center[...]) * scale[...])
            at += source.shape[0]

    @pl.when(first_ref[0] == 1)
    def _():
        put(same, 0)
        put(cross, rows)

    @pl.when(first_ref[0] != 1)
    def _():
        put(cross, 0)
        put(same, rows)


def near_kernel(
    first, same_0, cross_0, same_1, cross_1, center, scale, high_0, low_0, high_1, low_1, gram
):
    normalize(first, (same_0,), (cross_0,), center, scale, high_0, low_0)
    normalize(first, (same_1,), (cross_1,), center, scale, high_1, low_1)
    quarter = gram.shape[1] // 4
    for q in range(4):
        part = slice(q * quarter, (q + 1) * quarter)
        gram[:, part] = dot3((high_0[...], low_0[...]), (high_1[part, :], low_1[part, :]), 1, 1)


def cube_kernel(first, label, same, cross, center, scale, high_0, low_0, high, low, *rest):
    keeps, sends, whole = rest[:4], rest[4:8], rest[8]
    normalize(first, (same,), (cross,), center, scale, high, low)
    quarter = whole.shape[1]
    chunk = whole.shape[0] // 16
    for q in range(4):
        part = slice(q * quarter, (q + 1) * quarter)
        for right, at_col in (((high_0, low_0), 0), ((high, low), quarter)):
            whole[...] = dot3(
                (high_0[...], low_0[...]), (right[0][part, :], right[1][part, :]), 1, 1
            )
            for p in range(16):
                at = pl.multiple_of((label[0] ^ masks[q][p]) * chunk, chunk)
                target = keeps[q] if p < 8 else sends[q]
                target[p % 8 * chunk : (p % 8 + 1) * chunk, at_col : at_col + quarter] = whole[
                    pl.ds(at, chunk), :
                ]


def front_kernel(first, one, two, stats, same, cross):
    rows = one.shape[0]
    mean_one = jnp.sum(one[...], axis=0, keepdims=True) / rows
    mean_two = jnp.sum(two[...], axis=0, keepdims=True) / rows
    deviate_one = one[...] - mean_one
    deviate_two = two[...] - mean_two
    stats[...] = jnp.zeros(stats.shape, f32)
    stats[0:1, :] = mean_one
    stats[1:2, :] = mean_two
    stats[2:3, :] = jnp.sum(deviate_one * deviate_one, axis=0, keepdims=True)
    stats[3:4, :] = jnp.sum(deviate_two * deviate_two, axis=0, keepdims=True)
    stats[4:5, :] = jnp.sum(deviate_one * deviate_two, axis=0, keepdims=True)

    @pl.when(first[0] == 1)
    def _():
        same[...] = one[...]
        cross[...] = two[...]

    @pl.when(first[0] != 1)
    def _():
        same[...] = two[...]
        cross[...] = one[...]


def fold_kernel(*refs):
    half = refs[0].shape[0] // 2
    for q in range(4):
        keep, came, keep_out, send_out = refs[q::4]
        keep_out[...] = keep[:half, :] + came[:half, :]
        send_out[...] = keep[half:, :] + came[half:, :]


def last_fold_kernel(*refs):
    out = refs[8]
    cols = refs[0].shape[1]
    for q in range(4):
        out[:, q * cols : (q + 1) * cols] = refs[q][...] + refs[4 + q][...]


def match_kernel(mine, other, match):
    match[...] = jnp.full(match.shape, jnp.sum(mine[...] * other[...]), f32)


def part_kernel(share, match, mine, other, *parts):
    rows, cols = other.shape[0], parts[0].shape[1]
    square = 2.0 * match[0:1, 0:1] + jnp.sum(mine[...] * other[...], keepdims=True)
    for q in range(4):
        parts[q][:rows, :] = other[:, q * cols : (q + 1) * cols]
        parts[q][rows:, :] = jnp.broadcast_to(share[0] + share[1] * square, (8, cols))


def join_kernel(*refs):
    rows = refs[0].shape[0]
    for q in range(4):
        own, came, out = refs[q::4]
        out[:rows, :] = own[...]
        out[rows:, :] = came[...]


def add_sums(sums, rows, halves, at):
    normed = halves[0][at, :].astype(f32) + halves[1][at, :].astype(f32)
    sums[0:1, :] += jnp.sum(rows, axis=0, keepdims=True)
    sums[1:2, :] += jnp.sum(rows * normed, axis=0, keepdims=True)


def turned_kernel(gram, high_0, low_0, high_1, low_1, token, turned, sums):
    del token
    quarter = gram.shape[1] // 4
    sums[...] = jnp.zeros(sums.shape, f32)
    for q in range(4):
        part = slice(q * quarter, (q + 1) * quarter)
        term = dot3(split(gram[:, part]), (high_0[...], low_0[...]), 0, 0)
        turned[part, :] = term
        add_sums(sums, term, (high_1, low_1), part)


def ahead_kernel(gram, high_1, low_1, ahead):
    quarter = gram.shape[1] // 4
    for q in range(4):
        part = slice(q * quarter, (q + 1) * quarter)
        term = dot3(split(gram[:, part]), (high_1[part, :], low_1[part, :]), 1, 0)
        ahead[...] = term if q == 0 else ahead[...] + term


def half_kernel(base, label, *refs):
    parts = refs[:4]
    high_0, low_0, high_2, low_2, one, rest, loss, sums, high, low = refs[4:]
    chunk, quarter = high.shape[0] // 8, high.shape[1]
    step = parts[0].shape[0] // 8
    rest[...] = one[...]
    for q in range(4):
        part = slice(q * quarter, (q + 1) * quarter)
        terms = []
        for right, at_col in (((high_0, low_0), 0), ((high_2, low_2), quarter)):
            for p in range(8):
                to = slice(p * chunk, (p + 1) * chunk)
                high[to, :], low[to, :] = split(
                    parts[q][p * step : p * step + chunk, at_col : at_col + quarter]
                )
            terms.append(
                dot3((high[...], low[...]), (right[0][part, :], right[1][part, :]), 1, 0)
            )
        term = terms[0] + terms[1]
        for p in range(8):
            at = pl.multiple_of((label[0] ^ masks[q][base + p]) * chunk, chunk)
            rest[pl.ds(at, chunk), :] += term[p * chunk : (p + 1) * chunk, :]
    total = jnp.zeros((8, 128), f32)
    for p in range(8):
        total += parts[0][p * step + chunk : (p + 1) * step, :128]
    loss[...] = total
    sums[...] = jnp.zeros(sums.shape, f32)
    if base:
        add_sums(sums, rest[...], (high_0, low_0), slice(0, rest.shape[0]))


def first_half_kernel(*refs):
    half_kernel(0, *refs)


def second_half_kernel(*refs):
    half_kernel(8, *refs)


def last_kernel(factor, core, rest, above, kept, sent, total):
    rows = kept.shape[0]
    total[...] = (rest[...] + above[...]) * factor[0]
    kept[...] = total[pl.ds(pl.multiple_of(core[0] * rows, rows), rows), :]
    sent[...] = total[pl.ds(pl.multiple_of((1 - core[0]) * rows, rows), rows), :]


def across(array, bit):
    return lax.ppermute(
        array, "feat", [(i, feat_of[label_of[i] ^ (1 << bit)]) for i in range(16)]
    )


def step_across(arrays, step):
    return [across(array, order[step]) for array, order in zip(arrays, orders)]


def fold(keeps, sends, step):
    cames = step_across(sends, step)
    rows, cols = keeps[0].shape
    if step == 3:
        return local_call(last_fold_kernel, (), (*keeps, *cames), [shape(rows, 4 * cols)])[0]
    outs = local_call(fold_kernel, (), (*keeps, *cames), [shape(rows // 2, cols)] * 8)
    return outs[:4], outs[4:]


def body(view_one, view_two):
    rows, cols = view_one.shape
    batch = lax.axis_size("batch")
    feats = lax.axis_size("feat")
    clip_total = rows * batch
    features = cols * feats
    core = lax.axis_index("batch") % 2
    on_first = core == 0
    first = (1 - core).astype(jnp.int32).reshape((1,))
    label = jnp.array(label_of, jnp.int32)[lax.axis_index("feat")].reshape((1,))
    swap = [(i, i ^ 1) for i in range(batch)]
    down = [(i, (i - 2) % batch) for i in range(batch)]
    up = [(i, (i + 2) % batch) for i in range(batch)]
    down_cross = [(i, (i ^ 1) - 2 if i > 1 else (i ^ 1) - 2 + batch) for i in range(batch)]
    up_cross = [(i, ((i ^ 1) + 2) % batch) for i in range(batch)]

    def pick(one, two):
        return jnp.where(on_first, one, two)

    mine, same_0, mine_cross = local_call(
        front_kernel,
        (first,),
        (view_one, view_two),
        [shape(8, cols), shape(rows, cols), shape(rows, cols)],
        mib=60,
    )
    same_1 = lax.ppermute(same_0, "batch", down)
    cross_1 = lax.ppermute(mine_cross, "batch", down_cross)
    cross_up = lax.ppermute(mine_cross, "batch", up_cross)
    mate = lax.ppermute(mine, "batch", swap)
    pairs = [jnp.stack([pick(mine, mate), pick(mate, mine)])]
    for _ in range(batch // 2 - 1):
        pairs.append(lax.ppermute(pairs[-1], "batch", up))
    parts = jnp.concatenate(pairs, axis=0)
    cross_0 = lax.ppermute(mine_cross, "batch", swap)
    cross_0, cross_up = lax.optimization_barrier((cross_0, cross_up))
    center_one = jnp.mean(parts[:, 0], axis=0)
    center_two = jnp.mean(parts[:, 1], axis=0)
    shift_one = parts[:, 0] - center_one
    shift_two = parts[:, 1] - center_two
    spread_one = jnp.sum(parts[:, 2] + rows * shift_one * shift_one, axis=0) / clip_total
    spread_two = jnp.sum(parts[:, 3] + rows * shift_two * shift_two, axis=0) / clip_total
    scale_one = 1.0 / jnp.sqrt(spread_one + epsilon)
    scale_two = 1.0 / jnp.sqrt(spread_two + epsilon)
    covary = jnp.sum(parts[:, 4] + rows * shift_one * shift_two, axis=0) / clip_total
    diagonal = covary * scale_one * scale_two
    center = pick(center_one, center_two).reshape((1, cols))
    scale = pick(scale_one, scale_two).reshape((1, cols))

    block = 2 * rows
    quarter = block // 4
    product = 3 * 2 * block * block * cols
    halves = [shape(block, cols, bf16)] * 2
    row_scratch = [pltpu.VMEM((block, quarter), bf16)] * 2

    high_0, low_0, high_1, low_1, gram = local_call(
        near_kernel,
        (first,),
        (same_0, cross_0, same_1, cross_1, center, scale),
        halves * 2 + [shape(block, block)],
        flops=product,
        mib=60,
    )
    piece_1 = lax.psum_scatter(gram, "feat", scatter_dimension=0, tiled=True)

    same_1, cross_up, high_0 = lax.optimization_barrier((same_1, cross_up, high_0))
    same_2 = lax.ppermute(same_1, "batch", down)
    cross_2 = lax.ppermute(cross_up, "batch", up)

    high_2, low_2, *outs = local_call(
        cube_kernel,
        (first, label),
        (same_2, cross_2, center, scale, high_0, low_0),
        halves + [shape(block // 2, 2 * quarter)] * 8,
        scratch=[pltpu.VMEM((block, quarter), f32)],
        flops=2 * product,
    )
    keeps, sends = outs[:4], outs[4:]
    for step in (0, 1):
        keeps, sends = fold(keeps, sends, step)
    piece_1, keeps[0] = lax.optimization_barrier((piece_1, keeps[0]))
    other_1 = lax.ppermute(piece_1, "batch", swap)
    gram_1 = lax.all_gather(other_1, "feat", axis=0, tiled=True)
    (match_1,) = local_call(match_kernel, (), (piece_1, other_1), [shape(8, 128)])
    keeps, sends = fold(keeps, sends, 2)
    piece = fold(keeps, sends, 3)

    square_weight = off_weight * 0.5 / (float(clip_total) * float(clip_total))
    share = (
        jnp.sum((1.0 - diagonal) ** 2) - off_weight * jnp.sum(diagonal * diagonal)
    ) / batch
    share = jnp.stack([share, jnp.full((), square_weight, f32)])
    piece, share, match_1 = lax.optimization_barrier((piece, share, match_1))
    other = lax.ppermute(piece, "batch", swap)
    owns = local_call(
        part_kernel,
        (share,),
        (match_1, piece, other),
        [shape(block // 16 + 8, 2 * quarter)] * 4,
    )
    for step in (3, 2, 1):
        cames = step_across(owns, step)
        if step == 1:
            cames[0], turned_sums = lax.optimization_barrier((cames[0], turned_sums))
        owns = local_call(
            join_kernel, (), (*owns, *cames), [shape(2 * owns[0].shape[0], 2 * quarter)] * 4
        )
        if step == 2:
            token = owns[0][:8, :128]
            turned, turned_sums = local_call(
                turned_kernel,
                (),
                (gram_1, high_0, low_0, high_1, low_1, token),
                [shape(block, cols), shape(8, cols)],
                flops=product,
            )
            above = lax.ppermute(turned, "batch", up)
    cames = step_across(owns, 0)

    (ahead,) = local_call(
        ahead_kernel, (), (gram_1, high_1, low_1), [shape(block, cols)], flops=product
    )

    def add_half(kernel, parts, one):
        return local_call(
            kernel,
            (label,),
            (*parts, high_0, low_0, high_2, low_2, one),
            [shape(block, cols), shape(8, 128), shape(8, cols)],
            scratch=[pltpu.VMEM((rows, quarter), bf16)] * 2,
            flops=product,
        )

    half, loss_own, _ = add_half(first_half_kernel, owns, ahead)
    rest, loss_came, own_sums = add_half(second_half_kernel, cames, half)

    factor = 2.0 * off_weight / (float(clip_total) * float(clip_total))
    weight = (-2.0 * (1.0 - diagonal) - 2.0 * off_weight * diagonal) / clip_total
    own_sums = (own_sums + turned_sums) * factor
    normed_one = (view_one - center_one) * scale_one
    normed_two = (view_two - center_two) * scale_two
    zero = jnp.zeros((cols,), f32)
    product_sum = jnp.sum(normed_one * normed_two, axis=0) * weight
    sums = jnp.stack(
        [
            pick(own_sums[0], zero) + jnp.sum(normed_two, axis=0) * weight,
            pick(own_sums[1], zero) + product_sum,
            pick(zero, own_sums[0]) + jnp.sum(normed_one, axis=0) * weight,
            pick(zero, own_sums[1]) + product_sum,
        ]
    )
    sums, loss_total = lax.psum((sums, loss_own[0] + loss_came[0]), "batch")
    sums, above = lax.optimization_barrier((sums, above))
    sums = sums / clip_total

    kept, sent = local_call(
        last_kernel,
        (jnp.full((1,), factor, f32), core.astype(jnp.int32).reshape((1,))),
        (rest, above),
        [shape(rows, cols)] * 2,
        scratch=[pltpu.VMEM((block, cols), f32)],
    )
    came = lax.ppermute(sent, "batch", swap)
    gnorm_one = pick(kept, came) + normed_two * weight
    gnorm_two = pick(came, kept) + normed_one * weight
    grad_one = clip_total * (gnorm_one - sums[0] - normed_one * sums[1]) * scale_one
    grad_two = clip_total * (gnorm_two - sums[2] - normed_two * sums[3]) * scale_two
    return (grad_one, grad_two, loss_total[0] / features)


def solution(mesh):
    placed = (P("batch", "feat"), P("batch", "feat"))
    return jax.shard_map(
        body,
        mesh=mesh,
        in_specs=placed,
        out_specs=(P("batch", "feat"), P("batch", "feat"), P()),
        check_vma=False,
    )
```

```python
import jax
import jax.numpy as jnp
from jax import lax
from jax.experimental import pallas as pl
from jax.experimental.pallas import tpu as pltpu
from jax.sharding import PartitionSpec as P

epsilon = 1e-05
off_weight = 0.005
f32 = jnp.float32
bf16 = jnp.bfloat16

gray = (0, 1, 3, 2)
label_of = tuple(gray[i // 4] * 4 + gray[i % 4] for i in range(16))
feat_of = tuple(label_of.index(i) for i in range(16))
orders = ((3, 2, 1, 0), (2, 3, 0, 1), (1, 0, 3, 2), (0, 1, 2, 3))
masks = tuple(
    tuple(sum(((p >> (3 - j)) & 1) << order[j] for j in range(4)) for p in range(16))
    for order in orders
)

vmem = pl.BlockSpec(memory_space=pltpu.VMEM)
smem = pl.BlockSpec(memory_space=pltpu.SMEM)


def local_call(kernel, scalars, arrays, outs, scratch=(), flops=0, mib=40):
    moved = sum(a.size * a.dtype.itemsize for a in (*arrays, *outs))
    call = pl.pallas_call(
        kernel,
        out_shape=list(outs),
        in_specs=[smem] * len(scalars) + [vmem] * len(arrays),
        out_specs=[vmem] * len(outs),
        scratch_shapes=list(scratch),
        compiler_params=pltpu.CompilerParams(vmem_limit_bytes=mib * 1024 * 1024),
        cost_estimate=pl.CostEstimate(flops=flops, bytes_accessed=moved, transcendentals=0),
    )
    return list(call(*scalars, *arrays))


def shape(rows, cols, dtype=f32):
    return jax.ShapeDtypeStruct((rows, cols), dtype)


def split(value):
    high = value.astype(bf16)
    return high, (value - high.astype(f32)).astype(bf16)


def dot3(left, right, left_dim, right_dim):
    def one(a, b):
        return lax.dot_general(
            a, b, (((left_dim,), (right_dim,)), ((), ())), preferred_element_type=f32
        )

    return one(left[0], right[0]) + (one(left[0], right[1]) + one(left[1], right[0]))


def normalize(first_ref, same, cross, center, scale, high, low):
    rows = cross[0].shape[0]

    def put(pieces, at):
        for source in pieces:
            part = slice(at, at + source.shape[0])
            high[part, :], low[part, :] = split((source[...] - center[...]) * scale[...])
            at += source.shape[0]

    @pl.when(first_ref[0] == 1)
    def _():
        put(same, 0)
        put(cross, rows)

    @pl.when(first_ref[0] != 1)
    def _():
        put(cross, 0)
        put(same, rows)


def near_kernel(
    first, same_0, cross_0, same_1, cross_1, center, scale, high_0, low_0, high_1, low_1, gram
):
    normalize(first, (same_0,), (cross_0,), center, scale, high_0, low_0)
    normalize(first, (same_1,), (cross_1,), center, scale, high_1, low_1)
    quarter = gram.shape[1] // 4
    for q in range(4):
        part = slice(q * quarter, (q + 1) * quarter)
        gram[:, part] = dot3((high_0[...], low_0[...]), (high_1[part, :], low_1[part, :]), 1, 1)


def cube_kernel(first, label, same, cross, center, scale, high_0, low_0, high, low, *rest):
    keeps, sends, whole = rest[:4], rest[4:8], rest[8]
    normalize(first, (same,), (cross,), center, scale, high, low)
    quarter = whole.shape[1]
    chunk = whole.shape[0] // 16
    for q in range(4):
        part = slice(q * quarter, (q + 1) * quarter)
        for right, at_col in (((high_0, low_0), 0), ((high, low), quarter)):
            whole[...] = dot3(
                (high_0[...], low_0[...]), (right[0][part, :], right[1][part, :]), 1, 1
            )
            for p in range(16):
                at = pl.multiple_of((label[0] ^ masks[q][p]) * chunk, chunk)
                target = keeps[q] if p < 8 else sends[q]
                target[p % 8 * chunk : (p % 8 + 1) * chunk, at_col : at_col + quarter] = whole[
                    pl.ds(at, chunk), :
                ]


def front_kernel(first, one, two, stats, same, cross):
    rows = one.shape[0]
    mean_one = jnp.sum(one[...], axis=0, keepdims=True) / rows
    mean_two = jnp.sum(two[...], axis=0, keepdims=True) / rows
    deviate_one = one[...] - mean_one
    deviate_two = two[...] - mean_two
    stats[...] = jnp.zeros(stats.shape, f32)
    stats[0:1, :] = mean_one
    stats[1:2, :] = mean_two
    stats[2:3, :] = jnp.sum(deviate_one * deviate_one, axis=0, keepdims=True)
    stats[3:4, :] = jnp.sum(deviate_two * deviate_two, axis=0, keepdims=True)
    stats[4:5, :] = jnp.sum(deviate_one * deviate_two, axis=0, keepdims=True)

    @pl.when(first[0] == 1)
    def _():
        same[...] = one[...]
        cross[...] = two[...]

    @pl.when(first[0] != 1)
    def _():
        same[...] = two[...]
        cross[...] = one[...]


def fold_kernel(*refs):
    half = refs[0].shape[0] // 2
    for q in range(4):
        keep, came, keep_out, send_out = refs[q::4]
        keep_out[...] = keep[:half, :] + came[:half, :]
        send_out[...] = keep[half:, :] + came[half:, :]


def last_fold_kernel(*refs):
    out = refs[8]
    cols = refs[0].shape[1]
    for q in range(4):
        out[:, q * cols : (q + 1) * cols] = refs[q][...] + refs[4 + q][...]


def match_kernel(mine, other, match):
    match[...] = jnp.full(match.shape, jnp.sum(mine[...] * other[...]), f32)


def part_kernel(share, match, mine, other, *parts):
    rows, cols = other.shape[0], parts[0].shape[1]
    square = 2.0 * match[0:1, 0:1] + jnp.sum(mine[...] * other[...], keepdims=True)
    for q in range(4):
        parts[q][:rows, :] = other[:, q * cols : (q + 1) * cols]
        parts[q][rows:, :] = jnp.broadcast_to(share[0] + share[1] * square, (8, cols))


def join_kernel(*refs):
    rows = refs[0].shape[0]
    for q in range(4):
        own, came, out = refs[q::4]
        out[:rows, :] = own[...]
        out[rows:, :] = came[...]


def add_sums(sums, rows, halves, at):
    normed = halves[0][at, :].astype(f32) + halves[1][at, :].astype(f32)
    sums[0:1, :] += jnp.sum(rows, axis=0, keepdims=True)
    sums[1:2, :] += jnp.sum(rows * normed, axis=0, keepdims=True)


def turned_kernel(gram, high_0, low_0, high_1, low_1, token, turned, sums):
    del token
    quarter = gram.shape[1] // 4
    sums[...] = jnp.zeros(sums.shape, f32)
    for q in range(4):
        part = slice(q * quarter, (q + 1) * quarter)
        term = dot3(split(gram[:, part]), (high_0[...], low_0[...]), 0, 0)
        turned[part, :] = term
        add_sums(sums, term, (high_1, low_1), part)


def ahead_kernel(gram, high_1, low_1, ahead):
    quarter = gram.shape[1] // 4
    for q in range(4):
        part = slice(q * quarter, (q + 1) * quarter)
        term = dot3(split(gram[:, part]), (high_1[part, :], low_1[part, :]), 1, 0)
        ahead[...] = term if q == 0 else ahead[...] + term


def half_kernel(base, label, *refs):
    parts = refs[:4]
    high_0, low_0, high_2, low_2, one, rest, loss, sums, high, low = refs[4:]
    chunk, quarter = high.shape[0] // 8, high.shape[1]
    step = parts[0].shape[0] // 8
    rest[...] = one[...]
    for q in range(4):
        part = slice(q * quarter, (q + 1) * quarter)
        terms = []
        for right, at_col in (((high_0, low_0), 0), ((high_2, low_2), quarter)):
            for p in range(8):
                to = slice(p * chunk, (p + 1) * chunk)
                high[to, :], low[to, :] = split(
                    parts[q][p * step : p * step + chunk, at_col : at_col + quarter]
                )
            terms.append(
                dot3((high[...], low[...]), (right[0][part, :], right[1][part, :]), 1, 0)
            )
        term = terms[0] + terms[1]
        for p in range(8):
            at = pl.multiple_of((label[0] ^ masks[q][base + p]) * chunk, chunk)
            rest[pl.ds(at, chunk), :] += term[p * chunk : (p + 1) * chunk, :]
    total = jnp.zeros((8, 128), f32)
    for p in range(8):
        total += parts[0][p * step + chunk : (p + 1) * step, :128]
    loss[...] = total
    sums[...] = jnp.zeros(sums.shape, f32)
    if base:
        add_sums(sums, rest[...], (high_0, low_0), slice(0, rest.shape[0]))


def first_half_kernel(*refs):
    half_kernel(0, *refs)


def second_half_kernel(*refs):
    half_kernel(8, *refs)


def last_kernel(factor, core, rest, above, kept, sent, total):
    rows = kept.shape[0]
    total[...] = (rest[...] + above[...]) * factor[0]
    kept[...] = total[pl.ds(pl.multiple_of(core[0] * rows, rows), rows), :]
    sent[...] = total[pl.ds(pl.multiple_of((1 - core[0]) * rows, rows), rows), :]


def across(array, bit):
    return lax.ppermute(
        array, "feat", [(i, feat_of[label_of[i] ^ (1 << bit)]) for i in range(16)]
    )


def step_across(arrays, step):
    return [across(array, order[step]) for array, order in zip(arrays, orders)]


def fold(keeps, sends, step):
    cames = step_across(sends, step)
    rows, cols = keeps[0].shape
    if step == 3:
        return local_call(last_fold_kernel, (), (*keeps, *cames), [shape(rows, 4 * cols)])[0]
    outs = local_call(fold_kernel, (), (*keeps, *cames), [shape(rows // 2, cols)] * 8)
    return outs[:4], outs[4:]


def body(view_one, view_two):
    rows, cols = view_one.shape
    batch = lax.axis_size("batch")
    feats = lax.axis_size("feat")
    clip_total = rows * batch
    features = cols * feats
    core = lax.axis_index("batch") % 2
    on_first = core == 0
    first = (1 - core).astype(jnp.int32).reshape((1,))
    label = jnp.array(label_of, jnp.int32)[lax.axis_index("feat")].reshape((1,))
    swap = [(i, i ^ 1) for i in range(batch)]
    down = [(i, (i - 2) % batch) for i in range(batch)]
    up = [(i, (i + 2) % batch) for i in range(batch)]
    down_cross = [(i, (i ^ 1) - 2 if i > 1 else (i ^ 1) - 2 + batch) for i in range(batch)]
    up_cross = [(i, ((i ^ 1) + 2) % batch) for i in range(batch)]

    def pick(one, two):
        return jnp.where(on_first, one, two)

    mine, same_0, mine_cross = local_call(
        front_kernel,
        (first,),
        (view_one, view_two),
        [shape(8, cols), shape(rows, cols), shape(rows, cols)],
        mib=60,
    )
    same_1 = lax.ppermute(same_0, "batch", down)
    cross_1 = lax.ppermute(mine_cross, "batch", down_cross)
    cross_up = lax.ppermute(mine_cross, "batch", up_cross)
    mate = lax.ppermute(mine, "batch", swap)
    pairs = [jnp.stack([pick(mine, mate), pick(mate, mine)])]
    for _ in range(batch // 2 - 1):
        pairs.append(lax.ppermute(pairs[-1], "batch", up))
    parts = jnp.concatenate(pairs, axis=0)
    cross_0 = lax.ppermute(mine_cross, "batch", swap)
    cross_0, cross_up = lax.optimization_barrier((cross_0, cross_up))
    center_one = jnp.mean(parts[:, 0], axis=0)
    center_two = jnp.mean(parts[:, 1], axis=0)
    shift_one = parts[:, 0] - center_one
    shift_two = parts[:, 1] - center_two
    spread_one = jnp.sum(parts[:, 2] + rows * shift_one * shift_one, axis=0) / clip_total
    spread_two = jnp.sum(parts[:, 3] + rows * shift_two * shift_two, axis=0) / clip_total
    scale_one = 1.0 / jnp.sqrt(spread_one + epsilon)
    scale_two = 1.0 / jnp.sqrt(spread_two + epsilon)
    covary = jnp.sum(parts[:, 4] + rows * shift_one * shift_two, axis=0) / clip_total
    diagonal = covary * scale_one * scale_two
    center = pick(center_one, center_two).reshape((1, cols))
    scale = pick(scale_one, scale_two).reshape((1, cols))

    block = 2 * rows
    quarter = block // 4
    product = 3 * 2 * block * block * cols
    halves = [shape(block, cols, bf16)] * 2
    row_scratch = [pltpu.VMEM((block, quarter), bf16)] * 2

    high_0, low_0, high_1, low_1, gram = local_call(
        near_kernel,
        (first,),
        (same_0, cross_0, same_1, cross_1, center, scale),
        halves * 2 + [shape(block, block)],
        flops=product,
        mib=60,
    )
    piece_1 = lax.psum_scatter(gram, "feat", scatter_dimension=0, tiled=True)

    same_1, cross_up, high_0 = lax.optimization_barrier((same_1, cross_up, high_0))
    same_2 = lax.ppermute(same_1, "batch", down)
    cross_2 = lax.ppermute(cross_up, "batch", up)

    high_2, low_2, *outs = local_call(
        cube_kernel,
        (first, label),
        (same_2, cross_2, center, scale, high_0, low_0),
        halves + [shape(block // 2, 2 * quarter)] * 8,
        scratch=[pltpu.VMEM((block, quarter), f32)],
        flops=2 * product,
    )
    keeps, sends = outs[:4], outs[4:]
    for step in (0, 1):
        keeps, sends = fold(keeps, sends, step)
    piece_1, keeps[0] = lax.optimization_barrier((piece_1, keeps[0]))
    other_1 = lax.ppermute(piece_1, "batch", swap)
    gram_1 = lax.all_gather(other_1, "feat", axis=0, tiled=True)
    (match_1,) = local_call(match_kernel, (), (piece_1, other_1), [shape(8, 128)])
    keeps, sends = fold(keeps, sends, 2)
    piece = fold(keeps, sends, 3)

    square_weight = off_weight * 0.5 / (float(clip_total) * float(clip_total))
    share = (
        jnp.sum((1.0 - diagonal) ** 2) - off_weight * jnp.sum(diagonal * diagonal)
    ) / batch
    share = jnp.stack([share, jnp.full((), square_weight, f32)])
    piece, share, match_1 = lax.optimization_barrier((piece, share, match_1))
    other = lax.ppermute(piece, "batch", swap)
    owns = local_call(
        part_kernel,
        (share,),
        (match_1, piece, other),
        [shape(block // 16 + 8, 2 * quarter)] * 4,
    )
    for step in (3, 2, 1):
        cames = step_across(owns, step)
        if step == 1:
            cames[0], turned_sums = lax.optimization_barrier((cames[0], turned_sums))
        owns = local_call(
            join_kernel, (), (*owns, *cames), [shape(2 * owns[0].shape[0], 2 * quarter)] * 4
        )
        if step == 2:
            token = owns[0][:8, :128]
            turned, turned_sums = local_call(
                turned_kernel,
                (),
                (gram_1, high_0, low_0, high_1, low_1, token),
                [shape(block, cols), shape(8, cols)],
                flops=product,
                mib=60,
            )
            above = lax.ppermute(turned, "batch", up)
    cames = step_across(owns, 0)

    (ahead,) = local_call(
        ahead_kernel, (), (gram_1, high_1, low_1), [shape(block, cols)], flops=product
    )

    def add_half(kernel, parts, one):
        return local_call(
            kernel,
            (label,),
            (*parts, high_0, low_0, high_2, low_2, one),
            [shape(block, cols), shape(8, 128), shape(8, cols)],
            scratch=[pltpu.VMEM((rows, quarter), bf16)] * 2,
            flops=product,
        )

    half, loss_own, _ = add_half(first_half_kernel, owns, ahead)
    rest, loss_came, own_sums = add_half(second_half_kernel, cames, half)

    factor = 2.0 * off_weight / (float(clip_total) * float(clip_total))
    weight = (-2.0 * (1.0 - diagonal) - 2.0 * off_weight * diagonal) / clip_total
    own_sums = (own_sums + turned_sums) * factor
    normed_one = (view_one - center_one) * scale_one
    normed_two = (view_two - center_two) * scale_two
    zero = jnp.zeros((cols,), f32)
    product_sum = jnp.sum(normed_one * normed_two, axis=0) * weight
    sums = jnp.stack(
        [
            pick(own_sums[0], zero) + jnp.sum(normed_two, axis=0) * weight,
            pick(own_sums[1], zero) + product_sum,
            pick(zero, own_sums[0]) + jnp.sum(normed_one, axis=0) * weight,
            pick(zero, own_sums[1]) + product_sum,
        ]
    )
    sums, loss_total = lax.psum((sums, loss_own[0] + loss_came[0]), "batch")
    sums, above = lax.optimization_barrier((sums, above))
    sums = sums / clip_total

    kept, sent = local_call(
        last_kernel,
        (jnp.full((1,), factor, f32), core.astype(jnp.int32).reshape((1,))),
        (rest, above),
        [shape(rows, cols)] * 2,
        scratch=[pltpu.VMEM((block, cols), f32)],
        mib=60,
    )
    came = lax.ppermute(sent, "batch", swap)
    gnorm_one = pick(kept, came) + normed_two * weight
    gnorm_two = pick(came, kept) + normed_one * weight
    grad_one = clip_total * (gnorm_one - sums[0] - normed_one * sums[1]) * scale_one
    grad_two = clip_total * (gnorm_two - sums[2] - normed_two * sums[3]) * scale_two
    return (grad_one, grad_two, loss_total[0] / features)


def solution(mesh):
    placed = (P("batch", "feat"), P("batch", "feat"))
    return jax.shard_map(
        body,
        mesh=mesh,
        in_specs=placed,
        out_specs=(P("batch", "feat"), P("batch", "feat"), P()),
        check_vma=False,
    )
```

```python
import jax
import jax.numpy as jnp
from jax import lax
from jax.experimental import pallas as pl
from jax.experimental.pallas import tpu as pltpu
from jax.sharding import PartitionSpec as P

epsilon = 1e-05
off_weight = 0.005
f32 = jnp.float32
bf16 = jnp.bfloat16

gray = (0, 1, 3, 2)
label_of = tuple(gray[i // 4] * 4 + gray[i % 4] for i in range(16))
feat_of = tuple(label_of.index(i) for i in range(16))
orders = ((3, 2, 1, 0), (2, 3, 0, 1), (1, 0, 3, 2), (0, 1, 2, 3))
masks = tuple(
    tuple(sum(((p >> (3 - j)) & 1) << order[j] for j in range(4)) for p in range(16))
    for order in orders
)

vmem = pl.BlockSpec(memory_space=pltpu.VMEM)
smem = pl.BlockSpec(memory_space=pltpu.SMEM)


def local_call(kernel, scalars, arrays, outs, scratch=(), flops=0, mib=40):
    moved = sum(a.size * a.dtype.itemsize for a in (*arrays, *outs))
    call = pl.pallas_call(
        kernel,
        out_shape=list(outs),
        in_specs=[smem] * len(scalars) + [vmem] * len(arrays),
        out_specs=[vmem] * len(outs),
        scratch_shapes=list(scratch),
        compiler_params=pltpu.CompilerParams(vmem_limit_bytes=mib * 1024 * 1024),
        cost_estimate=pl.CostEstimate(flops=flops, bytes_accessed=moved, transcendentals=0),
    )
    return list(call(*scalars, *arrays))


def shape(rows, cols, dtype=f32):
    return jax.ShapeDtypeStruct((rows, cols), dtype)


def split(value):
    high = value.astype(bf16)
    return high, (value - high.astype(f32)).astype(bf16)


def dot3(left, right, left_dim, right_dim):
    def one(a, b):
        return lax.dot_general(
            a, b, (((left_dim,), (right_dim,)), ((), ())), preferred_element_type=f32
        )

    return one(left[0], right[0]) + (one(left[0], right[1]) + one(left[1], right[0]))


def normalize(first_ref, same, cross, center, scale, high, low):
    rows = cross[0].shape[0]

    def put(pieces, at):
        for source in pieces:
            part = slice(at, at + source.shape[0])
            high[part, :], low[part, :] = split((source[...] - center[...]) * scale[...])
            at += source.shape[0]

    @pl.when(first_ref[0] == 1)
    def _():
        put(same, 0)
        put(cross, rows)

    @pl.when(first_ref[0] != 1)
    def _():
        put(cross, 0)
        put(same, rows)


def near_kernel(
    first, same_0, cross_0, same_1, cross_1, center, scale, high_0, low_0, high_1, low_1, gram
):
    normalize(first, (same_0,), (cross_0,), center, scale, high_0, low_0)
    normalize(first, (same_1,), (cross_1,), center, scale, high_1, low_1)
    quarter = gram.shape[1] // 4
    for q in range(4):
        part = slice(q * quarter, (q + 1) * quarter)
        gram[:, part] = dot3((high_0[...], low_0[...]), (high_1[part, :], low_1[part, :]), 1, 1)


def cube_kernel(first, label, same, cross, center, scale, high_0, low_0, high, low, *rest):
    keeps, sends, whole = rest[:4], rest[4:8], rest[8]
    normalize(first, (same,), (cross,), center, scale, high, low)
    quarter = whole.shape[1]
    chunk = whole.shape[0] // 16
    for q in range(4):
        part = slice(q * quarter, (q + 1) * quarter)
        for right, at_col in (((high_0, low_0), 0), ((high, low), quarter)):
            whole[...] = dot3(
                (high_0[...], low_0[...]), (right[0][part, :], right[1][part, :]), 1, 1
            )
            for p in range(16):
                at = pl.multiple_of((label[0] ^ masks[q][p]) * chunk, chunk)
                target = keeps[q] if p < 8 else sends[q]
                target[p % 8 * chunk : (p % 8 + 1) * chunk, at_col : at_col + quarter] = whole[
                    pl.ds(at, chunk), :
                ]


def front_kernel(first, one, two, stats, same, cross):
    rows = one.shape[0]
    mean_one = jnp.sum(one[...], axis=0, keepdims=True) / rows
    mean_two = jnp.sum(two[...], axis=0, keepdims=True) / rows
    deviate_one = one[...] - mean_one
    deviate_two = two[...] - mean_two
    stats[...] = jnp.zeros(stats.shape, f32)
    stats[0:1, :] = mean_one
    stats[1:2, :] = mean_two
    stats[2:3, :] = jnp.sum(deviate_one * deviate_one, axis=0, keepdims=True)
    stats[3:4, :] = jnp.sum(deviate_two * deviate_two, axis=0, keepdims=True)
    stats[4:5, :] = jnp.sum(deviate_one * deviate_two, axis=0, keepdims=True)

    @pl.when(first[0] == 1)
    def _():
        same[...] = one[...]
        cross[...] = two[...]

    @pl.when(first[0] != 1)
    def _():
        same[...] = two[...]
        cross[...] = one[...]


def fold_kernel(*refs):
    half = refs[0].shape[0] // 2
    for q in range(4):
        keep, came, keep_out, send_out = refs[q::4]
        keep_out[...] = keep[:half, :] + came[:half, :]
        send_out[...] = keep[half:, :] + came[half:, :]


def last_fold_kernel(*refs):
    out = refs[8]
    cols = refs[0].shape[1]
    for q in range(4):
        out[:, q * cols : (q + 1) * cols] = refs[q][...] + refs[4 + q][...]


def match_kernel(mine, other, match):
    match[...] = jnp.full(match.shape, jnp.sum(mine[...] * other[...]), f32)


def part_kernel(share, match, mine, other, *parts):
    rows, cols = other.shape[0], parts[0].shape[1]
    square = 2.0 * match[0:1, 0:1] + jnp.sum(mine[...] * other[...], keepdims=True)
    for q in range(4):
        parts[q][:rows, :] = other[:, q * cols : (q + 1) * cols]
        parts[q][rows:, :] = jnp.broadcast_to(share[0] + share[1] * square, (8, cols))


def join_kernel(*refs):
    rows = refs[0].shape[0]
    for q in range(4):
        own, came, out = refs[q::4]
        out[:rows, :] = own[...]
        out[rows:, :] = came[...]


def add_sums(sums, rows, halves, at):
    normed = halves[0][at, :].astype(f32) + halves[1][at, :].astype(f32)
    sums[0:1, :] += jnp.sum(rows, axis=0, keepdims=True)
    sums[1:2, :] += jnp.sum(rows * normed, axis=0, keepdims=True)


def turned_kernel(gram, high_0, low_0, high_1, low_1, token, turned, sums):
    del token
    quarter = gram.shape[1] // 4
    sums[...] = jnp.zeros(sums.shape, f32)
    for q in range(4):
        part = slice(q * quarter, (q + 1) * quarter)
        term = dot3(split(gram[:, part]), (high_0[...], low_0[...]), 0, 0)
        turned[part, :] = term
        add_sums(sums, term, (high_1, low_1), part)


def ahead_kernel(gram, high_1, low_1, ahead):
    quarter = gram.shape[1] // 4
    for q in range(4):
        part = slice(q * quarter, (q + 1) * quarter)
        term = dot3(split(gram[:, part]), (high_1[part, :], low_1[part, :]), 1, 0)
        ahead[...] = term if q == 0 else ahead[...] + term


def half_kernel(base, label, *refs):
    parts = refs[:4]
    high_0, low_0, high_2, low_2, one, rest, loss, sums, high, low = refs[4:]
    chunk, quarter = high.shape[0] // 8, high.shape[1]
    step = parts[0].shape[0] // 8
    rest[...] = one[...]
    for q in range(4):
        part = slice(q * quarter, (q + 1) * quarter)
        terms = []
        for right, at_col in (((high_0, low_0), 0), ((high_2, low_2), quarter)):
            for p in range(8):
                to = slice(p * chunk, (p + 1) * chunk)
                high[to, :], low[to, :] = split(
                    parts[q][p * step : p * step + chunk, at_col : at_col + quarter]
                )
            terms.append(
                dot3((high[...], low[...]), (right[0][part, :], right[1][part, :]), 1, 0)
            )
        term = terms[0] + terms[1]
        for p in range(8):
            at = pl.multiple_of((label[0] ^ masks[q][base + p]) * chunk, chunk)
            rest[pl.ds(at, chunk), :] += term[p * chunk : (p + 1) * chunk, :]
    total = jnp.zeros((8, 128), f32)
    for p in range(8):
        total += parts[0][p * step + chunk : (p + 1) * step, :128]
    loss[...] = total
    sums[...] = jnp.zeros(sums.shape, f32)
    if base:
        add_sums(sums, rest[...], (high_0, low_0), slice(0, rest.shape[0]))


def first_half_kernel(*refs):
    half_kernel(0, *refs)


def second_half_kernel(*refs):
    half_kernel(8, *refs)


def last_kernel(factor, core, rest, above, kept, sent, total):
    rows = kept.shape[0]
    total[...] = (rest[...] + above[...]) * factor[0]
    kept[...] = total[pl.ds(pl.multiple_of(core[0] * rows, rows), rows), :]
    sent[...] = total[pl.ds(pl.multiple_of((1 - core[0]) * rows, rows), rows), :]


def across(array, bit):
    return lax.ppermute(
        array, "feat", [(i, feat_of[label_of[i] ^ (1 << bit)]) for i in range(16)]
    )


def step_across(arrays, step):
    return [across(array, order[step]) for array, order in zip(arrays, orders)]


def fold(keeps, sends, step):
    cames = step_across(sends, step)
    rows, cols = keeps[0].shape
    if step == 3:
        return local_call(last_fold_kernel, (), (*keeps, *cames), [shape(rows, 4 * cols)])[0]
    outs = local_call(fold_kernel, (), (*keeps, *cames), [shape(rows // 2, cols)] * 8)
    return outs[:4], outs[4:]


def body(view_one, view_two):
    rows, cols = view_one.shape
    batch = lax.axis_size("batch")
    feats = lax.axis_size("feat")
    clip_total = rows * batch
    features = cols * feats
    core = lax.axis_index("batch") % 2
    on_first = core == 0
    first = (1 - core).astype(jnp.int32).reshape((1,))
    label = jnp.array(label_of, jnp.int32)[lax.axis_index("feat")].reshape((1,))
    swap = [(i, i ^ 1) for i in range(batch)]
    down = [(i, (i - 2) % batch) for i in range(batch)]
    up = [(i, (i + 2) % batch) for i in range(batch)]
    down_cross = [(i, (i ^ 1) - 2 if i > 1 else (i ^ 1) - 2 + batch) for i in range(batch)]
    up_cross = [(i, ((i ^ 1) + 2) % batch) for i in range(batch)]

    def pick(one, two):
        return jnp.where(on_first, one, two)

    mine, same_0, mine_cross = local_call(
        front_kernel,
        (first,),
        (view_one, view_two),
        [shape(8, cols), shape(rows, cols), shape(rows, cols)],
        mib=60,
    )
    same_1 = lax.ppermute(same_0, "batch", down)
    cross_1 = lax.ppermute(mine_cross, "batch", down_cross)
    cross_up = lax.ppermute(mine_cross, "batch", up_cross)
    mate = lax.ppermute(mine, "batch", swap)
    pairs = [jnp.stack([pick(mine, mate), pick(mate, mine)])]
    for _ in range(batch // 2 - 1):
        pairs.append(lax.ppermute(pairs[-1], "batch", up))
    parts = jnp.concatenate(pairs, axis=0)
    cross_0 = lax.ppermute(mine_cross, "batch", swap)
    cross_0, cross_up = lax.optimization_barrier((cross_0, cross_up))
    center_one = jnp.mean(parts[:, 0], axis=0)
    center_two = jnp.mean(parts[:, 1], axis=0)
    shift_one = parts[:, 0] - center_one
    shift_two = parts[:, 1] - center_two
    spread_one = jnp.sum(parts[:, 2] + rows * shift_one * shift_one, axis=0) / clip_total
    spread_two = jnp.sum(parts[:, 3] + rows * shift_two * shift_two, axis=0) / clip_total
    scale_one = 1.0 / jnp.sqrt(spread_one + epsilon)
    scale_two = 1.0 / jnp.sqrt(spread_two + epsilon)
    covary = jnp.sum(parts[:, 4] + rows * shift_one * shift_two, axis=0) / clip_total
    diagonal = covary * scale_one * scale_two
    center = pick(center_one, center_two).reshape((1, cols))
    scale = pick(scale_one, scale_two).reshape((1, cols))

    block = 2 * rows
    quarter = block // 4
    product = 3 * 2 * block * block * cols
    halves = [shape(block, cols, bf16)] * 2
    row_scratch = [pltpu.VMEM((block, quarter), bf16)] * 2

    high_0, low_0, high_1, low_1, gram = local_call(
        near_kernel,
        (first,),
        (same_0, cross_0, same_1, cross_1, center, scale),
        halves * 2 + [shape(block, block)],
        flops=product,
        mib=60,
    )
    piece_1 = lax.psum_scatter(gram, "feat", scatter_dimension=0, tiled=True)

    same_1, cross_up, high_0 = lax.optimization_barrier((same_1, cross_up, high_0))
    same_2 = lax.ppermute(same_1, "batch", down)
    cross_2 = lax.ppermute(cross_up, "batch", up)

    high_2, low_2, *outs = local_call(
        cube_kernel,
        (first, label),
        (same_2, cross_2, center, scale, high_0, low_0),
        halves + [shape(block // 2, 2 * quarter)] * 8,
        scratch=[pltpu.VMEM((block, quarter), f32)],
        flops=2 * product,
    )
    keeps, sends = outs[:4], outs[4:]
    for step in (0, 1):
        keeps, sends = fold(keeps, sends, step)
    piece_1, keeps[0] = lax.optimization_barrier((piece_1, keeps[0]))
    other_1 = lax.ppermute(piece_1, "batch", swap)
    gram_1 = lax.all_gather(other_1, "feat", axis=0, tiled=True)
    (match_1,) = local_call(match_kernel, (), (piece_1, other_1), [shape(8, 128)])
    keeps, sends = fold(keeps, sends, 2)
    piece = fold(keeps, sends, 3)

    square_weight = off_weight * 0.5 / (float(clip_total) * float(clip_total))
    share = (
        jnp.sum((1.0 - diagonal) ** 2) - off_weight * jnp.sum(diagonal * diagonal)
    ) / batch
    share = jnp.stack([share, jnp.full((), square_weight, f32)])
    piece, share, match_1 = lax.optimization_barrier((piece, share, match_1))
    other = lax.ppermute(piece, "batch", swap)
    owns = local_call(
        part_kernel,
        (share,),
        (match_1, piece, other),
        [shape(block // 16 + 8, 2 * quarter)] * 4,
    )
    for step in (3, 2, 1):
        cames = step_across(owns, step)
        if step == 1:
            cames[0], turned_sums = lax.optimization_barrier((cames[0], turned_sums))
        owns = local_call(
            join_kernel, (), (*owns, *cames), [shape(2 * owns[0].shape[0], 2 * quarter)] * 4
        )
        if step == 2:
            token = owns[0][:8, :128]
            turned, turned_sums = local_call(
                turned_kernel,
                (),
                (gram_1, high_0, low_0, high_1, low_1, token),
                [shape(block, cols), shape(8, cols)],
                flops=product,
                mib=60,
            )
            above = lax.ppermute(turned, "batch", up)
    cames = step_across(owns, 0)

    (ahead,) = local_call(
        ahead_kernel, (), (gram_1, high_1, low_1), [shape(block, cols)], flops=product
    )

    def add_half(kernel, parts, one):
        return local_call(
            kernel,
            (label,),
            (*parts, high_0, low_0, high_2, low_2, one),
            [shape(block, cols), shape(8, 128), shape(8, cols)],
            scratch=[pltpu.VMEM((rows, quarter), bf16)] * 2,
            flops=product,
        )

    half, loss_own, _ = add_half(first_half_kernel, owns, ahead)
    rest, loss_came, own_sums = add_half(second_half_kernel, cames, half)

    factor = 2.0 * off_weight / (float(clip_total) * float(clip_total))
    weight = (-2.0 * (1.0 - diagonal) - 2.0 * off_weight * diagonal) / clip_total
    own_sums = (own_sums + turned_sums) * factor
    normed_one = (view_one - center_one) * scale_one
    normed_two = (view_two - center_two) * scale_two
    zero = jnp.zeros((cols,), f32)
    product_sum = jnp.sum(normed_one * normed_two, axis=0) * weight
    sums = jnp.stack(
        [
            pick(own_sums[0], zero) + jnp.sum(normed_two, axis=0) * weight,
            pick(own_sums[1], zero) + product_sum,
            pick(zero, own_sums[0]) + jnp.sum(normed_one, axis=0) * weight,
            pick(zero, own_sums[1]) + product_sum,
        ]
    )
    sums, loss_total = lax.psum((sums, loss_own[0] + loss_came[0]), "batch")
    sums, above = lax.optimization_barrier((sums, above))
    sums = sums / clip_total

    kept, sent = local_call(
        last_kernel,
        (jnp.full((1,), factor, f32), core.astype(jnp.int32).reshape((1,))),
        (rest, above),
        [shape(rows, cols)] * 2,
        scratch=[pltpu.VMEM((block, cols), f32)],
    )
    came = lax.ppermute(sent, "batch", swap)
    gnorm_one = pick(kept, came) + normed_two * weight
    gnorm_two = pick(came, kept) + normed_one * weight
    grad_one = clip_total * (gnorm_one - sums[0] - normed_one * sums[1]) * scale_one
    grad_two = clip_total * (gnorm_two - sums[2] - normed_two * sums[3]) * scale_two
    return (grad_one, grad_two, loss_total[0] / features)


def solution(mesh):
    placed = (P("batch", "feat"), P("batch", "feat"))
    return jax.shard_map(
        body,
        mesh=mesh,
        in_specs=placed,
        out_specs=(P("batch", "feat"), P("batch", "feat"), P()),
        check_vma=False,
    )
```
